32 devices in a mesh: dp: 8 (over z, x), mp: 4 (over y, core).
Axes of the slice: x: 2, y: 2, z: 4, core: 2. Of those that a mesh axis runs over, the one named last changes fastest.
Arguments:
- tokens: bfloat16 [32, 512, 768], P('dp', 'mp'), may hold values from -6 to 6
- lengths: int32 [32], P('dp'), may hold values from 128 to 512, as said below
- answer: int32 [32, 2], P('dp'), may hold values from 0 to 511, as said below
- head_order: int32 [12], replicated, may hold values from 0 to 11, as said below
- neuron_order: int32 [3072], replicated, may hold values from 0 to 3071, as said below
- w_qkv: bfloat16 [768, 3, 768], P(None, None, 'mp'), may hold values from -0.21875 to 0.21875
- b_qv: bfloat16 [2, 768], P(None, 'mp'), may hold values from -1.75 to 1.75
- w_out: bfloat16 [768, 768], P('mp'), may hold values from -0.75 to 0.75
- b_out: bfloat16 [768], replicated, may hold values from -1.75 to 1.75
- ln1_gain: bfloat16 [768], replicated, may hold values from 0.5 to 1.5
- ln1_bias: bfloat16 [768], replicated, may hold values from -1.75 to 1.75
- w_in: bfloat16 [768, 3072], P(None, 'mp'), may hold values from -0.21875 to 0.21875
- b_in: bfloat16 [3072], P('mp'), may hold values from -1.75 to 1.75
- w_down: bfloat16 [3072, 768], P('mp'), may hold values from -0.21875 to 0.21875
- b_down: bfloat16 [768], replicated, may hold values from -1.75 to 1.75
- ln2_gain: bfloat16 [768], replicated, may hold values from 0.5 to 1.5
- ln2_bias: bfloat16 [768], replicated, may hold values from -1.75 to 1.75
- w_span: float32 [768, 2], replicated, may hold values from -0.4375 to 0.4375
- out_grad: bfloat16 [32, 512, 768], P('dp', 'mp'), may hold values from -6 to 6
Outputs:
- layer_out: bfloat16 [32, 512, 768], P('dp', 'mp')
- row_loss: float32 [32], P('dp')
- tokens_grad: float32 [32, 512, 768], P('dp', 'mp')
- w_qkv_grad: float32 [768, 3, 768], P(None, None, 'mp')
- b_qv_grad: float32 [2, 768], P(None, 'mp')
- w_out_grad: float32 [768, 768], P('mp')
- b_out_grad: float32 [768], replicated
- ln1_gain_grad: float32 [768], replicated
- ln1_bias_grad: float32 [768], replicated
- w_in_grad: float32 [768, 3072], P(None, 'mp')
- b_in_grad: float32 [3072], P('mp')
- w_down_grad: float32 [3072, 768], P('mp')
- b_down_grad: float32 [768], replicated
- ln2_gain_grad: float32 [768], replicated
- ln2_bias_grad: float32 [768], replicated
- w_span_grad: float32 [768, 2], replicated
The draws below stay inside these ranges and needn't reach their ends.
Inputs may be any that keep to these rules, and one draw needn't show every extreme that they name: `lengths`: each aligned block of 4 rows holds a row of length 512. `answer`: 0 <= start <= end < the row's length; unanswerable rows have start and end 0. `head_order`: a permutation of the heads. `neuron_order`: a permutation of the units.
All inputs are finite; a program needn't handle non-finite values.
Results may differ from the reference program's by a relative error of at most 0.018.
Values may be sent and summed in bfloat16 or wider, within the bound.
No kernel may reach another device: no remote copies, remote signals or barrier semaphores. Data moves between devices by JAX's collectives and lax.ppermute only.
A program may use at most 128 MiB of HBM per device.

```python
import jax
import jax.numpy as jnp
from jax import lax

D = 768
HEADS = 12
HEAD_DIM = 64
FF = 3072
SEQ = 512
ROWS_DEV = 4
ROWS = 32
LIVE_HEADS = 6
LIVE_FF = 1536
N_MP = 4


def span_table(key):
    key = jax.random.fold_in(key, 11)
    keys = jax.random.split(key, 5)
    row_lengths = jax.random.randint(keys[0], (ROWS,), SEQ // 4, SEQ + 1)
    blocks = ROWS // ROWS_DEV
    choose = jax.random.randint(keys[1], (blocks,), 0, ROWS_DEV)
    full_rows = (jnp.arange(ROWS_DEV)[None, :] == choose[:, None]).reshape(ROWS)
    row_lengths = jnp.where(full_rows, SEQ, row_lengths)
    start_pos = jax.random.randint(keys[2], (ROWS,), 0, row_lengths)
    end_pos = start_pos + jax.random.randint(keys[3], (ROWS,), 0, row_lengths - start_pos)
    end_pos = jnp.where(full_rows, SEQ - 1, end_pos)
    answerable = jnp.logical_or(jax.random.randint(keys[4], (ROWS,), 0, 3) > 0, full_rows)
    start_pos = jnp.where(answerable, start_pos, 0)
    end_pos = jnp.where(answerable, end_pos, 0)
    return (row_lengths.astype(jnp.int32), jnp.stack([start_pos, end_pos], 1).astype(jnp.int32))


def importance_order(key, count):
    return jax.random.permutation(key, jnp.arange(count, dtype=jnp.int32)).astype(jnp.int32)


def draw_lengths(key, part):
    return span_table(key)[0]


def draw_answer(key, part):
    return span_table(key)[1]


def draw_head_order(key, part):
    key = jax.random.fold_in(key, 21)
    return importance_order(key, HEADS)


def draw_neuron_order(key, part):
    key = jax.random.fold_in(key, 22)
    return importance_order(key, FF)


def shard_levels(key, extent, cuts, low, largest):
    def one(dim, blocks):
        steps = jax.random.uniform(jax.random.fold_in(jax.random.fold_in(key, 6), dim), (blocks,), jnp.float32, low / len(cuts), largest / len(cuts))
        return jnp.repeat(jnp.exp(steps), extent[dim] // blocks).reshape((-1,) + (1,) * (len(extent) - dim - 1))

    gain = one(*cuts[0])
    for cut in cuts[1:]:
        gain = gain * one(*cut)
    return gain


def noise(key, dims, scale, bound, shards=(), kind=jnp.bfloat16):
    result = jax.random.normal(key, dims, jnp.float32) * scale
    if len(shards) > 0:
        result = shard_levels(key, dims, shards, -0.22, 0.18) * result
    return jnp.clip(result, min=-bound, max=bound).astype(kind)


def setup_inputs(seed: int = 0) -> dict:
    streams_of = jax.random.split(jax.random.key(seed), 20)
    tokens = noise(streams_of[0], (ROWS, SEQ, D), 1.0, 6.0, ((0, 8), (1, 4)))
    lengths = draw_lengths(jax.random.fold_in(streams_of[19], 71), 0)
    answer = draw_answer(jax.random.fold_in(streams_of[19], 71), 0)
    head_order = draw_head_order(jax.random.fold_in(streams_of[19], 71), 0)
    neuron_order = draw_neuron_order(jax.random.fold_in(streams_of[19], 71), 0)
    w_qkv = noise(streams_of[5], (D, 3, HEADS * HEAD_DIM), D ** -0.5, 0.21875, ((2, 4),))
    b_qv = noise(streams_of[6], (2, HEADS * HEAD_DIM), 0.3, 1.75, ((1, 4),))
    w_out = noise(streams_of[7], (HEADS * HEAD_DIM, D), HEAD_DIM ** -0.5, 0.75, ((0, 4),))
    b_out = noise(streams_of[8], (D,), 0.3, 1.75)
    ln1_gain = jnp.clip(1.0 + 0.1 * jax.random.normal(streams_of[9], (D,), jnp.float32), 0.5, 1.5).astype(jnp.bfloat16)
    ln1_bias = noise(streams_of[10], (D,), 0.3, 1.75)
    w_in = noise(streams_of[11], (D, FF), D ** -0.5, 0.21875, ((1, 4),))
    b_in = noise(streams_of[12], (FF,), 0.3, 1.75, ((0, 4),))
    w_down = noise(streams_of[13], (FF, D), (FF // 4) ** -0.5, 0.21875, ((0, 4),))
    b_down = noise(streams_of[14], (D,), 0.3, 1.75)
    ln2_gain = jnp.clip(1.0 + 0.1 * jax.random.normal(streams_of[15], (D,), jnp.float32), 0.5, 1.5).astype(jnp.bfloat16)
    ln2_bias = noise(streams_of[16], (D,), 0.3, 1.75)
    w_span = noise(streams_of[17], (D, 2), (D // 4) ** -0.5, 0.4375, (), jnp.float32)
    out_grad = noise(streams_of[18], (ROWS, SEQ, D), 1.0, 6.0, ((0, 8), (1, 4)))
    return {"tokens": tokens, "lengths": lengths, "answer": answer, "head_order": head_order, "neuron_order": neuron_order, "w_qkv": w_qkv, "b_qv": b_qv, "w_out": w_out, "b_out": b_out, "ln1_gain": ln1_gain, "ln1_bias": ln1_bias, "w_in": w_in, "b_in": b_in, "w_down": w_down, "b_down": b_down, "ln2_gain": ln2_gain, "ln2_bias": ln2_bias, "w_span": w_span, "out_grad": out_grad}


epsilon = 1e-12
highest = lax.Precision.HIGHEST

@jax.custom_vjp
def low(v):
    return lax.optimization_barrier(v.astype(jnp.bfloat16)).astype(jnp.float32)

@jax.custom_vjp
def low_back(v):
    return v

def low_keep(v):
    return (low(v), None)

def low_pass(kept, grad):
    return (grad,)

def back_keep(v):
    return (v, None)

def back_low(kept, grad):
    return (low(grad),)
low.defvjp(low_keep, low_pass)
low_back.defvjp(back_keep, back_low)

def norm_rows(values_in, norm_gain, norm_bias):
    row_mean = lax.optimization_barrier(jnp.mean(values_in, -1, keepdims=True))
    centered = values_in - row_mean
    variance = lax.optimization_barrier(jnp.mean(centered * centered, -1, keepdims=True))
    return centered * lax.rsqrt(variance + epsilon) * norm_gain + norm_bias

def row_forward(params, x_row, length, answer_row, head_live, unit_live):
    w_qkv, b_qv, w_out, b_out, ln1_gain, ln1_bias, w_in, b_in, w_down, b_down, ln2_gain, ln2_bias, w_span = params
    groups = N_MP
    head_width = HEADS * HEAD_DIM // groups
    group_heads = HEADS // groups
    ff_width = FF // groups
    head_shape = (groups, SEQ, group_heads, HEAD_DIM)
    spread = low_back(jnp.broadcast_to(x_row[None], (groups, SEQ, D)))
    projected = jnp.einsum('gsd,dcgw->gscw', spread, w_qkv.reshape(D, 3, groups, head_width), precision=highest)
    qv_bias = b_qv.reshape(2, groups, 1, head_width)
    query_rows = low(low_back(projected[:, :, 0] + qv_bias[0])).reshape(head_shape)
    key_rows = low(low_back(projected[:, :, 1])).reshape(head_shape)
    value_rows = low(low_back(projected[:, :, 2] + qv_bias[1])).reshape(head_shape)
    positions = jnp.arange(SEQ).astype(jnp.int32)
    valid = positions < length
    scores = jnp.einsum('gqhe,gkhe->ghqk', query_rows, key_rows, precision=highest) * HEAD_DIM ** (-0.5)
    scores = low_back(jnp.where(valid, scores, -1000000000.0))
    row_max = lax.optimization_barrier(jnp.max(scores, -1, keepdims=True))
    exp_scores = jnp.exp(scores - row_max)
    attn_probs = low(exp_scores / lax.optimization_barrier(jnp.sum(exp_scores, -1, keepdims=True)))
    mixed_heads = jnp.einsum('ghqk,gkhe->gqhe', attn_probs, value_rows, precision=highest)
    mixed_heads = mixed_heads * head_live.reshape(groups, 1, group_heads, 1)
    context = low(low_back(mixed_heads)).reshape(groups, SEQ, head_width)
    partial_value = jnp.einsum('gsw,gwd->gsd', context, w_out.reshape(groups, head_width, D), precision=highest)
    attended = low_back(lax.optimization_barrier(jnp.sum(low(partial_value), 0)))
    normed_first = norm_rows(x_row + attended + b_out, ln1_gain, ln1_bias)
    spread_first = low_back(jnp.broadcast_to(low(normed_first)[None], (groups, SEQ, D)))
    upper_act = jnp.einsum('gsd,dgf->gsf', spread_first, w_in.reshape(D, groups, ff_width), precision=highest)
    upper_act = low_back(upper_act + b_in.reshape(groups, 1, ff_width))
    hidden = low(jax.nn.gelu(upper_act, approximate=False) * unit_live.reshape(groups, 1, ff_width))
    part_ffn = jnp.einsum('gsf,gfd->gsd', hidden, w_down.reshape(groups, ff_width, D), precision=highest)
    ffn_branch = low_back(lax.optimization_barrier(jnp.sum(low(part_ffn), 0)))
    out_row = norm_rows(normed_first + ffn_branch + b_down, ln2_gain, ln2_bias)
    logits = jnp.dot(out_row, w_span, precision=highest)
    masked = jnp.where(valid[:, None], logits, -1000000000.0)
    span_max = lax.optimization_barrier(jnp.max(masked, 0, keepdims=True))
    log_total = span_max[0] + jnp.log(lax.optimization_barrier(jnp.sum(jnp.exp(masked - span_max), 0)))
    picked = lax.optimization_barrier(jnp.sum(jnp.where(positions[:, None] == answer_row[None, :], logits, 0.0), 0))
    return (out_row, jnp.sum(log_total - picked))

def forward(tokens_f, params, lengths, answer, head_live, unit_live):
    row_fn = jax.checkpoint(row_forward)

    def scan_step(scan_carry, scan_item):
        x_row, length, answer_row = scan_item
        return (scan_carry, row_fn(params, x_row, length, answer_row, head_live, unit_live))
    unused, results = lax.scan(scan_step, jnp.zeros((), jnp.float32), (tokens_f, lengths, answer))
    return results

def reference(tokens, lengths, answer, head_order, neuron_order, w_qkv, b_qv, w_out, b_out, ln1_gain, ln1_bias, w_in, b_in, w_down, b_down, ln2_gain, ln2_bias, w_span, out_grad):
    head_ids = jnp.arange(HEADS).astype(jnp.int32)
    head_live = jnp.any(head_order[:LIVE_HEADS][:, None] == head_ids[None, :], 0).astype(jnp.float32)
    unit_ids = jnp.arange(FF).astype(jnp.int32)
    unit_live = jnp.any(neuron_order[:LIVE_FF][:, None] == unit_ids[None, :], 0).astype(jnp.float32)
    params = tuple((item.astype(jnp.float32) for item in (w_qkv, b_qv, w_out, b_out, ln1_gain, ln1_bias, w_in, b_in, w_down, b_down, ln2_gain, ln2_bias, w_span)))

    def objective(tokens_f, params_f):
        return forward(tokens_f, params_f, lengths, answer, head_live, unit_live)
    (outs, losses), pullback = jax.vjp(objective, tokens.astype(jnp.float32), params)
    tokens_grad, grads = pullback((out_grad.astype(jnp.float32), jnp.ones_like(losses)))
    return (outs.astype(jnp.bfloat16), losses, tokens_grad, grads[0], grads[1], grads[2], grads[3], grads[4], grads[5], grads[6], grads[7], grads[8], grads[9], grads[10], grads[11], grads[12])
```

```python
import functools

import jax
import jax.numpy as jnp
from jax import lax
from jax.sharding import PartitionSpec as P

HEAD_DIM = 64
LIVE_HEADS = 6
LIVE_FF = 1536
UNIT_SLOTS = 448
MASKED = -1000000000.0

f32 = jnp.float32
bf16 = jnp.bfloat16
epsilon = 1e-12
highest = lax.Precision.HIGHEST


def norm_rows(values_in, norm_gain, norm_bias):
    row_mean = jnp.mean(values_in, -1, keepdims=True)
    centered = values_in - row_mean
    inv_std = lax.rsqrt(jnp.mean(centered * centered, -1, keepdims=True) + epsilon)
    normed = centered * inv_std
    return (normed * norm_gain + norm_bias, normed, inv_std)


def norm_back(grad_in, normed, inv_std, norm_gain):
    grad_normed = grad_in * norm_gain
    first_mean = jnp.mean(grad_normed, -1, keepdims=True)
    cross_mean = jnp.mean(grad_normed * normed, -1, keepdims=True)
    return inv_std * (grad_normed - first_mean - normed * cross_mean)


def gelu_slope(upper_act):
    cumulative = 0.5 * (1.0 + lax.erf(upper_act * 0.7071067811865476))
    density = jnp.exp(-0.5 * upper_act * upper_act) * 0.3989422804014327
    return cumulative + upper_act * density


def swap(x, axis, mask):
    return lax.ppermute(x, axis, [(i, i ^ mask) for i in range(lax.axis_size(axis))])


def masks_of(axis):
    return [1 << b for b in range((lax.axis_size(axis) - 1).bit_length())]


def bit_of(index, mask):
    return (index // mask) % 2


def pick(stacked, index):
    return lax.dynamic_index_in_dim(stacked, index, 0, keepdims=False)


def to_rows(x, rank):
    blocks = []
    for o in range(x.shape[0]):
        block = pick(x, rank ^ o)
        blocks.append(swap(block, "mp", o) if o else block)
    return jnp.concatenate(blocks, 0)


def from_rows(y, rank, rows):
    own = y.shape[0] // rows
    got = [y[o * own : (o + 1) * own] for o in range(rows)]
    got = [swap(block, "mp", o) if o else block for o, block in enumerate(got)]
    for mask in masks_of("mp"):
        moved = bit_of(rank, mask) == 1
        got = [jnp.where(moved, got[r ^ mask], got[r]) for r in range(rows)]
    return jnp.stack(got, 0)


def gather_blocks(block):
    blocks = [block]
    for mask in reversed(masks_of("mp")):
        far = [swap(b, "mp", mask) for b in blocks]
        blocks = [b for b in blocks] + far
    order = [0]
    for mask in reversed(masks_of("mp")):
        order = order + [o ^ mask for o in order]
    return [blocks[order.index(o)] for o in range(len(blocks))]


def reduce_blocks(blocks):
    terms = dict(enumerate(blocks))
    for mask in masks_of("mp"):
        far = [o for o in sorted(terms) if o & mask]
        got = swap(jnp.stack([terms[o].astype(bf16) for o in far]), "mp", mask)
        terms = {
            o: terms[o].astype(f32) + got[far.index(o ^ mask)].astype(f32)
            for o in terms
            if not o & mask
        }
    return terms[0]


def reduce_dp(total, dp_index):
    n = total.shape[0]
    top = n
    while top > 1:
        top //= 2
        bit = bit_of(dp_index, top)
        halves = total.reshape((2, top) + total.shape[1:])
        got = swap(pick(halves, 1 - bit).astype(bf16), "dp", top)
        total = pick(halves, bit).astype(f32) + got.astype(f32)
    total = total.astype(bf16)
    while top < n:
        total = jnp.concatenate([total, swap(total, "dp", top)], 0)
        top *= 2
    return total


def sum_all(x):
    for axis in ("mp", "dp"):
        for mask in masks_of(axis):
            x = x + swap(x, axis, mask)
    return x


def select_rows(one_hot, rows):
    return lax.dot_general(one_hot, rows, (((0,), (0,)), ((), ())), preferred_element_type=f32)


def program(
    slots,
    tokens,
    lengths,
    answer,
    head_order,
    neuron_order,
    w_qkv,
    b_qv,
    w_out,
    b_out,
    ln1_gain,
    ln1_bias,
    w_in,
    b_in,
    w_down,
    b_down,
    ln2_gain,
    ln2_bias,
    w_span,
    out_grad,
):
    rank = lax.axis_index("mp")
    dp_index = lax.axis_index("dp")
    ranks = lax.axis_size("mp")
    n_dp = lax.axis_size("dp")
    rows, own_len, model_dim = tokens.shape
    full_len = rows * own_len
    head_width = w_qkv.shape[2]
    group_heads = head_width // HEAD_DIM
    ff_width = w_in.shape[1]
    score_scale = HEAD_DIM ** (-0.5)

    x_row = to_rows(tokens, rank)
    spots = jnp.concatenate(
        [(rank ^ o) * own_len + jnp.arange(own_len, dtype=jnp.int32) for o in range(rows)]
    )
    length = pick(lengths, rank)
    row_answer = pick(answer, rank)
    key_valid = spots < length

    head_rows = w_qkv.reshape(model_dim, 3, group_heads, HEAD_DIM).transpose(2, 1, 3, 0)
    head_rows = jnp.concatenate(
        [head_rows, w_out.reshape(group_heads, 1, HEAD_DIM, model_dim)], 1
    ).reshape(group_heads, 4 * HEAD_DIM, model_dim)
    all_heads = jnp.concatenate(gather_blocks(head_rows), 0)
    live_heads = head_order[:LIVE_HEADS]
    live_spots = ((live_heads // group_heads) ^ rank) * group_heads + live_heads % group_heads
    head_w = jnp.stack([pick(all_heads, live_spots[k]) for k in range(LIVE_HEADS)])
    head_w = head_w.reshape(LIVE_HEADS, 4, HEAD_DIM, model_dim)
    b_qv_heads = b_qv.reshape(2, group_heads, HEAD_DIM).transpose(1, 0, 2)
    b_qv_heads = jnp.concatenate(gather_blocks(b_qv_heads), 0)
    head_b = jnp.stack([pick(b_qv_heads, live_spots[k]) for k in range(LIVE_HEADS)]).astype(f32)

    unit_ids = rank * ff_width + jnp.arange(ff_width, dtype=jnp.int32)
    unit_live = jnp.any(neuron_order[:LIVE_FF][:, None] == unit_ids[None, :], 0)
    slot_of = jnp.cumsum(unit_live.astype(jnp.int32)) - 1
    slot_ids = jnp.arange(slots, dtype=jnp.int32)
    chosen_units = (slot_of[:, None] == slot_ids[None, :]) & unit_live[:, None]
    unit_pick = chosen_units.astype(bf16)
    in_rows = lax.dot_general(
        unit_pick, w_in, (((0,), (1,)), ((), ())), preferred_element_type=f32
    ).astype(bf16)
    down_rows = select_rows(unit_pick, w_down).astype(bf16)
    slot_bias = jnp.sum(jnp.where(chosen_units, b_in.astype(f32)[:, None], 0.0), 0).astype(bf16)
    unit_in = jnp.concatenate(gather_blocks(in_rows), 0)
    unit_down = jnp.concatenate(gather_blocks(down_rows), 0)
    unit_bias = jnp.concatenate(gather_blocks(slot_bias), 0).astype(f32)

    projected = jnp.einsum("sd,hced->hcse", x_row, head_w[:, :3], preferred_element_type=f32)
    query = (projected[:, 0] + head_b[:, 0][:, None]).astype(bf16)
    key = projected[:, 1].astype(bf16)
    value = (projected[:, 2] + head_b[:, 1][:, None]).astype(bf16)
    scores = jnp.einsum("hqe,hke->hqk", query, key, preferred_element_type=f32) * score_scale
    masked = jnp.where(key_valid[None, None, :], scores, MASKED)
    row_max = jnp.max(masked, -1, keepdims=True)
    exp_scores = jnp.exp(masked - row_max)
    row_total = jnp.sum(exp_scores, -1, keepdims=True)
    probs = exp_scores / row_total
    probs_low = probs.astype(bf16)
    context = jnp.einsum("hqk,hke->hqe", probs_low, value, preferred_element_type=f32).astype(bf16)
    attended = jnp.einsum("hse,hed->sd", context, head_w[:, 3], preferred_element_type=f32)
    first_sum = x_row.astype(f32) + attended + b_out
    normed_first, first_unit, first_inv = norm_rows(first_sum, ln1_gain, ln1_bias)
    normed_low = normed_first.astype(bf16)

    upper = jnp.einsum("sd,fd->sf", normed_low, unit_in, preferred_element_type=f32) + unit_bias
    hidden = jax.nn.gelu(upper, approximate=False).astype(bf16)
    branch = jnp.einsum("sf,fd->sd", hidden, unit_down, preferred_element_type=f32)
    second_sum = normed_first + branch + b_down
    layer_out, second_unit, second_inv = norm_rows(second_sum, ln2_gain, ln2_bias)
    layer_out_own = from_rows(layer_out.astype(bf16), rank, rows)

    logits = jnp.einsum("sd,dc->sc", layer_out, w_span, precision=highest)
    span_masked = jnp.where(key_valid[:, None], logits, MASKED)
    span_max = jnp.max(span_masked, 0, keepdims=True)
    span_exp = jnp.exp(span_masked - span_max)
    span_total = jnp.sum(span_exp, 0, keepdims=True)
    chosen = spots[:, None] == row_answer[None, :]
    picked = jnp.sum(jnp.where(chosen, logits, 0.0), 0)
    row_loss = jnp.sum(span_max[0] + jnp.log(span_total[0]) - picked)
    losses = jnp.stack(gather_blocks(row_loss[None]), 0)[:, 0]
    losses = jnp.sum(
        jnp.where((jnp.arange(rows) ^ rank)[:, None] == jnp.arange(rows)[None, :], losses[:, None], 0.0), 0
    )
    grad_logits = span_exp / span_total - chosen.astype(f32)
    grad_out = to_rows(out_grad, rank).astype(f32) + jnp.einsum(
        "sc,dc->sd", grad_logits, w_span, precision=highest
    )
    span_grad = jnp.einsum("sd,sc->cd", layer_out, grad_logits, precision=highest)

    ln2_gain_grad = jnp.sum(grad_out * second_unit, 0)
    ln2_bias_grad = jnp.sum(grad_out, 0)
    grad_second = norm_back(grad_out, second_unit, second_inv, ln2_gain)
    b_down_grad = jnp.sum(grad_second, 0)
    grad_branch = grad_second.astype(bf16)
    down_grad = jnp.einsum("sf,sd->fd", hidden, grad_branch, preferred_element_type=f32)
    grad_hidden = jnp.einsum("sd,fd->sf", grad_branch, unit_down, preferred_element_type=f32)
    grad_upper = (grad_hidden * gelu_slope(upper)).astype(bf16)
    slot_bias_grad = jnp.sum(grad_upper, 0, dtype=f32)
    in_grad = jnp.einsum("sf,sd->fd", grad_upper, normed_low, preferred_element_type=f32)
    grad_first = grad_second + jnp.einsum(
        "sf,fd->sd", grad_upper, unit_in, preferred_element_type=f32
    )
    ln1_gain_grad = jnp.sum(grad_first * first_unit, 0)
    ln1_bias_grad = jnp.sum(grad_first, 0)
    grad_resid = norm_back(grad_first, first_unit, first_inv, ln1_gain)
    b_out_grad = jnp.sum(grad_resid, 0)
    grad_attended = grad_resid.astype(bf16)

    unit_grads = [
        jnp.concatenate([g[o * slots : (o + 1) * slots] for g in (in_grad, down_grad)], 0)
        for o in range(ranks)
    ]
    unit_grads = reduce_blocks(unit_grads).reshape(n_dp, 2 * slots // n_dp, model_dim)
    unit_grads = reduce_dp(unit_grads, dp_index).reshape(2 * slots, model_dim)
    piece = 2 * slots // n_dp
    natural = jnp.arange(2 * slots, dtype=jnp.int32)
    natural = ((natural // piece) ^ dp_index) * piece + natural % piece
    in_pick = ((slot_of[:, None] == natural[None, :]) & unit_live[:, None]).astype(bf16)
    down_pick = ((slot_of[:, None] + slots == natural[None, :]) & unit_live[:, None]).astype(bf16)
    w_in_grad = lax.dot_general(
        unit_grads, in_pick, (((0,), (1,)), ((), ())), preferred_element_type=f32
    )
    w_down_grad = lax.dot_general(
        down_pick, unit_grads, (((1,), (0,)), ((), ())), preferred_element_type=f32
    )

    out_grads = jnp.einsum("hse,sd->hed", context, grad_attended, preferred_element_type=f32)
    grad_context = jnp.einsum(
        "sd,hed->hse", grad_attended, head_w[:, 3], preferred_element_type=f32
    ).astype(bf16)
    grad_probs = jnp.einsum("hqe,hke->hqk", grad_context, value, preferred_element_type=f32)
    grad_value = jnp.einsum(
        "hqk,hqe->hke", probs_low, grad_context, preferred_element_type=f32
    ).astype(bf16)
    grad_scores = probs * (grad_probs - jnp.sum(grad_probs * probs, -1, keepdims=True))
    grad_scores = grad_scores.astype(bf16)
    grad_query = (
        jnp.einsum("hqk,hke->hqe", grad_scores, key, preferred_element_type=f32) * score_scale
    ).astype(bf16)
    grad_key = (
        jnp.einsum("hqk,hqe->hke", grad_scores, query, preferred_element_type=f32) * score_scale
    ).astype(bf16)
    grad_proj = jnp.stack([grad_query, grad_key, grad_value], 1)
    proj_grads = jnp.einsum("hcse,sd->hced", grad_proj, x_row, preferred_element_type=f32)
    head_grads = jnp.concatenate(
        [proj_grads.reshape(LIVE_HEADS, 3 * HEAD_DIM, model_dim), out_grads], 1
    ).astype(bf16)
    input_grad = jnp.einsum("hcse,hced->sd", grad_proj, head_w[:, :3], preferred_element_type=f32)
    tokens_grad = from_rows((grad_resid + input_grad).astype(bf16), rank, rows).astype(f32)

    all_spots = jnp.arange(ranks * group_heads, dtype=jnp.int32)
    head_hit = all_spots[:, None] == live_spots[None, :]
    spread = jnp.zeros((ranks * group_heads,) + head_grads.shape[1:], bf16)
    for k in range(LIVE_HEADS):
        spread = lax.dynamic_update_index_in_dim(spread, head_grads[k], live_spots[k], 0)
    spread = spread.reshape((ranks, group_heads) + head_grads.shape[1:])
    kept = group_heads * 4 * HEAD_DIM
    mine = reduce_blocks([spread[o] for o in range(ranks)])
    mine = reduce_dp(mine.reshape(n_dp, kept // n_dp, model_dim), dp_index)
    mine = mine.reshape(kept, model_dim)
    piece = kept // n_dp
    natural = jnp.arange(kept, dtype=jnp.int32)
    natural = ((natural // piece) ^ dp_index) * piece + natural % piece
    columns = jnp.arange(4 * head_width, dtype=jnp.int32)
    part, rest = columns // head_width, columns % head_width
    wanted = (rest // HEAD_DIM) * 4 * HEAD_DIM + part * HEAD_DIM + rest % HEAD_DIM
    row_pick = (natural[:, None] == wanted[None, :]).astype(bf16)
    w_qkv_grad = lax.dot_general(
        mine, row_pick[:, : 3 * head_width], (((0,), (0,)), ((), ())), preferred_element_type=f32
    ).reshape(model_dim, 3, head_width)
    w_out_grad = select_rows(row_pick[:, 3 * head_width :], mine)

    early = jnp.stack(
        [b_out_grad, ln1_gain_grad, ln1_bias_grad, b_down_grad, ln2_gain_grad, ln2_bias_grad]
    )
    block_hit = (jnp.arange(ranks) ^ rank)[:, None] == jnp.arange(ranks)[None, :]
    by_rank = jnp.sum(
        jnp.where(block_hit[:, :, None], slot_bias_grad.reshape(ranks, 1, slots), 0.0), 0
    )
    early = sum_all(jnp.concatenate([early.reshape(-1), span_grad.reshape(-1), by_rank.reshape(-1)]))
    shared = early[: 6 * model_dim].reshape(6, model_dim)
    w_span_grad = early[6 * model_dim : 8 * model_dim].reshape(2, model_dim).T
    my_slots = pick(early[8 * model_dim :].reshape(ranks, slots), rank)
    b_in_grad = jnp.sum(jnp.where(chosen_units, my_slots[None, :], 0.0), 1)
    late = jnp.stack(
        [jnp.sum(grad_query, 1, dtype=f32), jnp.sum(grad_value, 1, dtype=f32)]
    )
    head_ids = jnp.arange(ranks * group_heads, dtype=jnp.int32)
    late = jnp.sum(
        jnp.where((live_heads[:, None] == head_ids[None, :])[None, :, :, None], late[:, :, None], 0.0), 1
    )
    late = sum_all(late)
    b_qv_grad = lax.dynamic_slice_in_dim(late, rank * group_heads, group_heads, 1)
    b_qv_grad = b_qv_grad.reshape(2, head_width)
    return (
        layer_out_own,
        losses,
        tokens_grad,
        w_qkv_grad,
        b_qv_grad,
        w_out_grad,
        shared[0],
        shared[1],
        shared[2],
        w_in_grad,
        b_in_grad,
        w_down_grad,
        shared[3],
        shared[4],
        shared[5],
        w_span_grad,
    )


def shards(*args):
    neuron_order, w_in = args[4], args[11]
    ff_width = w_in.shape[1]
    owner = neuron_order[:LIVE_FF] // ff_width
    counts = jnp.sum(owner[:, None] == jnp.arange(lax.axis_size("mp"))[None, :], 0)
    if UNIT_SLOTS >= ff_width:
        return program(ff_width, *args)
    return lax.cond(
        jnp.max(counts) <= UNIT_SLOTS,
        functools.partial(program, UNIT_SLOTS),
        functools.partial(program, ff_width),
        *args,
    )


def solution(mesh):
    return jax.shard_map(
        shards,
        mesh=mesh,
        in_specs=(
            P("dp", "mp", None),
            P("dp"),
            P("dp", None),
            P(),
            P(),
            P(None, None, "mp"),
            P(None, "mp"),
            P("mp", None),
            P(),
            P(),
            P(),
            P(None, "mp"),
            P("mp"),
            P("mp", None),
            P(),
            P(),
            P(),
            P(),
            P("dp", "mp", None),
        ),
        out_specs=(
            P("dp", "mp", None),
            P("dp"),
            P("dp", "mp", None),
            P(None, None, "mp"),
            P(None, "mp"),
            P("mp", None),
            P(),
            P(),
            P(),
            P(None, "mp"),
            P("mp"),
            P("mp", None),
            P(),
            P(),
            P(),
            P(),
        ),
        check_vma=False,
    )
```

```python
import functools
import math

import jax
import jax.numpy as jnp
from jax import lax
from jax.experimental import pallas as pl
from jax.experimental.pallas import tpu as pltpu
from jax.sharding import PartitionSpec as P

HEAD_DIM = 64
LIVE_HEADS = 6
LIVE_FF = 1536
UNIT_SLOTS = 448
HEAD_SLOTS = 4
EXTRA = 16
MASKED = -1000000000.0
VMEM_MOST = 60 * 2**20
VMEM_SPARE = 10 * 2**20

f32 = jnp.float32
bf16 = jnp.bfloat16
i32 = jnp.int32
epsilon = 1e-12


def swap(x, axis, mask):
    return lax.ppermute(x, axis, [(i, i ^ mask) for i in range(lax.axis_size(axis))])


def masks_of(axis):
    return [1 << b for b in range((lax.axis_size(axis) - 1).bit_length())]


def bit_of(index, mask):
    return (index // mask) % 2


def pick(stacked, index):
    return lax.dynamic_index_in_dim(stacked, index, 0, keepdims=False)


def after(value, *others):
    return lax.optimization_barrier((value,) + others)[0]


def to_own(got, rank):
    for mask in masks_of("mp"):
        moved = bit_of(rank, mask) == 1
        got = [jnp.where(moved, got[r ^ mask], got[r]) for r in range(len(got))]
    return jnp.stack(got, 0)


def z_groups():
    masks = masks_of("dp")[1:]
    return [masks[i : i + 2] for i in range(0, len(masks), 2)]


def partner(group, j):
    return sum(m for i, m in enumerate(group) if (j >> (len(group) - 1 - i)) & 1)


def own_bits(group, dp_index):
    place = 0
    for mask in group:
        place = place * 2 + bit_of(dp_index, mask)
    return place


def join_sides(mine, other, right):
    return jnp.concatenate([jnp.where(right, other, mine), jnp.where(right, mine, other)], -1)


def gather_over(x, groups):
    for group in reversed(groups):
        got = [swap(x, "dp", partner(group, j)) for j in range(1, 1 << len(group))]
        x = jnp.concatenate([x] + got, -2)
    return x


def scatter_sum(x, got):
    x = x.astype(f32)
    for term in got:
        x = x + term.astype(f32)
    return x.astype(bf16)


def scatter_over(x, groups):
    for group in groups:
        n = 1 << len(group)
        rows = x.shape[-2] // n
        parts = [x[..., j * rows : (j + 1) * rows, :] for j in range(n)]
        x = scatter_sum(parts[0], [swap(parts[j], "dp", partner(group, j)) for j in range(1, n)])
    return x


class Incoming:
    def __init__(self, source, held, sem):
        self.copy, self.held, self.waiting = pltpu.make_async_copy(source, held, sem), held, True
        self.shape = held.shape
        self.copy.start()

    def ready(self):
        if self.waiting:
            self.copy.wait()
            self.waiting = False
        return self.held

    def __getitem__(self, index):
        return self.ready()[index]

    @property
    def at(self):
        return self.ready().at


class Outgoing:
    def __init__(self, held, target, sem):
        self.held, self.target, self.sem, self.sent = held, target, sem, False
        self.shape, self.at = held.shape, held.at

    def __getitem__(self, index):
        return self.held[index]

    def __setitem__(self, index, value):
        self.held[index] = value

    def send(self, *index):
        self.sent = True
        if index:
            pltpu.make_async_copy(self.held.at[index], self.target.at[index], self.sem).start()
        else:
            pltpu.make_async_copy(self.held, self.target, self.sem).start()

    def wait(self):
        if not self.sent:
            self.send()
        pltpu.make_async_copy(self.held, self.target, self.sem).wait()


def ready(*refs):
    for ref in refs:
        if isinstance(ref, Incoming):
            ref.ready()


def send(*refs):
    for ref in refs:
        if isinstance(ref, Outgoing):
            ref.send()


def held(item):
    dims, size = item.shape, jnp.dtype(item.dtype).itemsize
    if len(dims) < 2:
        return 4096
    tall = 32 // size
    return -(-dims[-1] // 128) * 128 * (-(-dims[-2] // tall) * tall) * size * math.prod(dims[:-2])


def shape(dims, kind):
    return jax.ShapeDtypeStruct(dims, kind)


PLACES = {"v": pltpu.VMEM, "b": pltpu.HBM}


def call(pin, kernel, name, ins, outs, scratch=(), flops=1e6, moved=5e6):
    in_kinds = [k if k != "v" or pin else "h" for k, _ in ins]
    out_kinds = [k if k != "v" or pin else "h" for k, _, _ in outs]
    args = [
        pltpu.with_memory_space_constraint(a, PLACES[k]) if k in PLACES else a
        for k, (_, a) in zip(in_kinds, ins)
    ]
    out_shape = [
        PLACES[k](d, t) if k in PLACES else shape(d, t) for k, (_, d, t) in zip(out_kinds, outs)
    ]
    buffers = [shape(a.shape, a.dtype) for k, a in zip(in_kinds, args) if k in "hb"]
    buffers += [shape(d, t) for k, (_, d, t) in zip(out_kinds, outs) if k in "hb"]
    scratch = [shape(d, t) for d, t in scratch]
    count, outs_count = len(in_kinds), len(out_kinds)

    def whole(*refs):
        given, results, refs = refs[:count], refs[count : count + outs_count], refs[count + outs_count :]
        bufs, refs = iter(refs[: len(buffers)]), refs[len(buffers) :]
        in_sem, out_sem = refs[:2]
        given = [
            Incoming(ref, next(bufs), in_sem.at[i]) if k in "hb" else ref
            for i, (k, ref) in enumerate(zip(in_kinds, given))
        ]
        results = [
            Outgoing(next(bufs), ref, out_sem.at[i]) if k in "hb" else ref
            for i, (k, ref) in enumerate(zip(out_kinds, results))
        ]
        kernel(*given, *results, *refs[2:])
        ready(*given)
        for ref in results:
            if isinstance(ref, Outgoing):
                ref.wait()

    spaces = {"s": pltpu.SMEM, "v": pltpu.VMEM, "h": pl.ANY, "b": pltpu.HBM}
    limit = sum(held(b) for b in buffers + scratch) + VMEM_SPARE
    return pl.pallas_call(
        whole,
        name=name,
        out_shape=out_shape,
        in_specs=[pl.BlockSpec(memory_space=spaces[k]) for k in in_kinds],
        out_specs=[pl.BlockSpec(memory_space=spaces[k]) for k in out_kinds],
        scratch_shapes=[pltpu.VMEM(b.shape, b.dtype) for b in buffers]
        + [pltpu.SemaphoreType.DMA((count,)), pltpu.SemaphoreType.DMA((outs_count,))]
        + [pltpu.SMEM(s.shape, s.dtype) if s.dtype == i32 else pltpu.VMEM(s.shape, s.dtype) for s in scratch],
        compiler_params=pltpu.CompilerParams(vmem_limit_bytes=min(VMEM_MOST, int(limit))),
        cost_estimate=pl.CostEstimate(flops=int(flops), bytes_accessed=int(moved), transcendentals=0),
    )(*args)


def row_sum(v):
    return jnp.sum(v, 0, keepdims=True)


def lane_mean(v):
    return jnp.mean(v, -1, keepdims=True)


def two_parts(x):
    high = x.astype(bf16)
    low = (x - high.astype(f32)).astype(bf16)
    return jnp.concatenate([high, low], 0), high.astype(f32) + low.astype(f32)


def one_part(x):
    half = x.shape[0] // 2
    return x[:half].astype(f32) + x[half:].astype(f32)


def mxu(a, b, a_dim, b_dim):
    return lax.dot_general(a, b, (((a_dim,), (b_dim,)), ((), ())), preferred_element_type=f32)


def loop(count, body):
    def step(i, carry):
        body(i)
        return carry

    lax.fori_loop(0, count, step, 0)


def span_of(i, size):
    return pl.ds(pl.multiple_of(i * size, size), size)


def by_rows(full, size, body):
    loop(full // size, lambda i: body(span_of(i, size)))


def fits_kernel(unit_slots, head_slots, ff_width, pair_heads, ranks, heads_ref, order_ref, fits_ref):
    order = order_ref[...]
    most = jnp.zeros((1, 1), f32)
    for r in range(ranks):
        mine = (order >= r * ff_width) & (order < (r + 1) * ff_width)
        most = jnp.maximum(most, jnp.sum(jnp.where(mine, 1.0, 0.0), keepdims=True))
    fine = jnp.where(most[0, 0] <= unit_slots, 1, 0)
    for pair in range(ranks // 2):
        count = 0
        for k in range(LIVE_HEADS):
            count += jnp.where(heads_ref[k] // pair_heads == pair, 1, 0)
        fine *= jnp.where(count <= head_slots, 1, 0)
    fits_ref[0] = fine


def pack_kernel(place_ref, order_ref, qkv_ref, far_qkv_ref, out_ref, far_out_ref, *refs):
    own_ref, send_ref, heads_ref, slots_ref, table_ref = refs
    group = out_ref.shape[0] // HEAD_DIM
    rank = place_ref[0]
    core, pair = rank % 2, rank // 2
    counts = {}
    for head in range(order_ref.shape[0]):
        count = counts.get(head // (2 * group), 0)
        live = 0
        for k in range(LIVE_HEADS):
            live += jnp.where(order_ref[k] == head, 1, 0)
        table_ref[head] = jnp.where(live > 0, count, -1)
        counts[head // (2 * group)] = count + live
    for side in range(2):
        for e in range(own_ref.shape[0]):
            heads_ref[side, e] = -1
    for k in range(LIVE_HEADS):
        head = order_ref[k]
        slot = table_ref[head]
        side = jnp.where(head // (2 * group) != pair, 1, 0)
        heads_ref[side, slot ^ core] = head
    own_ref[...] = jnp.zeros(own_ref.shape, bf16)
    send_ref[...] = jnp.zeros(send_ref.shape, bf16)
    square = (HEAD_DIM, HEAD_DIM)
    diagonal = lax.broadcasted_iota(i32, square, 0) == lax.broadcasted_iota(i32, square, 1)
    diagonal = jnp.where(diagonal, 1.0, 0.0).astype(bf16)
    ready(qkv_ref, far_qkv_ref, out_ref, far_out_ref)
    for side, (qkv, out) in enumerate(((qkv_ref, out_ref), (far_qkv_ref, far_out_ref))):
        for g in range(group):
            slot = table_ref[(rank ^ side) * group + g]
            if side == 0:
                slots_ref[g] = slot

            @pl.when(slot >= 0)
            def keep():
                at = slice(g * HEAD_DIM, (g + 1) * HEAD_DIM)
                parts = [mxu(diagonal, qkv[c, :, at], 1, 1).astype(bf16) for c in range(3)]
                head = jnp.concatenate(parts + [out[at]], 0)
                own_ref[slot ^ core] = head

                @pl.when(slot % 2 == core)
                def sent():
                    send_ref[slot // 2] = head


def units_kernel(zbits, place_ref, order_ref, in_ref, down_ref, *refs):
    sides_ref, pick_ref, rows_in_ref, rows_down_ref, at_ref = refs
    slots, width = pick_ref.shape
    side = sides_ref.shape[2]
    piece = slots >> zbits
    rank, dp_index = place_ref[0], place_ref[1]
    lanes = at_ref.shape[1]
    per = width // lanes
    order = order_ref[...]

    def hot(dims, index):
        return jnp.where(lax.broadcasted_iota(i32, dims, 0) == index, 1.0, 0.0).astype(bf16)

    count = order.shape[1]
    row_hot = hot((at_ref.shape[0], count), order // lanes)
    lane_hot = hot((lanes, count), order % lanes)
    live = mxu(row_hot, lane_hot, 1, 1)
    square = (lanes, lanes)
    first, second = (lax.broadcasted_iota(i32, square, d) for d in range(2))
    upto = jnp.where(first <= second, 1.0, 0.0).astype(bf16)
    within = mxu(live.astype(bf16), upto, 1, 0)
    totals = mxu(live.astype(bf16), jnp.ones(square, bf16), 1, 0)
    square = (at_ref.shape[0], at_ref.shape[0])
    first, second = (lax.broadcasted_iota(i32, square, d) for d in range(2))
    earlier = (second < first) & (second // per == first // per)
    offsets = mxu(jnp.where(earlier, 1.0, 0.0).astype(bf16), totals.astype(bf16), 1, 0)
    slot = (offsets + within).astype(i32) - 1
    index = jnp.zeros(slot.shape, i32)
    for p in range(1, slots // piece):
        index += jnp.where(slot >= p * piece, 1, 0)
    inside = slot - index * piece
    index = index ^ (dp_index // 2)
    place = jnp.zeros(slot.shape, i32)
    for b in range(zbits):
        place = place * 2 + ((index >> b) & 1)
    at_ref[...] = jnp.where(live > 0.5, place * piece + inside, -1)
    ids = lax.broadcasted_iota(i32, (slots, lanes), 0)
    for c in range(per):
        row = at_ref[pl.ds(rank * per + c, 1)]
        pick_ref[:, c * lanes : (c + 1) * lanes] = jnp.where(ids == row, 1.0, 0.0).astype(bf16)
    right = dp_index % 2 == 1
    rows_in = mxu(pick_ref[...], in_ref[...], 1, 1).astype(bf16)
    sides_ref[0] = jnp.where(right, rows_in[:, side:], rows_in[:, :side])
    rows_in_ref[...] = rows_in
    rows_down = mxu(pick_ref[...], down_ref[...], 1, 0).astype(bf16)
    sides_ref[1] = jnp.where(right, rows_down[:, side:], rows_down[:, :side])
    rows_down_ref[...] = rows_down


def source_of(sources, j, i):
    return sources[0].at[2 * j + i] if len(sources) == 1 else sources[i].at[j]


def each_head(heads_ref, side, body):
    def two(j):
        for i in range(2):
            pl.when(heads_ref[side, 2 * j + i] >= 0)(functools.partial(body, j, i))

    loop(heads_ref.shape[1] // 2, two)


def out_rows(sources, slots):
    parts = [source_of(sources, e // 2, e % 2)[3 * HEAD_DIM :] for e in range(slots)]
    return jnp.concatenate(parts, 0)


def attend_heads(side, x_ref, heads_ref, valid, bias_ref, sources, outs):
    q_ref, k_ref, v_ref, probs_ref, ctx_ref = outs
    wide = 3 * HEAD_DIM
    half = x_ref.shape[0] // 2
    ctx_ref[...] = jnp.zeros(ctx_ref.shape, bf16)

    def attend_head(j, i):
        e = 2 * j + i
        bias = bias_ref[side, e]
        both = mxu(x_ref[...], source_of(sources, j, i)[:wide], 1, 1)
        query = (both[:, :HEAD_DIM] + bias[0:1]).astype(bf16)
        key = both[:, HEAD_DIM : 2 * HEAD_DIM].astype(bf16)
        value = (both[:, 2 * HEAD_DIM :] + bias[1:2]).astype(bf16)
        q_ref[e], k_ref[e], v_ref[e] = query, key, value
        for c in range(2):
            part = slice(c * half, (c + 1) * half)
            scores = mxu(key, query[part], 1, 1) * HEAD_DIM ** (-0.5)
            scores = jnp.where(valid, scores, MASKED)
            exp_scores = jnp.exp(scores - jnp.max(scores, 0, keepdims=True))
            probs = (exp_scores * (1.0 / row_sum(exp_scores))).astype(bf16)
            probs_ref[e, :, part] = probs
            ctx_ref[span_of(e, HEAD_DIM), part] = mxu(value, probs, 0, 0).astype(bf16)

    each_head(heads_ref, side, attend_head)
    return mxu(ctx_ref[...], out_rows(sources, heads_ref.shape[1]), 0, 0)


def attend_own_kernel(own, heads_ref, length_ref, spots_ref, bias_ref, *refs):
    blocks, source, refs = refs[:-8], refs[-8:-7], refs[-7:]
    part_ref, x_ref = refs[:2]
    for o, block in enumerate(blocks):
        x_ref[o * own : (o + 1) * own] = block[:own]
    valid = spots_ref[...] < length_ref[0]
    ready(bias_ref, *source)
    part_ref[...] = attend_heads(0, x_ref, heads_ref, valid, bias_ref, source, refs[2:])


def attend_kernel(heads_ref, length_ref, spots_ref, bias_ref, vec_ref, part_ref, x_ref, *refs):
    sources, refs = refs[:2], refs[2:]
    unit_ref, inv_ref, low_ref, sum_ref = refs[:3] + refs[-1:]
    valid = spots_ref[...] < length_ref[0]
    ready(bias_ref, vec_ref, part_ref, x_ref, *sources)
    sum_ref[...] = attend_heads(1, x_ref, heads_ref, valid, bias_ref, sources, refs[3:-1])

    def norm(rows):
        first_sum = x_ref[rows].astype(f32) + (part_ref[rows] + sum_ref[rows]) + vec_ref[0:1]
        centered = first_sum - lane_mean(first_sum)
        inv = lax.rsqrt(lane_mean(centered * centered) + epsilon)
        unit = centered * inv
        unit_ref[rows] = unit
        inv_ref[rows] = inv
        low_ref[rows] = (unit * vec_ref[1:2] + vec_ref[2:3]).astype(bf16)

    by_rows(sum_ref.shape[0], 128, norm)


def join_block(target, mine, other, kind, right):
    half = mine.shape[-1]
    one, two = mine[kind], other[kind]
    target[:, :half] = jnp.where(right, two, one)
    target[:, half:] = jnp.where(right, one, two)


def feed_kernel(scalar_ref, low_ref, unit_ref, vec_ref, bias_ref, *refs):
    near_units, sides, refs = refs[:4], refs[4:8], refs[8:]
    spots_ref, span_ref, refs = refs[0], refs[1], refs[2:]
    grads, refs = refs[:-15], refs[-15:]
    far_ref, near_ref, out_ref, loss_ref, small_ref, second_ref, upper_ref, ins_ref = refs[:8]
    downs_ref, hidden_ref, slope_ref, total_ref, layer_ref, two_ref, logit_ref = refs[8:]
    full = low_ref.shape[0]
    half = full // 2
    right = scalar_ref[3] == 1
    ready(low_ref, unit_ref, vec_ref, bias_ref, *near_units)

    def first(rows):
        total_ref[rows] = unit_ref[rows] * vec_ref[1:2] + vec_ref[2:3] + vec_ref[3:4]

    by_rows(full, 128, first)
    for o in range(2):
        ins_ref[o] = near_units[o][...]
        downs_ref[o] = near_units[2 + o][...]

    def forward(o):
        for r in range(2):
            rows = slice(r * half, (r + 1) * half)
            upper = mxu(low_ref[rows], ins_ref[o], 1, 1) + bias_ref[pl.ds(o, 1)]
            cumulative = 0.5 * (1.0 + lax.erf(upper * 0.7071067811865476))
            density = jnp.exp(-0.5 * upper * upper) * 0.3989422804014327
            hidden = (upper * cumulative).astype(bf16)
            hidden_ref[o, rows] = hidden
            slope_ref[o, rows] = (cumulative + upper * density).astype(bf16)
            total_ref[rows] += mxu(hidden, downs_ref[o], 1, 0)

    loop(2, forward)
    ready(*sides)
    for o in range(2):
        join_block(ins_ref.at[2 + o], sides[2 * o], sides[2 * o + 1], 0, right)
        join_block(downs_ref.at[2 + o], sides[2 * o], sides[2 * o + 1], 1, right)
    loop(2, lambda o: forward(o + 2))
    ready(spots_ref, span_ref, *grads)

    def norm(rows):
        second_sum = total_ref[rows]
        centered = second_sum - lane_mean(second_sum)
        inv = lax.rsqrt(lane_mean(centered * centered) + epsilon)
        unit = centered * inv
        layer_out = unit * vec_ref[4:5] + vec_ref[5:6]
        two_ref[rows] = unit
        layer_ref[rows] = layer_out
        out_ref[rows] = layer_out.astype(bf16)
        logit_ref[rows, 2:3] = inv
        for c in range(2):
            logit_ref[rows, c : c + 1] = jnp.sum(layer_out * span_ref[c : c + 1], -1, keepdims=True)

    by_rows(full, 128, norm)
    small_ref[...] = jnp.zeros(small_ref.shape, f32)
    spots = spots_ref[...]
    valid = spots < scalar_ref[0]
    loss = jnp.zeros((1, 1), f32)
    for c in range(2):
        logits = logit_ref[:, c : c + 1]
        masked = jnp.where(valid, logits, MASKED)
        top = jnp.max(masked, 0, keepdims=True)
        exp_logits = jnp.exp(masked - top)
        total = row_sum(exp_logits)
        chosen = spots == scalar_ref[1 + c]
        loss += top + jnp.log(total) - row_sum(jnp.where(chosen, logits, 0.0))
        logit_ref[:, c : c + 1] = exp_logits / total - jnp.where(chosen, 1.0, 0.0)
    loss_ref[...] = loss
    own = full // len(grads)
    for o, grad in enumerate(grads):
        rows = slice(o * own, (o + 1) * own)
        unit, layer_out, inv = two_ref[rows], layer_ref[rows], logit_ref[rows, 2:3]
        grad_out = grad[...].astype(f32)
        for c in range(2):
            grad_logits = logit_ref[rows, c : c + 1]
            grad_out += grad_logits * span_ref[c : c + 1]
            small_ref[3 + c : 4 + c] += row_sum(layer_out * grad_logits)
        small_ref[0:1] += row_sum(grad_out * unit)
        small_ref[1:2] += row_sum(grad_out)
        grad_normed = grad_out * vec_ref[4:5]
        second = inv * (
            grad_normed - lane_mean(grad_normed) - unit * lane_mean(grad_normed * unit)
        )
        second_ref[rows] = second
        small_ref[2:3] += row_sum(second)

    def backward(j):
        branch_grad = second_ref[...].astype(bf16)
        for i in range(2):
            o = 2 * j + i
            hidden_grad = mxu(branch_grad, downs_ref[o], 1, 1)
            upper = (hidden_grad * slope_ref[o].astype(f32)).astype(bf16)
            upper_ref[o] = upper
            target = far_ref if i else near_ref
            target[1, j] = mxu(hidden_ref[o], branch_grad, 0, 0).astype(bf16)
            target[0, j] = mxu(upper, low_ref[...], 0, 0).astype(bf16)

    loop(2, backward)


def feed_back_kernel(upper_ref, ins_ref, second_ref, unit_ref, inv_ref, vec_ref, *refs):
    small_ref, resid_ref, att_ref, bias_ref, first_ref = refs
    ready(upper_ref, ins_ref, second_ref)
    first_ref[...] = second_ref[...]

    def back(o):
        upper = upper_ref[o]
        first_ref[...] += mxu(upper, ins_ref[o], 1, 0)
        bias_ref[pl.ds(o, 1)] = row_sum(upper.astype(f32))

    loop(upper_ref.shape[0], back)
    ready(unit_ref, inv_ref, vec_ref)
    small_ref[...] = jnp.zeros(small_ref.shape, f32)

    def norm(rows):
        first, unit = first_ref[rows], unit_ref[rows]
        grad_normed = first * vec_ref[1:2]
        resid = inv_ref[rows] * (
            grad_normed - lane_mean(grad_normed) - unit * lane_mean(grad_normed * unit)
        )
        resid_ref[rows] = resid
        att_ref[rows] = resid.astype(bf16)
        small_ref[0:1] += row_sum(first * unit)
        small_ref[1:2] += row_sum(first)
        small_ref[2:3] += row_sum(resid)

    by_rows(first_ref.shape[0], 128, norm)


def merge_kernel(right_ref, near_ref, got_ref, *refs):
    down_send_ref, in_send_ref, down_keep_ref, in_keep_ref = refs
    right = right_ref[0] == 1
    half = in_send_ref.shape[-1]
    ready(near_ref, got_ref)

    def total(kind, o, rows):
        return (near_ref[kind, o, rows].astype(f32) + got_ref[kind, o, rows].astype(f32)).astype(bf16)

    def merge(rows):
        down_send_ref[rows] = total(1, 1, rows)
        down_keep_ref[rows] = total(1, 0, rows)
        for o in range(2):
            block = total(0, o, rows)
            in_send_ref[o, rows] = jnp.where(right, block[:, :half], block[:, half:])
            in_keep_ref[o, rows] = jnp.where(right, block[:, half:], block[:, :half])

    by_rows(down_send_ref.shape[0], down_send_ref.shape[0] // 4, merge)


def second_merge_kernel(right_ref, down_ref, down_got_ref, in_ref, in_got_ref, *refs):
    down_send_ref, down_keep_ref, parts = refs[0], refs[1], refs[2:]
    right = right_ref[0] == 1
    half = down_send_ref.shape[-1]
    each = parts[0].shape[1]
    for j in range(1, len(parts) + 1):
        j %= len(parts)
        rows = slice(j * each, (j + 1) * each)
        for o in range(2):
            parts[j][o] = (in_ref[o, rows].astype(f32) + in_got_ref[o, rows].astype(f32)).astype(bf16)
        send(parts[j])
        block = (down_ref[rows].astype(f32) + down_got_ref[rows].astype(f32)).astype(bf16)
        down_send_ref[rows] = jnp.where(right, block[:, :half], block[:, half:])
        down_keep_ref[rows] = jnp.where(right, block[:, half:], block[:, :half])


def third_merge_kernel(down_ref, down_got_ref, in_ref, *refs):
    count = down_ref.shape[0] // in_ref.shape[1]
    gots, parts, ins = refs[: count - 1], refs[count - 1 : -2], refs[-2:]
    each = in_ref.shape[1]
    for j in range(1, count + 1):
        j %= count
        rows = slice(j * each, (j + 1) * each)
        parts[j][...] = (down_ref[rows].astype(f32) + down_got_ref[rows].astype(f32)).astype(bf16)
        send(parts[j])
    for o in range(2):
        total = in_ref[o].astype(f32)
        for got in gots:
            total += got[o].astype(f32)
        ins[o][...] = total.astype(bf16)


def attend_back_kernel(own, heads_ref, att_ref, resid_ref, x_ref, *refs):
    sides = ((refs[:5], refs[5:6]), (refs[6:11], refs[11:13]))
    layer_ref, far_ref, near_ref, late_ref = refs[13:17]
    moved, total_ref = refs[17:-1], refs[-1]
    wide = 3 * HEAD_DIM
    scale = HEAD_DIM ** (-0.5)
    _, half_slots, tall, width = near_ref.shape
    lane_head = lax.broadcasted_iota(i32, (1, width), 1) // HEAD_DIM
    slots = heads_ref.shape[1]
    late_ref[...] = jnp.zeros(late_ref.shape, f32)
    far_ref[...] = jnp.zeros(far_ref.shape, bf16)
    near_ref[...] = jnp.zeros(near_ref.shape, bf16)
    full = x_ref.shape[0]
    half = full // 2
    ready(att_ref, resid_ref, x_ref)
    total_ref[...] = resid_ref[...]
    for side, (saved, sources) in enumerate(sides):
        q_ref, k_ref, v_ref, probs_ref, ctx_ref = saved
        ready(*saved, *sources)
        out_grads = mxu(ctx_ref[...], att_ref[...], 1, 0).astype(bf16)
        for e in range(slots):
            part = out_grads[e * HEAD_DIM : (e + 1) * HEAD_DIM]
            at = (side * half_slots + e // 2) * tall + wide
            if e % 2:
                far_ref[at : at + HEAD_DIM] = part
            else:
                near_ref[side, e // 2, wide:] = part

        def back_head(j, i):
            e = 2 * j + i
            source = source_of(sources, j, i)
            ctx_grad = mxu(att_ref[...], source[wide:], 1, 1).astype(bf16)
            query, key, value = q_ref[e], k_ref[e], v_ref[e]
            grad_key = grad_value = None
            grad_query = []
            for c in range(2):
                part = slice(c * half, (c + 1) * half)
                probs_low = probs_ref[e, :, part]
                probs = probs_low.astype(f32)
                grad_probs = mxu(value, ctx_grad[part], 1, 1)
                grad_scores = probs * (grad_probs - row_sum(grad_probs * probs))
                grad_scores = grad_scores.astype(bf16)
                value_term = mxu(probs_low, ctx_grad[part], 1, 0)
                key_term = mxu(grad_scores, query[part], 1, 0)
                grad_value = value_term if grad_value is None else grad_value + value_term
                grad_key = key_term if grad_key is None else grad_key + key_term
                grad_query.append(mxu(grad_scores, key, 0, 0))
            grad_query = jnp.concatenate(grad_query, 0)
            grads = jnp.concatenate([grad_query * scale, grad_key * scale, grad_value], 1)
            grads = grads.astype(bf16)
            sums = row_sum(grads.astype(f32))
            for n in range(2):
                part = sums[:, 2 * n * HEAD_DIM : (2 * n + 1) * HEAD_DIM]
                spread = jnp.concatenate([part] * (width // HEAD_DIM), 1)
                late_ref[n : n + 1] += jnp.where(lane_head == heads_ref[side, e], spread, 0.0)
            total_ref[...] += mxu(grads, source[:wide], 1, 0)
            rows = mxu(grads, x_ref[...], 0, 0).astype(bf16)
            if i:
                at = pl.multiple_of((side * half_slots + j) * tall, tall)
                far_ref[pl.ds(at, wide)] = rows
            else:
                near_ref[side, j, :wide] = rows

        each_head(heads_ref, side, back_head)
    send(far_ref)
    ready(layer_ref)
    for o, ref in enumerate(moved):
        at = slice(o * own, (o + 1) * own)
        ref[0] = layer_ref[at]
        ref[1] = total_ref[at].astype(bf16)


def first_hop_kernel(near_ref, got_ref, small_ref, small_got_ref, send_ref, keep_ref, sum_ref):
    _, half_slots, tall, _ = near_ref.shape
    rows = keep_ref.shape[0]
    ready(near_ref, got_ref)

    def add(side, j, target):
        at = pl.multiple_of(j * tall, tall)
        got = got_ref[pl.ds(side * rows + at, tall)]
        target[pl.ds(at, tall)] = (near_ref[side, j].astype(f32) + got.astype(f32)).astype(bf16)

    loop(half_slots, lambda j: add(1, j, send_ref))
    send_ref[rows:], sum_ref[...] = two_parts(small_ref[...] + one_part(small_got_ref[...]))
    send(send_ref)
    loop(half_slots, lambda j: add(0, j, keep_ref))


def hop_kernel(parts, own_ref, keep_ref, small_ref, *refs):
    gots, refs = refs[: -parts - 1], refs[-parts - 1 :]
    sends, mine_ref, sum_ref = refs[: parts - 1], refs[-2], refs[-1]
    rows = keep_ref.shape[0]
    ready(keep_ref, *gots)
    small = [small_ref[...]] + [one_part(got[rows:]) for got in gots]
    while len(small) > 1:
        small = [small[i] + small[i + 1] for i in range(0, len(small), 2)]
    low, sum_ref[...] = two_parts(small[0])
    own = own_ref[0]
    each = rows // parts
    for j in range(1, parts + 1):
        j %= parts
        at = span_of(own ^ j, each)
        total = keep_ref[at].astype(f32)
        for got in gots:
            total += got[at].astype(f32)
        if j == 0:
            mine_ref[...] = total.astype(bf16)
        else:
            sends[j - 1][:each] = total.astype(bf16)
            sends[j - 1][each:] = low
            send(sends[j - 1])


def plain_hop(parts, own, keep, small, gots):
    rows, width = keep.shape
    small = [small] + [one_part(got[rows:]) for got in gots]
    while len(small) > 1:
        small = [small[i] + small[i + 1] for i in range(0, len(small), 2)]
    high = lax.reduce_precision(small[0], 8, 7)
    low = lax.reduce_precision(small[0] - high, 8, 7)
    total = keep.astype(f32)
    for got in gots:
        total += got[:rows].astype(f32)
    total = total.astype(bf16).reshape(parts, rows // parts, width)
    sent = jnp.concatenate([high, low], 0).astype(bf16)
    sends = [jnp.concatenate([pick(total, own[0] ^ j), sent], 0) for j in range(1, parts)]
    return sends + [pick(total, own[0]), high + low]


def hop(pin, parts, own, keep, small, gots):
    rows, width = keep.shape
    each = rows // parts
    if each % 16:
        return plain_hop(parts, own, keep, small, gots)
    tall = 2 * small.shape[0]
    return call(
        pin,
        functools.partial(hop_kernel, parts),
        "hop",
        [("s", own), ("v", keep), ("v", small)] + [("h", got) for got in gots],
        [("h", (each + tall, width), bf16)] * (parts - 1)
        + [("v", (each, width), bf16) if parts > 1 else ("h", (each, width), bf16)]
        + [("v", small.shape, f32) if parts > 1 else ("h", small.shape, f32)],
    )


def program(
    slots,
    head_slots,
    pin,
    tokens,
    lengths,
    answer,
    head_order,
    neuron_order,
    w_qkv,
    b_qv,
    w_out,
    b_out,
    ln1_gain,
    ln1_bias,
    w_in,
    b_in,
    w_down,
    b_down,
    ln2_gain,
    ln2_bias,
    w_span,
    out_grad,
):
    rank = lax.axis_index("mp")
    dp_index = lax.axis_index("dp")
    ranks = lax.axis_size("mp")
    n_dp = lax.axis_size("dp")
    rows, own_len, model_dim = tokens.shape
    full = rows * own_len
    head_width = w_qkv.shape[2]
    group_heads = head_width // HEAD_DIM
    all_heads = ranks * group_heads
    ff_width = w_in.shape[1]
    half_slots = head_slots // 2
    core = rank % 2
    others = [rank ^ o for o in range(rows)]
    right = bit_of(dp_index, 1) == 1
    right_one = right.astype(i32)[None]
    groups = z_groups()
    pieces = n_dp // 2
    piece = slots // pieces
    place = jnp.stack([rank, dp_index]).astype(i32)
    lanes = 128

    qkv = w_qkv.transpose(1, 0, 2)
    far_qkv, far_out = swap(qkv, "mp", 1), swap(w_out, "mp", 1)
    extra = jnp.concatenate(
        [
            jnp.pad(b_in[None], ((0, 0), (0, model_dim - ff_width))),
            jnp.pad(b_qv.reshape(1, -1), ((0, 0), (0, model_dim - 2 * head_width))),
            jnp.zeros((EXTRA - 2, model_dim), bf16),
        ],
        0,
    )
    sent_blocks = [jnp.concatenate([pick(tokens, other), extra], 0) for other in others]
    blocks = [swap(block, "mp", o) if o else block for o, block in enumerate(sent_blocks)]

    unit_order = after(neuron_order[:LIVE_FF][None], *sent_blocks)
    sent_units, unit_pick, in_rows, down_rows, unit_at = call(
        pin,
        functools.partial(units_kernel, (pieces - 1).bit_length()),
        "units",
        [("s", place), ("h", unit_order), ("h", w_in), ("h", w_down)],
        [
            ("h", (2, slots, model_dim // 2), bf16),
            ("h", (slots, ff_width), bf16),
            ("h", (slots, model_dim), bf16),
            ("h", (slots, model_dim), bf16),
            ("h", (ranks * ff_width // lanes, lanes), i32),
        ],
    )
    far_units = swap(sent_units, "mp", 2)

    tall = 4 * HEAD_DIM
    own_heads, sent_heads, heads, my_slots = call(
        pin,
        pack_kernel,
        "pack",
        [("s", place), ("s", head_order), ("h", after(qkv, sent_units))]
        + [("h", far_qkv), ("h", w_out), ("h", far_out)],
        [
            ("v", (head_slots, tall, model_dim), bf16),
            ("h", (half_slots, tall, model_dim), bf16),
            ("s", (2, head_slots), i32),
            ("s", (group_heads,), i32),
        ],
        [((all_heads,), i32)],
    )
    across = swap(sent_heads, "mp", 2)
    near_units = [swap(in_rows, "mp", 1), swap(down_rows, "mp", 1)]
    grad_blocks = [pick(out_grad, other) for other in others]
    spots = jnp.concatenate([other * own_len + jnp.arange(own_len, dtype=i32) for other in others])
    spots = spots[:, None]
    length = pick(lengths, rank)[None]
    scalars = jnp.concatenate([length, pick(answer, rank), right_one])
    vectors = jnp.concatenate([b_out, ln1_gain, ln1_bias, b_down, ln2_gain, ln2_bias, b_out, b_out])
    vectors = vectors.astype(f32).reshape(8, model_dim)
    *blocks, spots, length, scalars, vectors, _ = lax.optimization_barrier(
        (*blocks, spots, length, scalars, vectors, sent_heads, *grad_blocks)
    )[: rows + 5]
    head_ids = jnp.arange(all_heads, dtype=i32)
    bias_rows = jnp.stack([block[own_len + 1, : 2 * head_width] for block in blocks])
    bias_rows = bias_rows.reshape(rows, 2, group_heads, HEAD_DIM).transpose(0, 2, 1, 3)
    bias_rows = bias_rows.reshape(all_heads, 2, HEAD_DIM)
    head_place = ((heads // group_heads) ^ rank) * group_heads + heads % group_heads
    head_bias = jnp.sum(
        jnp.where(
            (head_place[:, :, None] == head_ids)[:, :, :, None, None],
            bias_rows.astype(f32),
            0.0,
        ),
        2,
    )
    unit_at = unit_at.reshape(ranks, ff_width)
    near_at = jnp.stack([pick(unit_at, other) for other in others])
    bias_in = jnp.stack([block[own_len, :ff_width] for block in blocks]).astype(f32)
    unit_bias = near_at[:, :, None] == jnp.arange(slots, dtype=i32)
    unit_bias = jnp.sum(jnp.where(unit_bias, bias_in[:, :, None], 0.0), 1)

    saved_outs = [("v", (head_slots, full, HEAD_DIM), bf16)] * 3 + [
        ("v", (head_slots, full, full), bf16),
        ("v", (head_slots * HEAD_DIM, full), bf16),
    ]
    own_part, x_row, *own_saved = call(
        pin,
        functools.partial(attend_own_kernel, own_len),
        "attend_own",
        [("s", heads), ("s", length), ("h", spots), ("h", head_bias)]
        + [("h", block) for block in blocks]
        + [("v", own_heads)],
        [("v", (full, model_dim), f32), ("v", (full, model_dim), bf16)] + saved_outs,
    )
    far_units, own_part = lax.optimization_barrier((far_units, own_part))
    far_side = swap(far_units, "dp", 1)
    far_pair = swap(far_units, "mp", 1)
    across = after(across, far_units)
    other_sources = [across, swap(across, "mp", 1)]
    grad_blocks = [
        swap(after(block, across), "mp", o) if o else block for o, block in enumerate(grad_blocks)
    ]
    first_unit, first_inv, normed_low, *other_saved = call(
        pin,
        attend_kernel,
        "attend",
        [("s", heads), ("s", length), ("h", spots), ("h", head_bias), ("h", vectors)]
        + [("v", own_part), ("v", x_row)]
        + [("b", source) for source in other_sources],
        [
            ("v", (full, model_dim), f32),
            ("v", (full, 1), f32),
            ("v", (full, model_dim), bf16),
        ]
        + saved_outs,
        [((full, model_dim), f32)],
    )
    normed_low, far_side, far_pair, *grad_blocks = lax.optimization_barrier(
        (normed_low, far_side, far_pair, *grad_blocks)
    )
    far_units = [far_units, far_side, far_pair, swap(far_side, "mp", 1)]

    unit_side = (2, ranks // 2, slots, model_dim)
    hidden_dims = (ranks, full, slots)
    block_dims = (ranks, slots, model_dim)
    unit_far, unit_near, layer_out, row_loss, loss_small, grad_second, grad_upper, all_in = call(
        pin,
        feed_kernel,
        "feed",
        [("s", scalars), ("v", normed_low), ("v", first_unit), ("h", vectors), ("h", unit_bias)]
        + [("b", u) for u in (in_rows, near_units[0], down_rows, near_units[1])]
        + [("b", u) for u in far_units]
        + [("h", spots), ("h", w_span.T)]
        + [("b", block) for block in grad_blocks],
        [
            ("h", unit_side, bf16),
            ("v", unit_side, bf16),
            ("v", (full, model_dim), bf16),
            ("h", (1, 1), f32),
            ("h", (8, model_dim), f32),
            ("v", (full, model_dim), f32),
            ("v", hidden_dims, bf16),
            ("v", block_dims, bf16),
        ],
        [
            (block_dims, bf16),
            (hidden_dims, bf16),
            (hidden_dims, bf16),
            ((full, model_dim), f32),
            ((full, model_dim), f32),
            ((full, model_dim), f32),
            ((full, 4), f32),
        ],
    )
    unit_got = swap(unit_far, "mp", 1)
    first_small, grad_resid, grad_attended, slot_bias_grad = call(
        pin,
        feed_back_kernel,
        "feed_back",
        [("v", grad_upper), ("v", all_in), ("v", grad_second), ("v", first_unit)]
        + [("v", first_inv), ("h", vectors)],
        [
            ("h", (8, model_dim), f32),
            ("v", (full, model_dim), f32),
            ("v", (full, model_dim), bf16),
            ("h", (ranks, slots), f32),
        ],
        [((full, model_dim), f32)],
    )

    halves = (slots, model_dim // 2)
    down_send, in_send, down_keep, in_keep = call(
        pin,
        merge_kernel,
        "merge",
        [("s", right_one), ("v", unit_near), ("b", unit_got)],
        [
            ("h", (slots, model_dim), bf16),
            ("h", (2,) + halves, bf16),
            ("b", (slots, model_dim), bf16),
            ("b", (2,) + halves, bf16),
        ],
    )
    grad_attended = after(grad_attended, down_send, in_send)
    down_got = swap(down_send, "mp", 2)
    in_got = swap(in_send, "dp", 1)

    head_far, head_near, late, *own_rows = call(
        pin,
        functools.partial(attend_back_kernel, own_len),
        "attend_back",
        [("s", heads), ("v", grad_attended), ("v", grad_resid), ("v", x_row)]
        + [("v", a) for a in own_saved + [own_heads] + other_saved]
        + [("b", a) for a in other_sources]
        + [("v", layer_out)],
        [
            ("h", (head_slots * tall, model_dim), bf16),
            ("v", (2, half_slots, tall, model_dim), bf16),
            ("h", (8, model_dim), f32),
        ]
        + [("b", (2, own_len, model_dim), bf16)] * rows,
        [((full, model_dim), f32)],
    )

    head_far, down_got, in_got = lax.optimization_barrier((head_far, down_got, in_got))
    head_got = swap(head_far, "mp", 1)
    group = groups[0]
    parts = 1 << len(group)
    part = (slots // parts, model_dim // 2)
    down_send, down_keep, *in_parts = call(
        pin,
        second_merge_kernel,
        "second_merge",
        [("s", right_one), ("b", down_keep), ("b", down_got), ("b", in_keep), ("b", in_got)],
        [("h", halves, bf16), ("b", halves, bf16), ("b", (2,) + part, bf16)]
        + [("h", (2,) + part, bf16)] * (parts - 1),
    )
    down_got = swap(down_send, "dp", 1)
    in_gots = [swap(in_parts[j], "dp", partner(group, j)) for j in range(1, parts)]

    block_hit = (jnp.arange(ranks) ^ rank)[:, None] == jnp.arange(ranks)[None, :]
    place_ids = jnp.arange(pieces, dtype=i32) ^ (dp_index // 2)
    bits = len(masks_of("dp")) - 1
    place_ids = sum(
        (((place_ids >> b) & 1) << (bits - 1 - b) for b in range(bits)), jnp.zeros((pieces,), i32)
    )
    place_hit = place_ids[:, None] == jnp.arange(pieces)
    by_rank = slot_bias_grad.reshape(ranks, 1, 1, pieces, piece)
    by_rank = jnp.where(block_hit[:, :, None, None, None] & place_hit[:, :, None], by_rank, 0.0)
    by_rank = jnp.sum(by_rank, (0, 3)).reshape(-1)
    bias_count = -(-by_rank.shape[0] // model_dim)
    by_rank = jnp.pad(by_rank, (0, bias_count * model_dim - by_rank.shape[0]))
    device_hit = jnp.arange(model_dim) == dp_index * ranks + rank
    late_row = 9 + bias_count
    fill = -(-(late_row + 2) // 8) * 8 - late_row - 2
    small = jnp.concatenate(
        [
            first_small[:3],
            loss_small[:5],
            by_rank.reshape(-1, model_dim),
            jnp.where(device_hit, row_loss, 0.0),
            late[:2],
            jnp.zeros((fill, model_dim), f32),
        ],
        0,
    )
    high = lax.reduce_precision(small, 8, 7)
    low = lax.reduce_precision(small - high, 8, 7)
    small = high + low
    small_got = swap(jnp.concatenate([high, low], 0).astype(bf16), "mp", 1)

    head_got = after(head_got, in_parts[1], small_got)
    kept = half_slots * tall
    small_dims = small.shape
    head_send, keep, small = call(
        pin,
        first_hop_kernel,
        "first_hop",
        [("v", head_near), ("b", head_got), ("h", small), ("h", small_got)],
        [
            ("h", (kept + 2 * small_dims[0], model_dim), bf16),
            ("v", (kept, model_dim), bf16),
            ("v", small_dims, f32),
        ],
    )
    gots = [swap(head_send, "mp", 2)]
    head_hops = [masks_of("dp")[:1]] + groups

    def head_hop(group, keep, small, gots):
        parts = 1 << len(group)
        own = own_bits(group, dp_index)[None].astype(i32)
        *sends, keep, small = hop(pin, parts, own, keep, small, gots)
        gots = [swap(sends[j - 1], "dp", partner(group, j)) for j in range(1, parts)]
        return keep, small, gots

    def widen(keep, group):
        got = [swap(keep, "dp", partner(group, j)) for j in range(1, 1 << len(group))]
        return jnp.concatenate([keep] + got, 0)

    keep, small, gots = head_hop(head_hops[0], keep, small, gots)
    down_got, *in_gots = lax.optimization_barrier((down_got, *in_gots, keep))[:-1]
    *unit_parts, in_mine, in_send = call(
        pin,
        third_merge_kernel,
        "third_merge",
        [("b", down_keep), ("b", down_got), ("b", in_parts[0])] + [("b", got) for got in in_gots],
        [("h", part, bf16)] * parts + [("h", part, bf16)] * 2,
    )
    down_gots = [swap(unit_parts[j], "dp", partner(group, j)) for j in range(1, parts)]
    in_send, in_mine = (scatter_over(x, groups[1:]) for x in (in_send, in_mine))
    in_got = swap(in_send, "mp", 2)
    down_mine = scatter_over(scatter_sum(unit_parts[0], down_gots), groups[1:])
    unit_part = jnp.stack([scatter_sum(in_mine, [in_got]), down_mine])
    unit_grads = gather_over(unit_part, groups)
    own_rows = [after(block, keep) if o else block for o, block in enumerate(own_rows)]
    own_rows = [swap(block, "mp", o) if o else block for o, block in enumerate(own_rows)]
    keep, small, gots = head_hop(head_hops[1], keep, small, gots)
    unit_side = swap(unit_grads, "dp", 1)
    *gots, own_rows[0] = lax.optimization_barrier((*gots, *own_rows))[: len(gots) + 1]
    for group in head_hops[2:]:
        keep, small, gots = head_hop(group, keep, small, gots)
    keep, small = hop(pin, 1, jnp.zeros((1,), i32), keep, small, gots)
    for group in reversed(groups):
        keep = widen(keep, group)
    keep, unit_side = lax.optimization_barrier((keep, unit_side))
    mine = widen(keep, head_hops[0])
    unit_grads = join_sides(unit_grads, unit_side, right)
    w_in_grad = mxu(unit_grads[0], unit_pick, 0, 0)
    w_down_grad = mxu(unit_pick, unit_grads[1], 0, 0)
    own_rows = to_own(own_rows, rank)
    layer_out_own = own_rows[:, 0]
    tokens_grad = own_rows[:, 1].astype(f32)
    both = jnp.concatenate([mine, swap(mine, "mp", 1)], 0)

    head_piece = kept // n_dp
    row_ids = jnp.arange(2 * kept, dtype=i32)
    from_core, row_ids = row_ids // kept, row_ids % kept
    own_piece = own_bits([m for group in head_hops for m in group], dp_index)
    natural = ((row_ids // head_piece) ^ own_piece) * head_piece + row_ids % head_piece
    natural = natural + from_core * kept
    columns = jnp.arange(4 * head_width, dtype=i32)
    kind, rest = columns // head_width, columns % head_width
    column_slot = jnp.sum(
        jnp.where((rest // HEAD_DIM)[:, None] == jnp.arange(group_heads), my_slots, 0), 1
    )
    wanted = ((column_slot ^ core) % 2) * kept + (column_slot // 2) * tall
    wanted = wanted + kind * HEAD_DIM + rest % HEAD_DIM
    wanted = jnp.where(column_slot >= 0, wanted, -1)
    row_pick = (natural[:, None] == wanted[None, :]).astype(bf16)
    w_qkv_grad = mxu(both, row_pick[:, : 3 * head_width], 0, 0).reshape(model_dim, 3, head_width)
    w_out_grad = mxu(row_pick[:, 3 * head_width :], both, 0, 0)

    by_rank = small[8 : 8 + bias_count].reshape(-1)[: ranks * slots].reshape(ranks, slots)
    by_rank = pick(by_rank, rank).reshape(pieces, 1, piece)
    by_rank = jnp.sum(jnp.where(place_hit[:, :, None], by_rank, 0.0), 0).reshape(slots)
    b_in_grad = jnp.sum(jnp.where(unit_pick > 0, by_rank[:, None], 0.0), 0)
    losses = small[8 + bias_count, : n_dp * ranks].reshape(n_dp, ranks)
    losses = lax.dynamic_index_in_dim(losses, dp_index, 0, keepdims=False)
    late = small[late_row : late_row + 2].reshape(2, ranks, head_width)
    b_qv_grad = lax.dynamic_index_in_dim(late, rank, 1, keepdims=False)
    return (
        layer_out_own,
        losses,
        tokens_grad,
        w_qkv_grad,
        b_qv_grad,
        w_out_grad,
        small[2],
        small[0],
        small[1],
        w_in_grad,
        b_in_grad,
        w_down_grad,
        small[5],
        small[3],
        small[4],
        small[6:8].T,
    )


def shards(*args):
    head_order, neuron_order, w_qkv, w_in = args[3], args[4], args[5], args[11]
    ranks = lax.axis_size("mp")
    pair_heads = 2 * w_qkv.shape[2] // HEAD_DIM
    ff_width = w_in.shape[1]
    (fits,) = call(
        False,
        functools.partial(fits_kernel, UNIT_SLOTS, HEAD_SLOTS, ff_width, pair_heads, ranks),
        "fits",
        [("s", head_order), ("h", neuron_order[:LIVE_FF][None])],
        [("s", (1,), i32)],
    )
    return lax.cond(
        fits[0] == 1,
        functools.partial(program, UNIT_SLOTS, HEAD_SLOTS, True),
        functools.partial(program, ff_width, pair_heads, False),
        *args,
    )


def solution(mesh):
    return jax.shard_map(
        shards,
        mesh=mesh,
        in_specs=(
            P("dp", "mp", None),
            P("dp"),
            P("dp", None),
            P(),
            P(),
            P(None, None, "mp"),
            P(None, "mp"),
            P("mp", None),
            P(),
            P(),
            P(),
            P(None, "mp"),
            P("mp"),
            P("mp", None),
            P(),
            P(),
            P(),
            P(),
            P("dp", "mp", None),
        ),
        out_specs=(
            P("dp", "mp", None),
            P("dp"),
            P("dp", "mp", None),
            P(None, None, "mp"),
            P(None, "mp"),
            P("mp", None),
            P(),
            P(),
            P(),
            P(None, "mp"),
            P("mp"),
            P("mp", None),
            P(),
            P(),
            P(),
            P(),
        ),
        check_vma=False,
    )
```

```python
import functools
import math

import jax
import jax.numpy as jnp
from jax import lax
from jax.experimental import pallas as pl
from jax.experimental.pallas import tpu as pltpu
from jax.sharding import PartitionSpec as P

HEAD_DIM = 64
LIVE_HEADS = 6
LIVE_FF = 1536
UNIT_SLOTS = 448
HEAD_SLOTS = 4
EXTRA = 16
MASKED = -1000000000.0
VMEM_MOST = 60 * 2**20
VMEM_SPARE = 8 * 2**20

f32 = jnp.float32
bf16 = jnp.bfloat16
i32 = jnp.int32
epsilon = 1e-12


def swap(x, axis, mask):
    return lax.ppermute(x, axis, [(i, i ^ mask) for i in range(lax.axis_size(axis))])


def masks_of(axis):
    return [1 << b for b in range((lax.axis_size(axis) - 1).bit_length())]


def bit_of(index, mask):
    return (index // mask) % 2


def pick(stacked, index):
    return lax.dynamic_index_in_dim(stacked, index, 0, keepdims=False)


def after(value, *others):
    return lax.optimization_barrier((value,) + others)[0]


def to_own(got, rank):
    for mask in masks_of("mp"):
        moved = bit_of(rank, mask) == 1
        got = [jnp.where(moved, got[r ^ mask], got[r]) for r in range(len(got))]
    return jnp.stack(got, 0)


def z_groups():
    masks = masks_of("dp")[1:]
    return [masks[i : i + 2] for i in range(0, len(masks), 2)]


def partner(group, j):
    return sum(m for i, m in enumerate(group) if (j >> (len(group) - 1 - i)) & 1)


def own_bits(group, dp_index):
    place = 0
    for mask in group:
        place = place * 2 + bit_of(dp_index, mask)
    return place


def join_sides(mine, other, right):
    return jnp.concatenate([jnp.where(right, other, mine), jnp.where(right, mine, other)], -1)


def gather_over(x, groups):
    for group in reversed(groups):
        got = [swap(x, "dp", partner(group, j)) for j in range(1, 1 << len(group))]
        x = jnp.concatenate([x] + got, -2)
    return x


def scatter_sum(x, got):
    x = x.astype(f32)
    for term in got:
        x = x + term.astype(f32)
    return x.astype(bf16)


def scatter_over(x, groups):
    for group in groups:
        n = 1 << len(group)
        rows = x.shape[-2] // n
        parts = [x[..., j * rows : (j + 1) * rows, :] for j in range(n)]
        x = scatter_sum(parts[0], [swap(parts[j], "dp", partner(group, j)) for j in range(1, n)])
    return x


class Incoming:
    def __init__(self, source, held, sem, late):
        self.copy, self.held, self.waiting = pltpu.make_async_copy(source, held, sem), held, True
        self.shape, self.started = held.shape, False
        if not late:
            self.start()

    def start(self):
        if not self.started:
            self.started = True
            self.copy.start()

    def ready(self):
        if self.waiting:
            self.start()
            self.copy.wait()
            self.waiting = False
        return self.held

    def __getitem__(self, index):
        return self.ready()[index]

    @property
    def at(self):
        return self.ready().at


class Outgoing:
    def __init__(self, held, target, sem):
        self.held, self.target, self.sem, self.sent = held, target, sem, False
        self.shape, self.at = held.shape, held.at

    def __getitem__(self, index):
        return self.held[index]

    def __setitem__(self, index, value):
        self.held[index] = value

    def send(self, *index):
        self.sent = True
        if index:
            pltpu.make_async_copy(self.held.at[index], self.target.at[index], self.sem).start()
        else:
            pltpu.make_async_copy(self.held, self.target, self.sem).start()

    def wait(self):
        if not self.sent:
            self.send()
        pltpu.make_async_copy(self.held, self.target, self.sem).wait()


def start(*refs):
    for ref in refs:
        if isinstance(ref, Incoming):
            ref.start()


def ready(*refs):
    for ref in refs:
        if isinstance(ref, Incoming):
            ref.ready()


def send(*refs):
    for ref in refs:
        if isinstance(ref, Outgoing):
            ref.send()


def held(item):
    dims, size = item.shape, jnp.dtype(item.dtype).itemsize
    if len(dims) < 2:
        return 4096
    tall = 32 // size
    return -(-dims[-1] // 128) * 128 * (-(-dims[-2] // tall) * tall) * size * math.prod(dims[:-2])


def shape(dims, kind):
    return jax.ShapeDtypeStruct(dims, kind)


PLACES = {"v": pltpu.VMEM, "b": pltpu.HBM, "l": pltpu.HBM, "r": pltpu.HBM}


def call(pin, kernel, name, ins, outs, scratch=(), sems=0, flops=1e6, moved=5e6):
    in_kinds = [k if k != "v" or pin else "h" for k, _ in ins]
    out_kinds = [k if k != "v" or pin else "h" for k, _, _ in outs]
    args = [
        pltpu.with_memory_space_constraint(a, PLACES[k]) if k in PLACES else a
        for k, (_, a) in zip(in_kinds, ins)
    ]
    out_shape = [
        PLACES[k](d, t) if k in PLACES else shape(d, t) for k, (_, d, t) in zip(out_kinds, outs)
    ]
    buffers = [shape(a.shape, a.dtype) for k, a in zip(in_kinds, args) if k in "hbl"]
    buffers += [shape(d, t) for k, (_, d, t) in zip(out_kinds, outs) if k in "hb"]
    scratch = [shape(d, t) for d, t in scratch]
    count, outs_count = len(in_kinds), len(out_kinds)

    def whole(*refs):
        given, results, refs = refs[:count], refs[count : count + outs_count], refs[count + outs_count :]
        bufs, refs = iter(refs[: len(buffers)]), refs[len(buffers) :]
        in_sem, out_sem = refs[:2]
        given = [
            Incoming(ref, next(bufs), in_sem.at[i], k == "l") if k in "hbl" else ref
            for i, (k, ref) in enumerate(zip(in_kinds, given))
        ]
        results = [
            Outgoing(next(bufs), ref, out_sem.at[i]) if k in "hb" else ref
            for i, (k, ref) in enumerate(zip(out_kinds, results))
        ]
        kernel(*given, *results, *refs[2:])
        ready(*given)
        for ref in results:
            if isinstance(ref, Outgoing):
                ref.wait()

    spaces = {"s": pltpu.SMEM, "v": pltpu.VMEM, "h": pl.ANY, "b": pltpu.HBM, "l": pltpu.HBM, "r": pltpu.HBM}
    limit = sum(held(b) for b in buffers + scratch) + VMEM_SPARE
    return pl.pallas_call(
        whole,
        name=name,
        out_shape=out_shape,
        in_specs=[pl.BlockSpec(memory_space=spaces[k]) for k in in_kinds],
        out_specs=[pl.BlockSpec(memory_space=spaces[k]) for k in out_kinds],
        scratch_shapes=[pltpu.VMEM(b.shape, b.dtype) for b in buffers]
        + [pltpu.SemaphoreType.DMA((count,)), pltpu.SemaphoreType.DMA((outs_count,))]
        + [pltpu.SMEM(s.shape, s.dtype) if s.dtype == i32 else pltpu.VMEM(s.shape, s.dtype) for s in scratch]
        + ([pltpu.SemaphoreType.DMA((sems,))] if sems else []),
        compiler_params=pltpu.CompilerParams(vmem_limit_bytes=min(VMEM_MOST, int(limit))),
        cost_estimate=pl.CostEstimate(flops=int(flops), bytes_accessed=int(moved), transcendentals=0),
    )(*args)


def row_sum(v):
    return jnp.sum(v, 0, keepdims=True)


def lane_mean(v):
    return jnp.mean(v, -1, keepdims=True)


def mxu(a, b, a_dim, b_dim):
    return lax.dot_general(a, b, (((a_dim,), (b_dim,)), ((), ())), preferred_element_type=f32)


def loop(count, body):
    def step(i, carry):
        body(i)
        return carry

    lax.fori_loop(0, count, step, 0)


def span_of(i, size):
    return pl.ds(i * size if isinstance(i, int) else pl.multiple_of(i * size, size), size)


def by_rows(full, size, body):
    loop(full // size, lambda i: body(span_of(i, size)))


def fits_kernel(unit_slots, head_slots, ff_width, pair_heads, ranks, heads_ref, order_ref, fits_ref):
    order = order_ref[...]
    most = jnp.zeros((1, 1), f32)
    for r in range(ranks):
        mine = (order >= r * ff_width) & (order < (r + 1) * ff_width)
        most = jnp.maximum(most, jnp.sum(jnp.where(mine, 1.0, 0.0), keepdims=True))
    fine = jnp.where(most[0, 0] <= unit_slots, 1, 0)
    for pair in range(ranks // 2):
        count = 0
        for k in range(LIVE_HEADS):
            count += jnp.where(heads_ref[k] // pair_heads == pair, 1, 0)
        fine *= jnp.where(count <= head_slots, 1, 0)
    fits_ref[0] = fine


def rows_kernel(qkv_ref, out_ref, rows_ref):
    square = (HEAD_DIM, HEAD_DIM)
    diagonal = lax.broadcasted_iota(i32, square, 0) == lax.broadcasted_iota(i32, square, 1)
    diagonal = jnp.where(diagonal, 1.0, 0.0).astype(bf16)
    for g in range(out_ref.shape[0] // HEAD_DIM):
        at = slice(g * HEAD_DIM, (g + 1) * HEAD_DIM)
        parts = [mxu(diagonal, qkv_ref[c, :, at], 1, 1).astype(bf16) for c in range(3)]
        rows_ref[g * 4 * HEAD_DIM : (g + 1) * 4 * HEAD_DIM] = jnp.concatenate(parts + [out_ref[at]], 0)


def choose_kernel(group, place_ref, order_ref, rows_ref, far_ref, send_ref, heads_ref, slots_ref, table_ref):
    tall = 4 * HEAD_DIM
    rank = place_ref[0]
    core, pair = rank % 2, rank // 2
    counts = {}
    for head in range(order_ref.shape[0]):
        count = counts.get(head // (2 * group), 0)
        live = 0
        for k in range(LIVE_HEADS):
            live += jnp.where(order_ref[k] == head, 1, 0)
        table_ref[head] = jnp.where(live > 0, count, -1)
        counts[head // (2 * group)] = count + live
    half = heads_ref.shape[1] // 2
    for side in range(2):
        for e in range(2 * half):
            heads_ref[side, e] = -1
    for k in range(LIVE_HEADS):
        head = order_ref[k]
        side = jnp.where(head // (2 * group) != pair, 1, 0)
        heads_ref[side, table_ref[head] ^ core] = head
    for g in range(group):
        slots_ref[g] = table_ref[rank * group + g]
    ready(rows_ref, far_ref)
    for j in range(half):
        head = jnp.maximum(heads_ref[0, 2 * j], 0)
        at = pl.ds(pl.multiple_of((head % group) * tall, tall), tall)
        mine = (head // group == rank) | (heads_ref[0, 2 * j] < 0)
        target = slice(j * tall, (j + 1) * tall)

        @pl.when(mine)
        def own():
            send_ref[target] = rows_ref[at]

        @pl.when(jnp.logical_not(mine))
        def far():
            send_ref[target] = far_ref[at]


def units_kernel(zbits, place_ref, order_ref, in_ref, down_ref, *refs):
    sides_ref, pick_ref, rows_ref, at_ref = refs
    slots, width = pick_ref.shape
    side = sides_ref.shape[2]
    piece = slots >> zbits
    rank, dp_index = place_ref[0], place_ref[1]
    lanes = at_ref.shape[1]
    per = width // lanes
    order = order_ref[...]

    def hot(dims, index):
        return jnp.where(lax.broadcasted_iota(i32, dims, 0) == index, 1.0, 0.0).astype(bf16)

    count = order.shape[1]
    row_hot = hot((at_ref.shape[0], count), order // lanes)
    lane_hot = hot((lanes, count), order % lanes)
    live = mxu(row_hot, lane_hot, 1, 1)
    square = (lanes, lanes)
    first, second = (lax.broadcasted_iota(i32, square, d) for d in range(2))
    upto = jnp.where(first <= second, 1.0, 0.0).astype(bf16)
    within = mxu(live.astype(bf16), upto, 1, 0)
    totals = mxu(live.astype(bf16), jnp.ones(square, bf16), 1, 0)
    square = (at_ref.shape[0], at_ref.shape[0])
    first, second = (lax.broadcasted_iota(i32, square, d) for d in range(2))
    earlier = (second < first) & (second // per == first // per)
    offsets = mxu(jnp.where(earlier, 1.0, 0.0).astype(bf16), totals.astype(bf16), 1, 0)
    slot = (offsets + within).astype(i32) - 1
    index = jnp.zeros(slot.shape, i32)
    for p in range(1, slots // piece):
        index += jnp.where(slot >= p * piece, 1, 0)
    inside = slot - index * piece
    index = index ^ (dp_index // 2)
    place = jnp.zeros(slot.shape, i32)
    for b in range(zbits):
        place = place * 2 + ((index >> b) & 1)
    at_ref[...] = jnp.where(live > 0.5, place * piece + inside, -1)
    ids = lax.broadcasted_iota(i32, (slots, lanes), 0)
    for c in range(per):
        row = at_ref[pl.ds(rank * per + c, 1)]
        pick_ref[:, c * lanes : (c + 1) * lanes] = jnp.where(ids == row, 1.0, 0.0).astype(bf16)
    right = dp_index % 2 == 1
    rows_in = mxu(pick_ref[...], in_ref[...], 1, 1).astype(bf16)
    part = sides_ref.shape[1]
    sides_ref[0] = jnp.where(right, rows_in[:part, side:], rows_in[:part, :side])
    rows_ref[0] = rows_in
    rows_down = mxu(pick_ref[...], down_ref[...], 1, 0).astype(bf16)
    sides_ref[1] = jnp.where(right, rows_down[:part, side:], rows_down[:part, :side])
    send(sides_ref)
    rows_ref[1] = rows_down


def source_of(sources, j, i):
    if len(sources) == 1:
        return sources[0].at[2 * j + i]
    return sources[i].at[span_of(j, 4 * HEAD_DIM)]


def each_head(heads_ref, side, body):
    def two(j):
        for i in range(2):
            pl.when(heads_ref[side, 2 * j + i] >= 0)(functools.partial(body, j, i))

    loop(heads_ref.shape[1] // 2, two)


def out_rows(sources, slots):
    parts = [source_of(sources, e // 2, e % 2)[3 * HEAD_DIM :] for e in range(slots)]
    return jnp.concatenate(parts, 0)


def attend_heads(side, x_ref, heads_ref, valid, bias_ref, sources, outs):
    q_ref, k_ref, v_ref, probs_ref, ctx_ref = outs
    wide = 3 * HEAD_DIM
    half = x_ref.shape[0] // 2
    ctx_ref[...] = jnp.zeros(ctx_ref.shape, bf16)

    def attend_head(j, i):
        e = 2 * j + i
        bias = bias_ref[side, e]
        both = mxu(x_ref[...], source_of(sources, j, i)[:wide], 1, 1)
        query = (both[:, :HEAD_DIM] + bias[0:1]).astype(bf16)
        key = both[:, HEAD_DIM : 2 * HEAD_DIM].astype(bf16)
        value = (both[:, 2 * HEAD_DIM :] + bias[1:2]).astype(bf16)
        q_ref[e], k_ref[e], v_ref[e] = query, key, value
        for c in range(2):
            part = slice(c * half, (c + 1) * half)
            scores = mxu(key, query[part], 1, 1) * HEAD_DIM ** (-0.5)
            scores = jnp.where(valid, scores, MASKED)
            exp_scores = jnp.exp(scores - jnp.max(scores, 0, keepdims=True))
            probs = (exp_scores * (1.0 / row_sum(exp_scores))).astype(bf16)
            probs_ref[e, :, part] = probs
            ctx_ref[span_of(e, HEAD_DIM), part] = mxu(value, probs, 0, 0).astype(bf16)

    each_head(heads_ref, side, attend_head)
    send(*outs)
    return mxu(ctx_ref[...], out_rows(sources, heads_ref.shape[1]), 0, 0)


def attend_own_kernel(own, group, place_ref, lengths_ref, heads_ref, rows_ref, far_ref, *refs):
    blocks, refs = refs[:-14], refs[-14:]
    part_ref, x_ref, spots_ref, bias_ref, unit_bias_ref, heads_out_ref = refs[:6]
    outs, (held_ref, table_ref, sem) = refs[6:11], refs[11:]
    rank = place_ref[0]
    tall = 4 * HEAD_DIM
    count = group * tall
    copies = [
        pltpu.make_async_copy(ref, held_ref.at[pl.ds(n * count, count)], sem.at[n])
        for n, ref in enumerate((rows_ref, far_ref))
    ]
    for copy in copies:
        copy.start()
    for o, block in enumerate(blocks):
        x_ref[o * own : (o + 1) * own] = block[:own]
        ids = lax.broadcasted_iota(i32, (own, 1), 0)
        spots_ref[o * own : (o + 1) * own] = ids + (rank ^ o) * own
        extra = block[own : own + EXTRA].astype(f32)
        unit_bias_ref[o : o + 1] = extra[0:1]
        for g in range(group):
            for n in range(2):
                at = (n * group + g) * HEAD_DIM
                table_ref[o * group + g, n : n + 1] = extra[1:2, at : at + HEAD_DIM]
    for side in range(2):
        for e in range(heads_ref.shape[1]):
            head = jnp.maximum(heads_ref[side, e], 0)
            bias_ref[side, e] = table_ref[((head // group) ^ rank) * group + head % group][:2]
    for copy in copies:
        copy.wait()
    for e in range(heads_ref.shape[1]):
        head = jnp.maximum(heads_ref[0, e], 0)
        at = jnp.where(head // group == rank, 0, count) + (head % group) * tall
        heads_out_ref[e] = held_ref[pl.ds(pl.multiple_of(at, tall), tall)]
    valid = spots_ref[...] < lengths_ref[rank]
    part_ref[...] = attend_heads(0, x_ref, heads_ref, valid, bias_ref, [heads_out_ref], outs)


def attend_kernel(place_ref, lengths_ref, heads_ref, spots_ref, bias_ref, vec_ref, part_ref, x_ref, *refs):
    sources, refs = refs[:2], refs[2:]
    unit_ref, inv_ref, low_ref, sum_ref = refs[:3] + refs[-1:]
    valid = spots_ref[...] < lengths_ref[place_ref[0]]
    ready(bias_ref, vec_ref, part_ref, x_ref, *sources)
    sum_ref[...] = attend_heads(1, x_ref, heads_ref, valid, bias_ref, sources, refs[3:-1])

    def norm(rows):
        first_sum = x_ref[rows].astype(f32) + (part_ref[rows] + sum_ref[rows]) + vec_ref[0:1]
        centered = first_sum - lane_mean(first_sum)
        inv = lax.rsqrt(lane_mean(centered * centered) + epsilon)
        unit = centered * inv
        unit_ref[rows] = unit
        inv_ref[rows] = inv
        low_ref[rows] = (unit * vec_ref[1:2] + vec_ref[2:3]).astype(bf16)

    by_rows(sum_ref.shape[0], 128, norm)


def join_block(target, mine, other, kind, right):
    half = mine.shape[-1]
    one, two = mine[kind], other[kind]
    target[:, :half] = jnp.where(right, two, one)
    target[:, half:] = jnp.where(right, one, two)


def feed_kernel(scalar_ref, low_ref, unit_ref, vec_ref, bias_ref, *refs):
    near_units, sides, refs = refs[:2], refs[2:6], refs[6:]
    spots_ref, span_ref, refs = refs[0], refs[1], refs[2:]
    grads, refs = refs[:-14], refs[-14:]
    far_ref, out_ref, loss_ref, small_ref, second_ref, upper_ref, ins_ref = refs[:7]
    downs_ref, hidden_ref, slope_ref, total_ref, layer_ref, two_ref, logit_ref = refs[7:]
    full = low_ref.shape[0]
    half = full // 2
    right = scalar_ref[3] == 1
    ready(low_ref, unit_ref, vec_ref, bias_ref, *near_units)

    def first(rows):
        total_ref[rows] = unit_ref[rows] * vec_ref[1:2] + vec_ref[2:3] + vec_ref[3:4]

    by_rows(full, 128, first)
    for o in range(2):
        ins_ref[o] = near_units[o][0]
        downs_ref[o] = near_units[o][1]

    def forward(o):
        for r in range(2):
            rows = slice(r * half, (r + 1) * half)
            upper = mxu(low_ref[rows], ins_ref[o], 1, 1) + bias_ref[pl.ds(o, 1)]
            cumulative = 0.5 * (1.0 + lax.erf(upper * 0.7071067811865476))
            density = jnp.exp(-0.5 * upper * upper) * 0.3989422804014327
            hidden = (upper * cumulative).astype(bf16)
            hidden_ref[o, rows] = hidden
            slope_ref[o, rows] = (cumulative + upper * density).astype(bf16)
            total_ref[rows] += mxu(hidden, downs_ref[o], 1, 0)

    loop(2, forward)
    ready(*sides)
    for o in range(2):
        join_block(ins_ref.at[2 + o], sides[2 * o], sides[2 * o + 1], 0, right)
        join_block(downs_ref.at[2 + o], sides[2 * o], sides[2 * o + 1], 1, right)
    loop(2, lambda o: forward(o + 2))
    ready(spots_ref, span_ref, *grads)

    def norm(rows):
        second_sum = total_ref[rows]
        centered = second_sum - lane_mean(second_sum)
        inv = lax.rsqrt(lane_mean(centered * centered) + epsilon)
        unit = centered * inv
        layer_out = unit * vec_ref[4:5] + vec_ref[5:6]
        two_ref[rows] = unit
        layer_ref[rows] = layer_out
        out_ref[rows] = layer_out.astype(bf16)
        logit_ref[rows, 2:3] = inv
        for c in range(2):
            logit_ref[rows, c : c + 1] = jnp.sum(layer_out * span_ref[c : c + 1], -1, keepdims=True)

    by_rows(full, 128, norm)
    small_ref[...] = jnp.zeros(small_ref.shape, f32)
    spots = spots_ref[...]
    valid = spots < scalar_ref[0]
    loss = jnp.zeros((1, 1), f32)
    for c in range(2):
        logits = logit_ref[:, c : c + 1]
        masked = jnp.where(valid, logits, MASKED)
        top = jnp.max(masked, 0, keepdims=True)
        exp_logits = jnp.exp(masked - top)
        total = row_sum(exp_logits)
        chosen = spots == scalar_ref[1 + c]
        loss += top + jnp.log(total) - row_sum(jnp.where(chosen, logits, 0.0))
        logit_ref[:, c : c + 1] = exp_logits / total - jnp.where(chosen, 1.0, 0.0)
    loss_ref[...] = loss
    own = full // len(grads)
    for o, grad in enumerate(grads):
        rows = slice(o * own, (o + 1) * own)
        unit, layer_out, inv = two_ref[rows], layer_ref[rows], logit_ref[rows, 2:3]
        grad_out = grad[...].astype(f32)
        for c in range(2):
            grad_logits = logit_ref[rows, c : c + 1]
            grad_out += grad_logits * span_ref[c : c + 1]
            small_ref[3 + c : 4 + c] += row_sum(layer_out * grad_logits)
        small_ref[0:1] += row_sum(grad_out * unit)
        small_ref[1:2] += row_sum(grad_out)
        grad_normed = grad_out * vec_ref[4:5]
        second = inv * (
            grad_normed - lane_mean(grad_normed) - unit * lane_mean(grad_normed * unit)
        )
        second_ref[rows] = second
        small_ref[2:3] += row_sum(second)

    branch_grad = second_ref[...].astype(bf16)
    args = (branch_grad, low_ref, downs_ref, hidden_ref, slope_ref, upper_ref)
    loop(2, lambda j: back_block(2 * j + 1, *args, far_ref.at[:, j]))


def back_block(o, branch_grad, low_ref, downs_ref, hidden_ref, slope_ref, upper_ref, target):
    hidden_grad = mxu(branch_grad, downs_ref[o], 1, 1)
    upper = (hidden_grad * slope_ref[o].astype(f32)).astype(bf16)
    upper_ref[o] = upper
    target[1] = mxu(hidden_ref[o], branch_grad, 0, 0).astype(bf16)
    target[0] = mxu(upper, low_ref[...], 0, 0).astype(bf16)


def feed_back_kernel(upper_ref, ins_ref, second_ref, unit_ref, inv_ref, vec_ref, *refs):
    low_ref, downs_ref, hidden_ref, slope_ref = refs[:4]
    near_ref, small_ref, resid_ref, att_ref, bias_ref, first_ref, near_upper_ref = refs[4:]
    ready(upper_ref, ins_ref, second_ref, low_ref, downs_ref, hidden_ref, slope_ref)
    first_ref[...] = second_ref[...]

    def back(j):
        branch_grad = second_ref[...].astype(bf16)
        args = (branch_grad, low_ref, downs_ref, hidden_ref, slope_ref, near_upper_ref)
        back_block(2 * j, *args, near_ref.at[:, j])
        for upper, o in ((near_upper_ref[2 * j], 2 * j), (upper_ref[2 * j + 1], 2 * j + 1)):
            first_ref[...] += mxu(upper, ins_ref[o], 1, 0)
            bias_ref[pl.ds(o, 1)] = row_sum(upper.astype(f32))

    loop(upper_ref.shape[0] // 2, back)
    ready(unit_ref, inv_ref, vec_ref)
    small_ref[...] = jnp.zeros(small_ref.shape, f32)

    def norm(rows):
        first, unit = first_ref[rows], unit_ref[rows]
        grad_normed = first * vec_ref[1:2]
        resid = inv_ref[rows] * (
            grad_normed - lane_mean(grad_normed) - unit * lane_mean(grad_normed * unit)
        )
        resid_ref[rows] = resid
        att_ref[rows] = resid.astype(bf16)
        small_ref[0:1] += row_sum(first * unit)
        small_ref[1:2] += row_sum(first)
        small_ref[2:3] += row_sum(resid)

    by_rows(first_ref.shape[0], 128, norm)


def merge_kernel(right_ref, near_ref, got_ref, *refs):
    down_send_ref, in_send_ref, down_keep_ref, in_keep_ref = refs
    right = right_ref[0] == 1
    half = in_send_ref.shape[-1]
    ready(near_ref, got_ref)

    def total(kind, o, rows):
        return (near_ref[kind, o, rows].astype(f32) + got_ref[kind, o, rows].astype(f32)).astype(bf16)

    def merge(rows):
        down_send_ref[rows] = total(1, 1, rows)
        down_keep_ref[rows] = total(1, 0, rows)
        for o in range(2):
            block = total(0, o, rows)
            in_send_ref[o, rows] = jnp.where(right, block[:, :half], block[:, half:])
            in_keep_ref[o, rows] = jnp.where(right, block[:, half:], block[:, :half])

    by_rows(down_send_ref.shape[0], down_send_ref.shape[0] // 4, merge)


def second_merge_kernel(right_ref, down_ref, down_got_ref, in_ref, in_got_ref, *refs):
    down_send_ref, down_keep_ref, parts = refs[0], refs[1], refs[2:]
    right = right_ref[0] == 1
    half = down_send_ref.shape[-1]
    each = parts[0].shape[1]
    for j in range(1, len(parts) + 1):
        j %= len(parts)
        rows = slice(j * each, (j + 1) * each)
        for o in range(2):
            parts[j][o] = (in_ref[o, rows].astype(f32) + in_got_ref[o, rows].astype(f32)).astype(bf16)
        send(parts[j])
        block = (down_ref[rows].astype(f32) + down_got_ref[rows].astype(f32)).astype(bf16)
        down_send_ref[rows] = jnp.where(right, block[:, :half], block[:, half:])
        down_keep_ref[rows] = jnp.where(right, block[:, half:], block[:, :half])


def down_parts_kernel(down_ref, got_ref, *parts):
    each = parts[0].shape[0]
    ready(down_ref, got_ref)
    for j in range(1, len(parts) + 1):
        j %= len(parts)
        rows = slice(j * each, (j + 1) * each)
        parts[j][...] = (down_ref[rows].astype(f32) + got_ref[rows].astype(f32)).astype(bf16)
        send(parts[j])


def in_sum_kernel(in_ref, *refs):
    gots, outs = refs[:-2], refs[-2:]
    for o in (1, 0):
        total = in_ref[o].astype(f32)
        for got in gots:
            total += got[o].astype(f32)
        outs[1 - o][...] = total.astype(bf16)
        send(outs[1 - o])


def attend_back_kernel(own, heads_ref, att_ref, resid_ref, x_ref, *refs):
    sides = ((refs[:5], refs[5:6]), (refs[6:11], refs[11:13]))
    layer_ref, far_ref, near_ref, late_ref = refs[13:17]
    moved, total_ref = refs[17:-1], refs[-1]
    wide = 3 * HEAD_DIM
    scale = HEAD_DIM ** (-0.5)
    _, half_slots, tall, width = near_ref.shape
    lane_head = lax.broadcasted_iota(i32, (1, width), 1) // HEAD_DIM
    slots = heads_ref.shape[1]
    late_ref[...] = jnp.zeros(late_ref.shape, f32)
    far_ref[...] = jnp.zeros(far_ref.shape, bf16)
    near_ref[...] = jnp.zeros(near_ref.shape, bf16)
    full = x_ref.shape[0]
    half = full // 2
    ready(att_ref, resid_ref, x_ref)
    total_ref[...] = resid_ref[...]
    for side, (saved, sources) in enumerate(sides):
        q_ref, k_ref, v_ref, probs_ref, ctx_ref = saved
        ready(*saved, *sources)
        if side == 0:
            start(*sides[1][0], *sides[1][1], layer_ref)
        out_grads = mxu(ctx_ref[...], att_ref[...], 1, 0).astype(bf16)
        for e in range(slots):
            part = out_grads[e * HEAD_DIM : (e + 1) * HEAD_DIM]
            at = (side * half_slots + e // 2) * tall + wide
            if e % 2:
                far_ref[at : at + HEAD_DIM] = part
            else:
                near_ref[side, e // 2, wide:] = part

        def back_head(j, i):
            e = 2 * j + i
            source = source_of(sources, j, i)
            ctx_grad = mxu(att_ref[...], source[wide:], 1, 1).astype(bf16)
            query, key, value = q_ref[e], k_ref[e], v_ref[e]
            grad_key = grad_value = None
            grad_query = []
            for c in range(2):
                part = slice(c * half, (c + 1) * half)
                probs_low = probs_ref[e, :, part]
                probs = probs_low.astype(f32)
                grad_probs = mxu(value, ctx_grad[part], 1, 1)
                grad_scores = probs * (grad_probs - row_sum(grad_probs * probs))
                grad_scores = grad_scores.astype(bf16)
                value_term = mxu(probs_low, ctx_grad[part], 1, 0)
                key_term = mxu(grad_scores, query[part], 1, 0)
                grad_value = value_term if grad_value is None else grad_value + value_term
                grad_key = key_term if grad_key is None else grad_key + key_term
                grad_query.append(mxu(grad_scores, key, 0, 0))
            grad_query = jnp.concatenate(grad_query, 0)
            grads = jnp.concatenate([grad_query * scale, grad_key * scale, grad_value], 1)
            grads = grads.astype(bf16)
            sums = row_sum(grads.astype(f32))
            for n in range(2):
                part = sums[:, 2 * n * HEAD_DIM : (2 * n + 1) * HEAD_DIM]
                spread = jnp.concatenate([part] * (width // HEAD_DIM), 1)
                late_ref[n : n + 1] += jnp.where(lane_head == heads_ref[side, e], spread, 0.0)
            total_ref[...] += mxu(grads, source[:wide], 1, 0)
            rows = mxu(grads, x_ref[...], 0, 0).astype(bf16)
            if i:
                at = pl.multiple_of((side * half_slots + j) * tall, tall)
                far_ref[pl.ds(at, wide)] = rows
            else:
                near_ref[side, j, :wide] = rows

        each_head(heads_ref, side, back_head)
    send(far_ref)
    ready(layer_ref)
    for o in range(full // own):
        at = slice(o * own, (o + 1) * own)
        ref = moved[0] if o % 2 else moved[1]
        ref[o // 2, 0] = layer_ref[at]
        ref[o // 2, 1] = total_ref[at].astype(bf16)


def first_hop_kernel(near_ref, got_ref, small_ref, small_got_ref, send_ref, keep_ref, sum_ref):
    _, half_slots, tall, _ = near_ref.shape
    rows = keep_ref.shape[0]
    ready(near_ref, got_ref)

    def add(side, j, target):
        at = pl.multiple_of(j * tall, tall)
        got = got_ref[pl.ds(side * rows + at, tall)]
        target[pl.ds(at, tall)] = (near_ref[side, j].astype(f32) + got.astype(f32)).astype(bf16)

    loop(half_slots, lambda j: add(1, j, send_ref))
    total = (small_ref[...].astype(f32) + small_got_ref[...].astype(f32)).astype(bf16)
    send_ref[rows:] = total
    sum_ref[...] = total
    send(send_ref)
    loop(half_slots, lambda j: add(0, j, keep_ref))


def hop_kernel(parts, own_ref, keep_ref, small_ref, *refs):
    gots, refs = refs[: -parts - 1], refs[-parts - 1 :]
    sends, mine_ref, sum_ref = refs[: parts - 1], refs[-2], refs[-1]
    rows = keep_ref.shape[0]
    ready(keep_ref, *gots)
    small = [part.astype(f32) for part in [small_ref[...]] + [got[rows:] for got in gots]]
    while len(small) > 1:
        small = [small[i] + small[i + 1] for i in range(0, len(small), 2)]
    low = small[0].astype(bf16)
    sum_ref[...] = low if parts > 1 else small[0]
    own = own_ref[0]
    each = rows // parts
    for j in range(1, parts + 1):
        j %= parts
        at = span_of(own ^ j, each)
        total = keep_ref[at].astype(f32)
        for got in gots:
            total += got[at].astype(f32)
        if j == 0:
            mine_ref[...] = total.astype(bf16)
        else:
            sends[j - 1][:each] = total.astype(bf16)
            sends[j - 1][each:] = low
            send(sends[j - 1])


def plain_hop(parts, own, keep, small, gots):
    rows, width = keep.shape
    small = [part.astype(f32) for part in [small] + [got[rows:] for got in gots]]
    while len(small) > 1:
        small = [small[i] + small[i + 1] for i in range(0, len(small), 2)]
    sent = small[0].astype(bf16)
    kept = sent if parts > 1 else small[0]
    total = keep.astype(f32)
    for got in gots:
        total += got[:rows].astype(f32)
    total = total.astype(bf16).reshape(parts, rows // parts, width)
    sends = [jnp.concatenate([pick(total, own[0] ^ j), sent], 0) for j in range(1, parts)]
    return sends + [pick(total, own[0]), kept]


def hop(pin, parts, own, keep, small, gots):
    rows, width = keep.shape
    each = rows // parts
    if each % 16:
        return plain_hop(parts, own, keep, small, gots)
    tall = small.shape[0]
    return call(
        pin,
        functools.partial(hop_kernel, parts),
        "hop",
        [("s", own), ("v", keep), ("v", small)] + [("h", got) for got in gots],
        [("h", (each + tall, width), bf16)] * (parts - 1)
        + [("v", (each, width), bf16) if parts > 1 else ("h", (each, width), bf16)]
        + [("v", small.shape, bf16) if parts > 1 else ("h", small.shape, f32)],
    )


def program(
    slots,
    head_slots,
    pin,
    tokens,
    lengths,
    answer,
    head_order,
    neuron_order,
    w_qkv,
    b_qv,
    w_out,
    b_out,
    ln1_gain,
    ln1_bias,
    w_in,
    b_in,
    w_down,
    b_down,
    ln2_gain,
    ln2_bias,
    w_span,
    out_grad,
):
    rank = lax.axis_index("mp")
    dp_index = lax.axis_index("dp")
    ranks = lax.axis_size("mp")
    n_dp = lax.axis_size("dp")
    rows, own_len, model_dim = tokens.shape
    full = rows * own_len
    head_width = w_qkv.shape[2]
    group_heads = head_width // HEAD_DIM
    all_heads = ranks * group_heads
    ff_width = w_in.shape[1]
    half_slots = head_slots // 2
    core = rank % 2
    others = [rank ^ o for o in range(rows)]
    right = bit_of(dp_index, 1) == 1
    right_one = right.astype(i32)[None]
    groups = z_groups()
    pieces = n_dp // 2
    piece = slots // pieces
    place = jnp.stack([rank, dp_index]).astype(i32)
    lanes = 128

    tall = 4 * HEAD_DIM
    (head_rows,) = call(
        pin,
        rows_kernel,
        "rows",
        [("h", w_qkv.transpose(1, 0, 2)), ("h", w_out)],
        [("h", (group_heads * tall, model_dim), bf16)],
    )
    far_rows = swap(head_rows, "mp", 1)
    extra = jnp.concatenate(
        [
            jnp.pad(b_in[None], ((0, 0), (0, model_dim - ff_width))),
            jnp.pad(b_qv.reshape(1, -1), ((0, 0), (0, model_dim - 2 * head_width))),
            jnp.zeros((EXTRA - 2, model_dim), bf16),
        ],
        0,
    )
    unit_order = after(neuron_order[:LIVE_FF][None], head_rows)
    sent_units, unit_pick, unit_rows, unit_at = call(
        pin,
        functools.partial(units_kernel, (pieces - 1).bit_length()),
        "units",
        [("s", place), ("h", unit_order), ("h", w_in), ("h", w_down)],
        [
            ("h", (2, slots // 2, model_dim // 2), bf16),
            ("h", (slots, ff_width), bf16),
            ("h", (2, slots, model_dim), bf16),
            ("h", (ranks * ff_width // lanes, lanes), i32),
        ],
    )
    far_units = swap(sent_units, "mp", 2)
    sent_blocks = [jnp.concatenate([pick(tokens, other), extra], 0) for other in others]
    *sent_blocks, _, far_rows = lax.optimization_barrier((*sent_blocks, sent_units, far_rows))
    blocks = [swap(block, "mp", o) if o else block for o, block in enumerate(sent_blocks)]

    sent_heads, heads, my_slots = call(
        pin,
        functools.partial(choose_kernel, group_heads),
        "choose",
        [("s", place), ("s", head_order), ("h", after(head_rows, *sent_blocks)), ("h", far_rows)],
        [
            ("h", (half_slots * tall, model_dim), bf16),
            ("s", (2, head_slots), i32),
            ("s", (group_heads,), i32),
        ],
        [((all_heads,), i32)],
    )
    across = swap(after(sent_heads, *blocks), "mp", 2)
    pair_rows = swap(unit_rows, "mp", 1)
    scalars = jnp.concatenate([pick(lengths, rank)[None], pick(answer, rank), right_one])
    vectors = jnp.concatenate([b_out, ln1_gain, ln1_bias, b_down, ln2_gain, ln2_bias, b_out, b_out])
    vectors = vectors.astype(f32).reshape(8, model_dim)
    span = w_span.T
    grad_blocks = [pick(out_grad, other) for other in others]
    far_units, vectors, span, scalars, *grad_blocks = lax.optimization_barrier(
        (far_units, vectors, span, scalars, *grad_blocks, sent_heads)
    )[: 4 + rows]
    far_units = jnp.concatenate([far_units, swap(far_units, "dp", groups[0][0])], 1)
    far_side = swap(far_units, "dp", 1)
    *blocks, pair_rows = lax.optimization_barrier((*blocks, pair_rows, sent_heads))[: rows + 1]

    saved_outs = [("v", (head_slots, full, HEAD_DIM), bf16)] * 3 + [
        ("v", (head_slots, full, full), bf16),
        ("v", (head_slots * HEAD_DIM, full), bf16),
    ]
    lengths_in = [("s", place), ("s", lengths)]
    own_part, x_row, spots, head_bias, bias_in, own_heads, *own_saved = call(
        pin,
        functools.partial(attend_own_kernel, own_len, group_heads),
        "attend_own",
        lengths_in
        + [("s", heads), ("r", head_rows), ("r", far_rows)]
        + [("h", block) for block in blocks],
        [
            ("v", (full, model_dim), f32),
            ("b", (full, model_dim), bf16),
            ("h", (full, 1), i32),
            ("h", (2, head_slots, 2, HEAD_DIM), f32),
            ("h", (rows, model_dim), f32),
            ("b", (head_slots, tall, model_dim), bf16),
        ]
        + saved_outs,
        [((2 * group_heads * tall, model_dim), bf16), ((all_heads, 8, HEAD_DIM), f32)],
        sems=2,
    )
    unit_at = unit_at.reshape(ranks, ff_width)
    near_at = jnp.stack([pick(unit_at, other) for other in others])
    unit_bias = near_at[:, :, None] == jnp.arange(slots, dtype=i32)
    unit_bias = jnp.sum(jnp.where(unit_bias, bias_in[:, :ff_width, None], 0.0), 1)
    far_side, own_part = lax.optimization_barrier((far_side, own_part))
    far_pair = swap(far_units, "mp", 1)
    side_pair = swap(far_side, "mp", 1)
    across = after(across, far_side)
    other_sources = [across, swap(across, "mp", 1)]
    grad_blocks = [
        swap(after(block, across), "mp", o) if o else block for o, block in enumerate(grad_blocks)
    ]
    first_unit, first_inv, normed_low, *other_saved = call(
        pin,
        attend_kernel,
        "attend",
        lengths_in
        + [("s", heads), ("h", spots), ("h", head_bias), ("h", vectors)]
        + [("v", own_part), ("b", x_row)]
        + [("b", source) for source in other_sources],
        [
            ("v", (full, model_dim), f32),
            ("v", (full, 1), f32),
            ("v", (full, model_dim), bf16),
        ]
        + saved_outs,
        [((full, model_dim), f32)],
    )
    normed_low, side_pair, far_pair, *grad_blocks = lax.optimization_barrier(
        (normed_low, side_pair, far_pair, *grad_blocks)
    )
    far_units = [far_units, far_side, far_pair, side_pair]

    unit_side = (2, ranks // 2, slots, model_dim)
    hidden_dims = (ranks, full, slots)
    block_dims = (ranks, slots, model_dim)
    unit_far, layer_out, row_loss, loss_small, grad_second, grad_upper, *kept_units = call(
        pin,
        feed_kernel,
        "feed",
        [("s", scalars), ("v", normed_low), ("v", first_unit), ("h", vectors), ("h", unit_bias)]
        + [("b", unit_rows), ("b", pair_rows)]
        + [("b", u) for u in far_units]
        + [("h", spots), ("h", span)]
        + [("b", block) for block in grad_blocks],
        [
            ("h", unit_side, bf16),
            ("b", (full, model_dim), bf16),
            ("h", (1, 1), f32),
            ("h", (8, model_dim), f32),
            ("v", (full, model_dim), f32),
            ("v", hidden_dims, bf16),
            ("v", block_dims, bf16),
            ("v", block_dims, bf16),
            ("v", hidden_dims, bf16),
            ("v", hidden_dims, bf16),
        ],
        [
            ((full, model_dim), f32),
            ((full, model_dim), f32),
            ((full, model_dim), f32),
            ((full, 4), f32),
        ],
    )
    unit_got = swap(unit_far, "mp", 1)
    unit_near, first_small, grad_resid, grad_attended, slot_bias_grad = call(
        pin,
        feed_back_kernel,
        "feed_back",
        [("v", grad_upper), ("v", kept_units[0]), ("v", grad_second), ("v", first_unit)]
        + [("v", first_inv), ("h", vectors), ("v", normed_low)]
        + [("v", a) for a in kept_units[1:]],
        [
            ("v", unit_side, bf16),
            ("h", (8, model_dim), f32),
            ("v", (full, model_dim), f32),
            ("v", (full, model_dim), bf16),
            ("h", (ranks, slots), f32),
        ],
        [((full, model_dim), f32), (hidden_dims, bf16)],
    )

    halves = (slots, model_dim // 2)
    down_send, in_send, down_keep, in_keep = call(
        pin,
        merge_kernel,
        "merge",
        [("s", right_one), ("v", unit_near), ("h", unit_got)],
        [
            ("h", (slots, model_dim), bf16),
            ("h", (2,) + halves, bf16),
            ("b", (slots, model_dim), bf16),
            ("b", (2,) + halves, bf16),
        ],
    )
    grad_attended = after(grad_attended, down_send, in_send)
    down_got = swap(down_send, "mp", 2)
    in_got = swap(in_send, "dp", 1)

    head_far, head_near, late, rows_far, rows_near = call(
        pin,
        functools.partial(attend_back_kernel, own_len),
        "attend_back",
        [("s", heads), ("v", grad_attended), ("v", grad_resid), ("b", x_row)]
        + [("v", a) for a in own_saved]
        + [("b", own_heads)]
        + [("v", a) for a in other_saved]
        + [("l", a) for a in other_sources + [layer_out]],
        [
            ("h", (head_slots * tall, model_dim), bf16),
            ("v", (2, half_slots, tall, model_dim), bf16),
            ("h", (8, model_dim), f32),
        ]
        + [("b", (rows // 2, 2, own_len, model_dim), bf16)] * 2,
        [((full, model_dim), f32)],
    )

    head_far, down_got, in_got = lax.optimization_barrier((head_far, down_got, in_got))
    head_got = swap(head_far, "mp", 1)
    block_hit = (jnp.arange(ranks) ^ rank)[:, None] == jnp.arange(ranks)[None, :]
    place_ids = jnp.arange(pieces, dtype=i32) ^ (dp_index // 2)
    bits = len(masks_of("dp")) - 1
    place_ids = sum(
        (((place_ids >> b) & 1) << (bits - 1 - b) for b in range(bits)), jnp.zeros((pieces,), i32)
    )
    place_hit = place_ids[:, None] == jnp.arange(pieces)
    by_rank = slot_bias_grad.reshape(ranks, 1, 1, pieces, piece)
    by_rank = jnp.where(block_hit[:, :, None, None, None] & place_hit[:, :, None], by_rank, 0.0)
    by_rank = jnp.sum(by_rank, (0, 3)).reshape(-1)
    bias_count = -(-by_rank.shape[0] // model_dim)
    by_rank = jnp.pad(by_rank, (0, bias_count * model_dim - by_rank.shape[0]))
    device_hit = jnp.arange(model_dim) == dp_index * ranks + rank
    late_row = 10 + bias_count
    fill = -(-(late_row + 2) // 16) * 16 - late_row - 2
    loss_high = lax.reduce_precision(row_loss, 8, 7)
    small = jnp.concatenate(
        [
            first_small[:3],
            loss_small[:5],
            by_rank.reshape(-1, model_dim),
            jnp.where(device_hit, loss_high, 0.0),
            jnp.where(device_hit, row_loss - loss_high, 0.0),
            late[:2],
            jnp.zeros((fill, model_dim), f32),
        ],
        0,
    ).astype(bf16)
    small_got = swap(small, "mp", 1)

    kept = half_slots * tall
    small_dims = small.shape
    head_send, keep, small = call(
        pin,
        first_hop_kernel,
        "first_hop",
        [("v", head_near), ("h", head_got), ("h", small), ("h", small_got)],
        [
            ("h", (kept + small_dims[0], model_dim), bf16),
            ("v", (kept, model_dim), bf16),
            ("v", small_dims, bf16),
        ],
    )
    gots = [swap(head_send, "mp", 2)]
    down_got, in_got = lax.optimization_barrier((down_got, in_got, head_send))[:2]
    group = groups[0]
    parts = 1 << len(group)
    part = (slots // parts, model_dim // 2)
    down_send, down_keep, *in_parts = call(
        pin,
        second_merge_kernel,
        "second_merge",
        [("s", right_one), ("b", down_keep), ("h", down_got), ("b", in_keep), ("h", in_got)],
        [("h", halves, bf16), ("b", halves, bf16), ("b", (2,) + part, bf16)]
        + [("h", (2,) + part, bf16)] * (parts - 1),
    )
    down_got = swap(down_send, "dp", 1)
    in_gots = [swap(in_parts[j], "dp", partner(group, j)) for j in range(1, parts)]

    head_hops = [masks_of("dp")[:1]] + groups

    def head_hop(group, keep, small, gots):
        parts = 1 << len(group)
        own = own_bits(group, dp_index)[None].astype(i32)
        *sends, keep, small = hop(pin, parts, own, keep, small, gots)
        gots = [swap(sends[j - 1], "dp", partner(group, j)) for j in range(1, parts)]
        return keep, small, gots

    def widen(keep, group):
        got = [swap(keep, "dp", partner(group, j)) for j in range(1, 1 << len(group))]
        return jnp.concatenate([keep] + got, 0)

    unit_parts = call(
        pin,
        down_parts_kernel,
        "down_parts",
        [("b", down_keep), ("h", down_got)],
        [("h", part, bf16)] * parts,
    )
    down_gots = [swap(unit_parts[j], "dp", partner(group, j)) for j in range(1, parts)]
    gots[0] = after(gots[0], unit_parts[1])
    keep, small, gots = head_hop(head_hops[0], keep, small, gots)
    in_gots[0] = after(in_gots[0], keep)
    in_send, in_mine = call(
        pin,
        in_sum_kernel,
        "in_sum",
        [("b", in_parts[0])] + [("h", got) for got in in_gots],
        [("h", part, bf16)] * 2,
    )
    in_send, in_mine = (scatter_over(x, groups[1:]) for x in (in_send, in_mine))
    in_got = swap(in_send, "mp", 2)
    gots[0], in_got, *down_gots = lax.optimization_barrier((gots[0], in_got, *down_gots))
    down_mine = scatter_over(scatter_sum(unit_parts[0], down_gots), groups[1:])
    unit_part = jnp.stack([scatter_sum(in_mine, [in_got]), down_mine])
    rows_got = swap(after(rows_far, keep), "mp", 1)
    gots[0], rows_got = lax.optimization_barrier((gots[0], rows_got))
    rows_across = swap(jnp.stack([rows_near[1], rows_got[1]]), "mp", 2)
    keep, small, gots = head_hop(head_hops[1], keep, small, gots)
    for group in head_hops[2:]:
        keep, small, gots = head_hop(group, keep, small, gots)
    keep, small = hop(pin, 1, jnp.zeros((1,), i32), keep, small, gots)
    for group in reversed(groups):
        got = [swap(keep, "dp", partner(group, j)) for j in range(1, 1 << len(group))]
        keep = jnp.concatenate([keep] + got, 0)
    unit_part, rows_across, keep = lax.optimization_barrier((unit_part, rows_across, keep))
    own_rows = [rows_near[0], rows_got[0], rows_across[0], rows_across[1]]
    unit_grads = gather_over(unit_part, groups)
    unit_side = swap(unit_grads, "dp", 1)
    mine = widen(keep, head_hops[0])
    unit_grads = join_sides(unit_grads, unit_side, right)
    w_in_grad = mxu(unit_grads[0], unit_pick, 0, 0)
    w_down_grad = mxu(unit_pick, unit_grads[1], 0, 0)
    own_rows = to_own(own_rows, rank)
    layer_out_own = own_rows[:, 0]
    tokens_grad = own_rows[:, 1].astype(f32)
    both = jnp.concatenate([mine, swap(mine, "mp", 1)], 0)

    head_piece = kept // n_dp
    row_ids = jnp.arange(2 * kept, dtype=i32)
    from_core, row_ids = row_ids // kept, row_ids % kept
    own_piece = own_bits([m for group in head_hops for m in group], dp_index)
    natural = ((row_ids // head_piece) ^ own_piece) * head_piece + row_ids % head_piece
    natural = natural + from_core * kept
    columns = jnp.arange(4 * head_width, dtype=i32)
    kind, rest = columns // head_width, columns % head_width
    column_slot = jnp.sum(
        jnp.where((rest // HEAD_DIM)[:, None] == jnp.arange(group_heads), my_slots, 0), 1
    )
    wanted = ((column_slot ^ core) % 2) * kept + (column_slot // 2) * tall
    wanted = wanted + kind * HEAD_DIM + rest % HEAD_DIM
    wanted = jnp.where(column_slot >= 0, wanted, -1)
    row_pick = (natural[:, None] == wanted[None, :]).astype(bf16)
    w_qkv_grad = mxu(both, row_pick[:, : 3 * head_width], 0, 0).reshape(model_dim, 3, head_width)
    w_out_grad = mxu(row_pick[:, 3 * head_width :], both, 0, 0)

    by_rank = small[8 : 8 + bias_count].reshape(-1)[: ranks * slots].reshape(ranks, slots)
    by_rank = pick(by_rank, rank).reshape(pieces, 1, piece)
    by_rank = jnp.sum(jnp.where(place_hit[:, :, None], by_rank, 0.0), 0).reshape(slots)
    b_in_grad = jnp.sum(jnp.where(unit_pick > 0, by_rank[:, None], 0.0), 0)
    losses = small[8 + bias_count] + small[9 + bias_count]
    losses = losses[: n_dp * ranks].reshape(n_dp, ranks)
    losses = lax.dynamic_index_in_dim(losses, dp_index, 0, keepdims=False)
    late = small[late_row : late_row + 2].reshape(2, ranks, head_width)
    b_qv_grad = lax.dynamic_index_in_dim(late, rank, 1, keepdims=False)
    return (
        layer_out_own,
        losses,
        tokens_grad,
        w_qkv_grad,
        b_qv_grad,
        w_out_grad,
        small[2],
        small[0],
        small[1],
        w_in_grad,
        b_in_grad,
        w_down_grad,
        small[5],
        small[3],
        small[4],
        small[6:8].T,
    )


def shards(*args):
    head_order, neuron_order, w_qkv, w_in = args[3], args[4], args[5], args[11]
    ranks = lax.axis_size("mp")
    pair_heads = 2 * w_qkv.shape[2] // HEAD_DIM
    ff_width = w_in.shape[1]
    (fits,) = call(
        False,
        functools.partial(fits_kernel, UNIT_SLOTS, HEAD_SLOTS, ff_width, pair_heads, ranks),
        "fits",
        [("s", head_order), ("h", neuron_order[:LIVE_FF][None])],
        [("s", (1,), i32)],
    )
    return lax.cond(
        fits[0] == 1,
        functools.partial(program, UNIT_SLOTS, HEAD_SLOTS, True),
        functools.partial(program, ff_width, pair_heads, False),
        *args,
    )


def solution(mesh):
    return jax.shard_map(
        shards,
        mesh=mesh,
        in_specs=(
            P("dp", "mp", None),
            P("dp"),
            P("dp", None),
            P(),
            P(),
            P(None, None, "mp"),
            P(None, "mp"),
            P("mp", None),
            P(),
            P(),
            P(),
            P(None, "mp"),
            P("mp"),
            P("mp", None),
            P(),
            P(),
            P(),
            P(),
            P("dp", "mp", None),
        ),
        out_specs=(
            P("dp", "mp", None),
            P("dp"),
            P("dp", "mp", None),
            P(None, None, "mp"),
            P(None, "mp"),
            P("mp", None),
            P(),
            P(),
            P(),
            P(None, "mp"),
            P("mp"),
            P("mp", None),
            P(),
            P(),
            P(),
            P(),
        ),
        check_vma=False,
    )
```

```python
import functools
import math

import jax
import jax.numpy as jnp
from jax import lax
from jax.experimental import pallas as pl
from jax.experimental.pallas import tpu as pltpu
from jax.sharding import PartitionSpec as P

HEAD_DIM = 64
LIVE_HEADS = 6
LIVE_FF = 1536
UNIT_SLOTS = 448
HEAD_SLOTS = 4
EXTRA = 16
MASKED = -1000000000.0
VMEM_MOST = 60 * 2**20
VMEM_SPARE = 8 * 2**20

f32 = jnp.float32
bf16 = jnp.bfloat16
i32 = jnp.int32
epsilon = 1e-12


def swap(x, axis, mask):
    return lax.ppermute(x, axis, [(i, i ^ mask) for i in range(lax.axis_size(axis))])


def masks_of(axis):
    return [1 << b for b in range((lax.axis_size(axis) - 1).bit_length())]


def bit_of(index, mask):
    return (index // mask) % 2


def pick(stacked, index):
    return lax.dynamic_index_in_dim(stacked, index, 0, keepdims=False)


def after(value, *others):
    return lax.optimization_barrier((value,) + others)[0]


def to_own(got, rank):
    for mask in masks_of("mp"):
        moved = bit_of(rank, mask) == 1
        got = [jnp.where(moved, got[r ^ mask], got[r]) for r in range(len(got))]
    return jnp.stack(got, 0)


def z_groups():
    masks = masks_of("dp")[1:]
    return [masks[i : i + 2] for i in range(0, len(masks), 2)]


def partner(group, j):
    return sum(m for i, m in enumerate(group) if (j >> (len(group) - 1 - i)) & 1)


def own_bits(group, dp_index):
    place = 0
    for mask in group:
        place = place * 2 + bit_of(dp_index, mask)
    return place


def join_sides(mine, other, right):
    return jnp.concatenate([jnp.where(right, other, mine), jnp.where(right, mine, other)], -1)


def gather_over(x, groups):
    for group in reversed(groups):
        got = [swap(x, "dp", partner(group, j)) for j in range(1, 1 << len(group))]
        x = jnp.concatenate([x] + got, -2)
    return x


def scatter_sum(x, got):
    x = x.astype(f32)
    for term in got:
        x = x + term.astype(f32)
    return x.astype(bf16)


def scatter_over(x, groups):
    for group in groups:
        n = 1 << len(group)
        rows = x.shape[-2] // n
        parts = [x[..., j * rows : (j + 1) * rows, :] for j in range(n)]
        x = scatter_sum(parts[0], [swap(parts[j], "dp", partner(group, j)) for j in range(1, n)])
    return x


class Incoming:
    def __init__(self, source, held, sem, late):
        self.copy, self.held, self.waiting = pltpu.make_async_copy(source, held, sem), held, True
        self.shape, self.started = held.shape, False
        if not late:
            self.start()

    def start(self):
        if not self.started:
            self.started = True
            self.copy.start()

    def ready(self):
        if self.waiting:
            self.start()
            self.copy.wait()
            self.waiting = False
        return self.held

    def __getitem__(self, index):
        return self.ready()[index]

    @property
    def at(self):
        return self.ready().at


class Outgoing:
    def __init__(self, held, target, sem):
        self.held, self.target, self.sem, self.sent = held, target, sem, False
        self.shape, self.at = held.shape, held.at

    def __getitem__(self, index):
        return self.held[index]

    def __setitem__(self, index, value):
        self.held[index] = value

    def send(self, *index):
        self.sent = True
        if index:
            pltpu.make_async_copy(self.held.at[index], self.target.at[index], self.sem).start()
        else:
            pltpu.make_async_copy(self.held, self.target, self.sem).start()

    def wait(self):
        if not self.sent:
            self.send()
        pltpu.make_async_copy(self.held, self.target, self.sem).wait()


def start(*refs):
    for ref in refs:
        if isinstance(ref, Incoming):
            ref.start()


def ready(*refs):
    for ref in refs:
        if isinstance(ref, Incoming):
            ref.ready()


def send(*refs):
    for ref in refs:
        if isinstance(ref, Outgoing):
            ref.send()


def held(item):
    dims, size = item.shape, jnp.dtype(item.dtype).itemsize
    if len(dims) < 2:
        return 4096
    tall = 32 // size
    return -(-dims[-1] // 128) * 128 * (-(-dims[-2] // tall) * tall) * size * math.prod(dims[:-2])


def shape(dims, kind):
    return jax.ShapeDtypeStruct(dims, kind)


PLACES = {"v": pltpu.VMEM, "b": pltpu.HBM, "l": pltpu.HBM, "r": pltpu.HBM}


def call(pin, kernel, name, ins, outs, scratch=(), sems=0, flops=1e6, moved=5e6):
    in_kinds = [k if k != "v" or pin else "h" for k, _ in ins]
    out_kinds = [k if k != "v" or pin else "h" for k, _, _ in outs]
    args = [
        pltpu.with_memory_space_constraint(a, PLACES[k]) if k in PLACES else a
        for k, (_, a) in zip(in_kinds, ins)
    ]
    out_shape = [
        PLACES[k](d, t) if k in PLACES else shape(d, t) for k, (_, d, t) in zip(out_kinds, outs)
    ]
    buffers = [shape(a.shape, a.dtype) for k, a in zip(in_kinds, args) if k in "hbl"]
    buffers += [shape(d, t) for k, (_, d, t) in zip(out_kinds, outs) if k in "hb"]
    scratch = [shape(d, t) for d, t in scratch]
    count, outs_count = len(in_kinds), len(out_kinds)

    def whole(*refs):
        given, results, refs = refs[:count], refs[count : count + outs_count], refs[count + outs_count :]
        bufs, refs = iter(refs[: len(buffers)]), refs[len(buffers) :]
        in_sem, out_sem = refs[:2]
        given = [
            Incoming(ref, next(bufs), in_sem.at[i], k == "l") if k in "hbl" else ref
            for i, (k, ref) in enumerate(zip(in_kinds, given))
        ]
        results = [
            Outgoing(next(bufs), ref, out_sem.at[i]) if k in "hb" else ref
            for i, (k, ref) in enumerate(zip(out_kinds, results))
        ]
        kernel(*given, *results, *refs[2:])
        ready(*given)
        for ref in results:
            if isinstance(ref, Outgoing):
                ref.wait()

    spaces = {"s": pltpu.SMEM, "v": pltpu.VMEM, "h": pl.ANY, "b": pltpu.HBM, "l": pltpu.HBM, "r": pltpu.HBM}
    limit = sum(held(b) for b in buffers + scratch) + VMEM_SPARE
    return pl.pallas_call(
        whole,
        name=name,
        out_shape=out_shape,
        in_specs=[pl.BlockSpec(memory_space=spaces[k]) for k in in_kinds],
        out_specs=[pl.BlockSpec(memory_space=spaces[k]) for k in out_kinds],
        scratch_shapes=[pltpu.VMEM(b.shape, b.dtype) for b in buffers]
        + [pltpu.SemaphoreType.DMA((count,)), pltpu.SemaphoreType.DMA((outs_count,))]
        + [pltpu.SMEM(s.shape, s.dtype) if s.dtype == i32 else pltpu.VMEM(s.shape, s.dtype) for s in scratch]
        + ([pltpu.SemaphoreType.DMA((sems,))] if sems else []),
        compiler_params=pltpu.CompilerParams(vmem_limit_bytes=min(VMEM_MOST, int(limit))),
        cost_estimate=pl.CostEstimate(flops=int(flops), bytes_accessed=int(moved), transcendentals=0),
    )(*args)


def row_sum(v):
    return jnp.sum(v, 0, keepdims=True)


def lane_mean(v):
    return jnp.mean(v, -1, keepdims=True)


def mxu(a, b, a_dim, b_dim):
    return lax.dot_general(a, b, (((a_dim,), (b_dim,)), ((), ())), preferred_element_type=f32)


def loop(count, body):
    def step(i, carry):
        body(i)
        return carry

    lax.fori_loop(0, count, step, 0)


def span_of(i, size):
    return pl.ds(i * size if isinstance(i, int) else pl.multiple_of(i * size, size), size)


def by_rows(full, size, body):
    loop(full // size, lambda i: body(span_of(i, size)))


def fits_kernel(unit_slots, head_slots, ff_width, pair_heads, ranks, heads_ref, order_ref, fits_ref):
    order = order_ref[...]
    most = jnp.zeros((1, 1), f32)
    for r in range(ranks):
        mine = (order >= r * ff_width) & (order < (r + 1) * ff_width)
        most = jnp.maximum(most, jnp.sum(jnp.where(mine, 1.0, 0.0), keepdims=True))
    fine = jnp.where(most[0, 0] <= unit_slots, 1, 0)
    for pair in range(ranks // 2):
        count = 0
        for k in range(LIVE_HEADS):
            count += jnp.where(heads_ref[k] // pair_heads == pair, 1, 0)
        fine *= jnp.where(count <= head_slots, 1, 0)
    fits_ref[0] = fine


def rows_kernel(qkv_ref, out_ref, rows_ref):
    square = (HEAD_DIM, HEAD_DIM)
    diagonal = lax.broadcasted_iota(i32, square, 0) == lax.broadcasted_iota(i32, square, 1)
    diagonal = jnp.where(diagonal, 1.0, 0.0).astype(bf16)
    for g in range(out_ref.shape[0] // HEAD_DIM):
        at = slice(g * HEAD_DIM, (g + 1) * HEAD_DIM)
        parts = [mxu(diagonal, qkv_ref[c, :, at], 1, 1).astype(bf16) for c in range(3)]
        rows_ref[g * 4 * HEAD_DIM : (g + 1) * 4 * HEAD_DIM] = jnp.concatenate(parts + [out_ref[at]], 0)


def choose_kernel(group, place_ref, order_ref, rows_ref, far_ref, send_ref, heads_ref, slots_ref, table_ref):
    tall = 4 * HEAD_DIM
    rank = place_ref[0]
    core, pair = rank % 2, rank // 2
    counts = {}
    for head in range(order_ref.shape[0]):
        count = counts.get(head // (2 * group), 0)
        live = 0
        for k in range(LIVE_HEADS):
            live += jnp.where(order_ref[k] == head, 1, 0)
        table_ref[head] = jnp.where(live > 0, count, -1)
        counts[head // (2 * group)] = count + live
    half = heads_ref.shape[1] // 2
    for side in range(2):
        for e in range(2 * half):
            heads_ref[side, e] = -1
    for k in range(LIVE_HEADS):
        head = order_ref[k]
        side = jnp.where(head // (2 * group) != pair, 1, 0)
        heads_ref[side, table_ref[head] ^ core] = head
    for g in range(group):
        slots_ref[g] = table_ref[rank * group + g]
    ready(rows_ref, far_ref)
    for j in range(half):
        head = jnp.maximum(heads_ref[0, 2 * j], 0)
        at = pl.ds(pl.multiple_of((head % group) * tall, tall), tall)
        mine = (head // group == rank) | (heads_ref[0, 2 * j] < 0)
        target = slice(j * tall, (j + 1) * tall)

        @pl.when(mine)
        def own():
            send_ref[target] = rows_ref[at]

        @pl.when(jnp.logical_not(mine))
        def far():
            send_ref[target] = far_ref[at]


def units_kernel(zbits, place_ref, order_ref, in_ref, down_ref, *refs):
    sides_ref, pick_ref, rows_ref, at_ref = refs
    slots, width = pick_ref.shape
    side = sides_ref.shape[2]
    piece = slots >> zbits
    rank, dp_index = place_ref[0], place_ref[1]
    lanes = at_ref.shape[1]
    per = width // lanes
    order = order_ref[...]

    def hot(dims, index):
        return jnp.where(lax.broadcasted_iota(i32, dims, 0) == index, 1.0, 0.0).astype(bf16)

    count = order.shape[1]
    row_hot = hot((at_ref.shape[0], count), order // lanes)
    lane_hot = hot((lanes, count), order % lanes)
    live = mxu(row_hot, lane_hot, 1, 1)
    square = (lanes, lanes)
    first, second = (lax.broadcasted_iota(i32, square, d) for d in range(2))
    upto = jnp.where(first <= second, 1.0, 0.0).astype(bf16)
    within = mxu(live.astype(bf16), upto, 1, 0)
    totals = mxu(live.astype(bf16), jnp.ones(square, bf16), 1, 0)
    square = (at_ref.shape[0], at_ref.shape[0])
    first, second = (lax.broadcasted_iota(i32, square, d) for d in range(2))
    earlier = (second < first) & (second // per == first // per)
    offsets = mxu(jnp.where(earlier, 1.0, 0.0).astype(bf16), totals.astype(bf16), 1, 0)
    slot = (offsets + within).astype(i32) - 1
    index = jnp.zeros(slot.shape, i32)
    for p in range(1, slots // piece):
        index += jnp.where(slot >= p * piece, 1, 0)
    inside = slot - index * piece
    index = index ^ (dp_index // 2)
    place = jnp.zeros(slot.shape, i32)
    for b in range(zbits):
        place = place * 2 + ((index >> b) & 1)
    at_ref[...] = jnp.where(live > 0.5, place * piece + inside, -1)
    ids = lax.broadcasted_iota(i32, (slots, lanes), 0)
    for c in range(per):
        row = at_ref[pl.ds(rank * per + c, 1)]
        pick_ref[:, c * lanes : (c + 1) * lanes] = jnp.where(ids == row, 1.0, 0.0).astype(bf16)
    right = dp_index % 2 == 1
    rows_in = mxu(pick_ref[...], in_ref[...], 1, 1).astype(bf16)
    part = sides_ref.shape[1]
    sides_ref[0] = jnp.where(right, rows_in[:part, side:], rows_in[:part, :side])
    rows_ref[0] = rows_in
    rows_down = mxu(pick_ref[...], down_ref[...], 1, 0).astype(bf16)
    sides_ref[1] = jnp.where(right, rows_down[:part, side:], rows_down[:part, :side])
    send(sides_ref)
    rows_ref[1] = rows_down


def source_of(sources, j, i):
    if len(sources) == 1:
        return sources[0].at[2 * j + i]
    return sources[i].at[span_of(j, 4 * HEAD_DIM)]


def each_head(heads_ref, side, body):
    def two(j):
        for i in range(2):
            pl.when(heads_ref[side, 2 * j + i] >= 0)(functools.partial(body, j, i))

    loop(heads_ref.shape[1] // 2, two)


def out_rows(sources, slots):
    parts = [source_of(sources, e // 2, e % 2)[3 * HEAD_DIM :] for e in range(slots)]
    return jnp.concatenate(parts, 0)


def attend_heads(side, x_ref, heads_ref, valid, bias_ref, sources, outs):
    q_ref, k_ref, v_ref, probs_ref, ctx_ref = outs
    wide = 3 * HEAD_DIM
    half = x_ref.shape[0] // 2
    ctx_ref[...] = jnp.zeros(ctx_ref.shape, bf16)

    def attend_head(j, i):
        e = 2 * j + i
        bias = bias_ref[side, e]
        both = mxu(x_ref[...], source_of(sources, j, i)[:wide], 1, 1)
        query = (both[:, :HEAD_DIM] + bias[0:1]).astype(bf16)
        key = both[:, HEAD_DIM : 2 * HEAD_DIM].astype(bf16)
        value = (both[:, 2 * HEAD_DIM :] + bias[1:2]).astype(bf16)
        q_ref[e], k_ref[e], v_ref[e] = query, key, value
        for c in range(2):
            part = slice(c * half, (c + 1) * half)
            scores = mxu(key, query[part], 1, 1) * HEAD_DIM ** (-0.5)
            scores = jnp.where(valid, scores, MASKED)
            exp_scores = jnp.exp(scores - jnp.max(scores, 0, keepdims=True))
            probs = (exp_scores * (1.0 / row_sum(exp_scores))).astype(bf16)
            probs_ref[e, :, part] = probs
            ctx_ref[span_of(e, HEAD_DIM), part] = mxu(value, probs, 0, 0).astype(bf16)

    each_head(heads_ref, side, attend_head)
    send(*outs)
    return mxu(ctx_ref[...], out_rows(sources, heads_ref.shape[1]), 0, 0)


def attend_own_kernel(own, group, place_ref, lengths_ref, heads_ref, rows_ref, far_ref, *refs):
    blocks, refs = refs[:-14], refs[-14:]
    part_ref, x_ref, spots_ref, bias_ref, unit_bias_ref, heads_out_ref = refs[:6]
    outs, (held_ref, table_ref, sem) = refs[6:11], refs[11:]
    rank = place_ref[0]
    tall = 4 * HEAD_DIM
    count = group * tall
    copies = [
        pltpu.make_async_copy(ref, held_ref.at[pl.ds(n * count, count)], sem.at[n])
        for n, ref in enumerate((rows_ref, far_ref))
    ]
    for copy in copies:
        copy.start()
    for o, block in enumerate(blocks):
        x_ref[o * own : (o + 1) * own] = block[:own]
        ids = lax.broadcasted_iota(i32, (own, 1), 0)
        spots_ref[o * own : (o + 1) * own] = ids + (rank ^ o) * own
        extra = block[own : own + EXTRA].astype(f32)
        unit_bias_ref[o : o + 1] = extra[0:1]
        for g in range(group):
            for n in range(2):
                at = (n * group + g) * HEAD_DIM
                table_ref[o * group + g, n : n + 1] = extra[1:2, at : at + HEAD_DIM]
    for side in range(2):
        for e in range(heads_ref.shape[1]):
            head = jnp.maximum(heads_ref[side, e], 0)
            bias_ref[side, e] = table_ref[((head // group) ^ rank) * group + head % group][:2]
    for copy in copies:
        copy.wait()
    for e in range(heads_ref.shape[1]):
        head = jnp.maximum(heads_ref[0, e], 0)
        at = jnp.where(head // group == rank, 0, count) + (head % group) * tall
        heads_out_ref[e] = held_ref[pl.ds(pl.multiple_of(at, tall), tall)]
    valid = spots_ref[...] < lengths_ref[rank]
    part_ref[...] = attend_heads(0, x_ref, heads_ref, valid, bias_ref, [heads_out_ref], outs)


def attend_kernel(place_ref, lengths_ref, heads_ref, spots_ref, bias_ref, vec_ref, part_ref, x_ref, *refs):
    sources, refs = refs[:2], refs[2:]
    unit_ref, inv_ref, low_ref, sum_ref = refs[:3] + refs[-1:]
    valid = spots_ref[...] < lengths_ref[place_ref[0]]
    ready(bias_ref, vec_ref, part_ref, x_ref, *sources)
    sum_ref[...] = attend_heads(1, x_ref, heads_ref, valid, bias_ref, sources, refs[3:-1])

    def norm(rows):
        first_sum = x_ref[rows].astype(f32) + (part_ref[rows] + sum_ref[rows]) + vec_ref[0:1]
        centered = first_sum - lane_mean(first_sum)
        inv = lax.rsqrt(lane_mean(centered * centered) + epsilon)
        unit = centered * inv
        unit_ref[rows] = unit
        inv_ref[rows] = inv
        low_ref[rows] = (unit * vec_ref[1:2] + vec_ref[2:3]).astype(bf16)

    by_rows(sum_ref.shape[0], 128, norm)


def join_block(target, mine, other, kind, right):
    half = mine.shape[-1]
    one, two = mine[kind], other[kind]
    target[:, :half] = jnp.where(right, two, one)
    target[:, half:] = jnp.where(right, one, two)


def feed_kernel(scalar_ref, low_ref, unit_ref, vec_ref, bias_ref, *refs):
    near_units, sides, refs = refs[:2], refs[2:6], refs[6:]
    spots_ref, span_ref, refs = refs[0], refs[1], refs[2:]
    grads, refs = refs[:-14], refs[-14:]
    far_ref, out_ref, loss_ref, small_ref, second_ref, upper_ref, ins_ref = refs[:7]
    downs_ref, hidden_ref, slope_ref, total_ref, layer_ref, two_ref, logit_ref = refs[7:]
    full = low_ref.shape[0]
    half = full // 2
    right = scalar_ref[3] == 1
    ready(low_ref, unit_ref, vec_ref, bias_ref, *near_units)

    def first(rows):
        total_ref[rows] = unit_ref[rows] * vec_ref[1:2] + vec_ref[2:3] + vec_ref[3:4]

    by_rows(full, 128, first)
    for o in range(2):
        ins_ref[o] = near_units[o][0]
        downs_ref[o] = near_units[o][1]

    def forward(o):
        for r in range(2):
            rows = slice(r * half, (r + 1) * half)
            upper = mxu(low_ref[rows], ins_ref[o], 1, 1) + bias_ref[pl.ds(o, 1)]
            cumulative = 0.5 * (1.0 + lax.erf(upper * 0.7071067811865476))
            density = jnp.exp(-0.5 * upper * upper) * 0.3989422804014327
            hidden = (upper * cumulative).astype(bf16)
            hidden_ref[o, rows] = hidden
            slope_ref[o, rows] = (cumulative + upper * density).astype(bf16)
            total_ref[rows] += mxu(hidden, downs_ref[o], 1, 0)

    loop(2, forward)
    ready(*sides)
    for o in range(2):
        join_block(ins_ref.at[2 + o], sides[2 * o], sides[2 * o + 1], 0, right)
        join_block(downs_ref.at[2 + o], sides[2 * o], sides[2 * o + 1], 1, right)
    loop(2, lambda o: forward(o + 2))
    ready(spots_ref, span_ref, *grads)

    def norm(rows):
        second_sum = total_ref[rows]
        centered = second_sum - lane_mean(second_sum)
        inv = lax.rsqrt(lane_mean(centered * centered) + epsilon)
        unit = centered * inv
        layer_out = unit * vec_ref[4:5] + vec_ref[5:6]
        two_ref[rows] = unit
        layer_ref[rows] = layer_out
        out_ref[rows] = layer_out.astype(bf16)
        logit_ref[rows, 2:3] = inv
        for c in range(2):
            logit_ref[rows, c : c + 1] = jnp.sum(layer_out * span_ref[c : c + 1], -1, keepdims=True)

    by_rows(full, 128, norm)
    small_ref[...] = jnp.zeros(small_ref.shape, f32)
    spots = spots_ref[...]
    valid = spots < scalar_ref[0]
    loss = jnp.zeros((1, 1), f32)
    for c in range(2):
        logits = logit_ref[:, c : c + 1]
        masked = jnp.where(valid, logits, MASKED)
        top = jnp.max(masked, 0, keepdims=True)
        exp_logits = jnp.exp(masked - top)
        total = row_sum(exp_logits)
        chosen = spots == scalar_ref[1 + c]
        loss += top + jnp.log(total) - row_sum(jnp.where(chosen, logits, 0.0))
        logit_ref[:, c : c + 1] = exp_logits / total - jnp.where(chosen, 1.0, 0.0)
    loss_ref[...] = loss
    own = full // len(grads)
    for o, grad in enumerate(grads):
        rows = slice(o * own, (o + 1) * own)
        unit, layer_out, inv = two_ref[rows], layer_ref[rows], logit_ref[rows, 2:3]
        grad_out = grad[...].astype(f32)
        for c in range(2):
            grad_logits = logit_ref[rows, c : c + 1]
            grad_out += grad_logits * span_ref[c : c + 1]
            small_ref[3 + c : 4 + c] += row_sum(layer_out * grad_logits)
        small_ref[0:1] += row_sum(grad_out * unit)
        small_ref[1:2] += row_sum(grad_out)
        grad_normed = grad_out * vec_ref[4:5]
        second = inv * (
            grad_normed - lane_mean(grad_normed) - unit * lane_mean(grad_normed * unit)
        )
        second_ref[rows] = second
        small_ref[2:3] += row_sum(second)

    branch_grad = second_ref[...].astype(bf16)
    args = (branch_grad, low_ref, downs_ref, hidden_ref, slope_ref, upper_ref)
    loop(2, lambda j: back_block(2 * j + 1, *args, far_ref.at[:, j]))


def back_block(o, branch_grad, low_ref, downs_ref, hidden_ref, slope_ref, upper_ref, target):
    hidden_grad = mxu(branch_grad, downs_ref[o], 1, 1)
    upper = (hidden_grad * slope_ref[o].astype(f32)).astype(bf16)
    upper_ref[o] = upper
    target[1] = mxu(hidden_ref[o], branch_grad, 0, 0).astype(bf16)
    target[0] = mxu(upper, low_ref[...], 0, 0).astype(bf16)


def feed_back_kernel(upper_ref, ins_ref, second_ref, unit_ref, inv_ref, vec_ref, *refs):
    low_ref, downs_ref, hidden_ref, slope_ref = refs[:4]
    near_ref, small_ref, resid_ref, att_ref, bias_ref, first_ref, near_upper_ref = refs[4:]
    ready(upper_ref, ins_ref, second_ref, low_ref, downs_ref, hidden_ref, slope_ref)
    first_ref[...] = second_ref[...]

    def back(j):
        branch_grad = second_ref[...].astype(bf16)
        args = (branch_grad, low_ref, downs_ref, hidden_ref, slope_ref, near_upper_ref)
        back_block(2 * j, *args, near_ref.at[:, j])
        for upper, o in ((near_upper_ref[2 * j], 2 * j), (upper_ref[2 * j + 1], 2 * j + 1)):
            first_ref[...] += mxu(upper, ins_ref[o], 1, 0)
            bias_ref[pl.ds(o, 1)] = row_sum(upper.astype(f32))

    loop(upper_ref.shape[0] // 2, back)
    ready(unit_ref, inv_ref, vec_ref)
    small_ref[...] = jnp.zeros(small_ref.shape, f32)

    def norm(rows):
        first, unit = first_ref[rows], unit_ref[rows]
        grad_normed = first * vec_ref[1:2]
        resid = inv_ref[rows] * (
            grad_normed - lane_mean(grad_normed) - unit * lane_mean(grad_normed * unit)
        )
        resid_ref[rows] = resid
        att_ref[rows] = resid.astype(bf16)
        small_ref[0:1] += row_sum(first * unit)
        small_ref[1:2] += row_sum(first)
        small_ref[2:3] += row_sum(resid)

    by_rows(first_ref.shape[0], 128, norm)


def merge_kernel(right_ref, near_ref, got_ref, *refs):
    down_send_ref, in_send_ref, down_keep_ref, in_keep_ref = refs
    right = right_ref[0] == 1
    half = in_send_ref.shape[-1]
    ready(near_ref, got_ref)

    def total(kind, o, rows):
        return (near_ref[kind, o, rows].astype(f32) + got_ref[kind, o, rows].astype(f32)).astype(bf16)

    def merge(rows):
        down_send_ref[rows] = total(1, 1, rows)
        down_keep_ref[rows] = total(1, 0, rows)
        for o in range(2):
            block = total(0, o, rows)
            in_send_ref[o, rows] = jnp.where(right, block[:, :half], block[:, half:])
            in_keep_ref[o, rows] = jnp.where(right, block[:, half:], block[:, :half])

    by_rows(down_send_ref.shape[0], down_send_ref.shape[0] // 4, merge)


def second_merge_kernel(right_ref, down_ref, down_got_ref, in_ref, in_got_ref, *refs):
    down_send_ref, down_keep_ref, parts = refs[0], refs[1], refs[2:]
    right = right_ref[0] == 1
    half = down_send_ref.shape[-1]
    each = parts[0].shape[1]
    for j in range(1, len(parts) + 1):
        j %= len(parts)
        rows = slice(j * each, (j + 1) * each)
        for o in range(2):
            parts[j][o] = (in_ref[o, rows].astype(f32) + in_got_ref[o, rows].astype(f32)).astype(bf16)
        send(parts[j])
        block = (down_ref[rows].astype(f32) + down_got_ref[rows].astype(f32)).astype(bf16)
        down_send_ref[rows] = jnp.where(right, block[:, :half], block[:, half:])
        down_keep_ref[rows] = jnp.where(right, block[:, half:], block[:, :half])


def down_parts_kernel(down_ref, got_ref, *parts):
    each = parts[0].shape[0]
    ready(down_ref, got_ref)
    for j in range(1, len(parts) + 1):
        j %= len(parts)
        rows = slice(j * each, (j + 1) * each)
        parts[j][...] = (down_ref[rows].astype(f32) + got_ref[rows].astype(f32)).astype(bf16)
        send(parts[j])


def in_sum_kernel(in_ref, *refs):
    gots, outs = refs[:-2], refs[-2:]
    for o in (1, 0):
        total = in_ref[o].astype(f32)
        for got in gots:
            total += got[o].astype(f32)
        outs[1 - o][...] = total.astype(bf16)
        send(outs[1 - o])


def attend_back_kernel(own, heads_ref, att_ref, resid_ref, x_ref, *refs):
    sides = ((refs[:5], refs[5:6]), (refs[6:11], refs[11:13]))
    layer_ref, far_ref, near_ref, late_ref = refs[13:17]
    moved, total_ref = refs[17:-1], refs[-1]
    wide = 3 * HEAD_DIM
    scale = HEAD_DIM ** (-0.5)
    _, half_slots, tall, width = near_ref.shape
    lane_head = lax.broadcasted_iota(i32, (1, width), 1) // HEAD_DIM
    slots = heads_ref.shape[1]
    late_ref[...] = jnp.zeros(late_ref.shape, f32)
    far_ref[...] = jnp.zeros(far_ref.shape, bf16)
    near_ref[...] = jnp.zeros(near_ref.shape, bf16)
    full = x_ref.shape[0]
    half = full // 2
    ready(att_ref, resid_ref, x_ref)
    total_ref[...] = resid_ref[...]
    for side, (saved, sources) in enumerate(sides):
        q_ref, k_ref, v_ref, probs_ref, ctx_ref = saved
        ready(*saved, *sources)
        if side == 0:
            start(*sides[1][0], *sides[1][1], layer_ref)
        out_grads = mxu(ctx_ref[...], att_ref[...], 1, 0).astype(bf16)
        for e in range(slots):
            part = out_grads[e * HEAD_DIM : (e + 1) * HEAD_DIM]
            at = (side * half_slots + e // 2) * tall + wide
            if e % 2:
                far_ref[at : at + HEAD_DIM] = part
            else:
                near_ref[side, e // 2, wide:] = part

        def back_head(j, i):
            e = 2 * j + i
            source = source_of(sources, j, i)
            ctx_grad = mxu(att_ref[...], source[wide:], 1, 1).astype(bf16)
            query, key, value = q_ref[e], k_ref[e], v_ref[e]
            grad_key = grad_value = None
            grad_query = []
            for c in range(2):
                part = slice(c * half, (c + 1) * half)
                probs_low = probs_ref[e, :, part]
                probs = probs_low.astype(f32)
                grad_probs = mxu(value, ctx_grad[part], 1, 1)
                grad_scores = probs * (grad_probs - row_sum(grad_probs * probs))
                grad_scores = grad_scores.astype(bf16)
                value_term = mxu(probs_low, ctx_grad[part], 1, 0)
                key_term = mxu(grad_scores, query[part], 1, 0)
                grad_value = value_term if grad_value is None else grad_value + value_term
                grad_key = key_term if grad_key is None else grad_key + key_term
                grad_query.append(mxu(grad_scores, key, 0, 0))
            grad_query = jnp.concatenate(grad_query, 0)
            grads = jnp.concatenate([grad_query * scale, grad_key * scale, grad_value], 1)
            grads = grads.astype(bf16)
            sums = row_sum(grads.astype(f32))
            for n in range(2):
                part = sums[:, 2 * n * HEAD_DIM : (2 * n + 1) * HEAD_DIM]
                spread = jnp.concatenate([part] * (width // HEAD_DIM), 1)
                late_ref[n : n + 1] += jnp.where(lane_head == heads_ref[side, e], spread, 0.0)
            total_ref[...] += mxu(grads, source[:wide], 1, 0)
            rows = mxu(grads, x_ref[...], 0, 0).astype(bf16)
            if i:
                at = pl.multiple_of((side * half_slots + j) * tall, tall)
                far_ref[pl.ds(at, wide)] = rows
            else:
                near_ref[side, j, :wide] = rows

        each_head(heads_ref, side, back_head)
    send(far_ref)
    ready(layer_ref)
    for o in range(full // own):
        at = slice(o * own, (o + 1) * own)
        ref = moved[0] if o % 2 else moved[1]
        ref[o // 2, 0] = layer_ref[at]
        ref[o // 2, 1] = total_ref[at].astype(bf16)


def first_hop_kernel(near_ref, got_ref, small_ref, small_got_ref, send_ref, keep_ref, sum_ref):
    _, half_slots, tall, _ = near_ref.shape
    rows = keep_ref.shape[0]
    ready(near_ref, got_ref)

    def add(side, j, target):
        at = pl.multiple_of(j * tall, tall)
        got = got_ref[pl.ds(side * rows + at, tall)]
        target[pl.ds(at, tall)] = (near_ref[side, j].astype(f32) + got.astype(f32)).astype(bf16)

    loop(half_slots, lambda j: add(1, j, send_ref))
    total = (small_ref[...].astype(f32) + small_got_ref[...].astype(f32)).astype(bf16)
    send_ref[rows:] = total
    sum_ref[...] = total
    send(send_ref)
    loop(half_slots, lambda j: add(0, j, keep_ref))


def hop_kernel(parts, own_ref, keep_ref, small_ref, *refs):
    gots, refs = refs[: -parts - 1], refs[-parts - 1 :]
    sends, mine_ref, sum_ref = refs[: parts - 1], refs[-2], refs[-1]
    rows = keep_ref.shape[0]
    ready(keep_ref, *gots)
    small = [part.astype(f32) for part in [small_ref[...]] + [got[rows:] for got in gots]]
    while len(small) > 1:
        small = [small[i] + small[i + 1] for i in range(0, len(small), 2)]
    low = small[0].astype(bf16)
    sum_ref[...] = low if parts > 1 else small[0]
    own = own_ref[0]
    each = rows // parts
    for j in range(1, parts + 1):
        j %= parts
        at = span_of(own ^ j, each)
        total = keep_ref[at].astype(f32)
        for got in gots:
            total += got[at].astype(f32)
        if j == 0:
            mine_ref[...] = total.astype(bf16)
        else:
            sends[j - 1][:each] = total.astype(bf16)
            sends[j - 1][each:] = low
            send(sends[j - 1])


def plain_hop(parts, own, keep, small, gots):
    rows, width = keep.shape
    small = [part.astype(f32) for part in [small] + [got[rows:] for got in gots]]
    while len(small) > 1:
        small = [small[i] + small[i + 1] for i in range(0, len(small), 2)]
    sent = small[0].astype(bf16)
    kept = sent if parts > 1 else small[0]
    total = keep.astype(f32)
    for got in gots:
        total += got[:rows].astype(f32)
    total = total.astype(bf16).reshape(parts, rows // parts, width)
    sends = [jnp.concatenate([pick(total, own[0] ^ j), sent], 0) for j in range(1, parts)]
    return sends + [pick(total, own[0]), kept]


def hop(pin, parts, own, keep, small, gots):
    rows, width = keep.shape
    each = rows // parts
    if each % 16:
        return plain_hop(parts, own, keep, small, gots)
    tall = small.shape[0]
    return call(
        pin,
        functools.partial(hop_kernel, parts),
        "hop",
        [("s", own), ("v", keep), ("v", small)] + [("h", got) for got in gots],
        [("h", (each + tall, width), bf16)] * (parts - 1)
        + [("v", (each, width), bf16) if parts > 1 else ("h", (each, width), bf16)]
        + [("v", small.shape, bf16) if parts > 1 else ("h", small.shape, f32)],
    )


def program(
    slots,
    head_slots,
    pin,
    tokens,
    lengths,
    answer,
    head_order,
    neuron_order,
    w_qkv,
    b_qv,
    w_out,
    b_out,
    ln1_gain,
    ln1_bias,
    w_in,
    b_in,
    w_down,
    b_down,
    ln2_gain,
    ln2_bias,
    w_span,
    out_grad,
):
    rank = lax.axis_index("mp")
    dp_index = lax.axis_index("dp")
    ranks = lax.axis_size("mp")
    n_dp = lax.axis_size("dp")
    rows, own_len, model_dim = tokens.shape
    full = rows * own_len
    head_width = w_qkv.shape[2]
    group_heads = head_width // HEAD_DIM
    all_heads = ranks * group_heads
    ff_width = w_in.shape[1]
    half_slots = head_slots // 2
    core = rank % 2
    others = [rank ^ o for o in range(rows)]
    right = bit_of(dp_index, 1) == 1
    right_one = right.astype(i32)[None]
    groups = z_groups()
    pieces = n_dp // 2
    piece = slots // pieces
    place = jnp.stack([rank, dp_index]).astype(i32)
    lanes = 128

    tall = 4 * HEAD_DIM
    (head_rows,) = call(
        pin,
        rows_kernel,
        "rows",
        [("h", w_qkv.transpose(1, 0, 2)), ("h", w_out)],
        [("h", (group_heads * tall, model_dim), bf16)],
    )
    far_rows = swap(head_rows, "mp", 1)
    extra = jnp.concatenate(
        [
            jnp.pad(b_in[None], ((0, 0), (0, model_dim - ff_width))),
            jnp.pad(b_qv.reshape(1, -1), ((0, 0), (0, model_dim - 2 * head_width))),
            jnp.zeros((EXTRA - 2, model_dim), bf16),
        ],
        0,
    )
    unit_order = after(neuron_order[:LIVE_FF][None], head_rows)
    sent_units, unit_pick, unit_rows, unit_at = call(
        pin,
        functools.partial(units_kernel, (pieces - 1).bit_length()),
        "units",
        [("s", place), ("h", unit_order), ("h", w_in), ("h", w_down)],
        [
            ("h", (2, slots // 2, model_dim // 2), bf16),
            ("h", (slots, ff_width), bf16),
            ("h", (2, slots, model_dim), bf16),
            ("h", (ranks * ff_width // lanes, lanes), i32),
        ],
    )
    far_units = swap(sent_units, "mp", 2)
    sent_blocks = [jnp.concatenate([pick(tokens, other), extra], 0) for other in others]
    *sent_blocks, _, far_rows = lax.optimization_barrier((*sent_blocks, sent_units, far_rows))
    blocks = [swap(block, "mp", o) if o else block for o, block in enumerate(sent_blocks)]

    sent_heads, heads, my_slots = call(
        pin,
        functools.partial(choose_kernel, group_heads),
        "choose",
        [("s", place), ("s", head_order), ("h", after(head_rows, *sent_blocks)), ("h", far_rows)],
        [
            ("h", (half_slots * tall, model_dim), bf16),
            ("s", (2, head_slots), i32),
            ("s", (group_heads,), i32),
        ],
        [((all_heads,), i32)],
    )
    across = swap(after(sent_heads, *blocks), "mp", 2)
    pair_rows = swap(unit_rows, "mp", 1)
    scalars = jnp.concatenate([pick(lengths, rank)[None], pick(answer, rank), right_one])
    vectors = jnp.concatenate([b_out, ln1_gain, ln1_bias, b_down, ln2_gain, ln2_bias, b_out, b_out])
    vectors = vectors.astype(f32).reshape(8, model_dim)
    span = w_span.T
    grad_blocks = [pick(out_grad, other) for other in others]
    far_units, vectors, span, scalars, *grad_blocks = lax.optimization_barrier(
        (far_units, vectors, span, scalars, *grad_blocks, sent_heads)
    )[: 4 + rows]
    far_units = jnp.concatenate([far_units, swap(far_units, "dp", groups[0][0])], 1)
    far_side = swap(far_units, "dp", 1)
    *blocks, pair_rows = lax.optimization_barrier((*blocks, pair_rows, sent_heads))[: rows + 1]

    saved_outs = [("v", (head_slots, full, HEAD_DIM), bf16)] * 3 + [
        ("v", (head_slots, full, full), bf16),
        ("v", (head_slots * HEAD_DIM, full), bf16),
    ]
    lengths_in = [("s", place), ("s", lengths)]
    own_part, x_row, spots, head_bias, bias_in, own_heads, *own_saved = call(
        pin,
        functools.partial(attend_own_kernel, own_len, group_heads),
        "attend_own",
        lengths_in
        + [("s", heads), ("r", head_rows), ("r", far_rows)]
        + [("h", block) for block in blocks],
        [
            ("v", (full, model_dim), f32),
            ("b", (full, model_dim), bf16),
            ("h", (full, 1), i32),
            ("h", (2, head_slots, 2, HEAD_DIM), f32),
            ("h", (rows, model_dim), f32),
            ("b", (head_slots, tall, model_dim), bf16),
        ]
        + saved_outs,
        [((2 * group_heads * tall, model_dim), bf16), ((all_heads, 8, HEAD_DIM), f32)],
        sems=2,
    )
    unit_at = unit_at.reshape(ranks, ff_width)
    near_at = jnp.stack([pick(unit_at, other) for other in others])
    unit_bias = near_at[:, :, None] == jnp.arange(slots, dtype=i32)
    unit_bias = jnp.sum(jnp.where(unit_bias, bias_in[:, :ff_width, None], 0.0), 1)
    far_side, own_part = lax.optimization_barrier((far_side, own_part))
    far_pair = swap(far_units, "mp", 1)
    side_pair = swap(far_side, "mp", 1)
    across = after(across, far_side)
    other_sources = [across, swap(across, "mp", 1)]
    grad_blocks = [
        swap(after(block, across), "mp", o) if o else block for o, block in enumerate(grad_blocks)
    ]
    first_unit, first_inv, normed_low, *other_saved = call(
        pin,
        attend_kernel,
        "attend",
        lengths_in
        + [("s", heads), ("h", spots), ("h", head_bias), ("h", vectors)]
        + [("v", own_part), ("b", x_row)]
        + [("b", source) for source in other_sources],
        [
            ("v", (full, model_dim), f32),
            ("v", (full, 1), f32),
            ("v", (full, model_dim), bf16),
        ]
        + saved_outs,
        [((full, model_dim), f32)],
    )
    normed_low, side_pair, far_pair, *grad_blocks = lax.optimization_barrier(
        (normed_low, side_pair, far_pair, *grad_blocks)
    )
    far_units = [far_units, far_side, far_pair, side_pair]

    unit_side = (2, ranks // 2, slots, model_dim)
    hidden_dims = (ranks, full, slots)
    block_dims = (ranks, slots, model_dim)
    unit_far, layer_out, row_loss, loss_small, grad_second, grad_upper, *kept_units = call(
        pin,
        feed_kernel,
        "feed",
        [("s", scalars), ("v", normed_low), ("v", first_unit), ("h", vectors), ("h", unit_bias)]
        + [("b", unit_rows), ("b", pair_rows)]
        + [("b", u) for u in far_units]
        + [("h", spots), ("h", span)]
        + [("b", block) for block in grad_blocks],
        [
            ("h", unit_side, bf16),
            ("b", (full, model_dim), bf16),
            ("h", (1, 1), f32),
            ("h", (8, model_dim), f32),
            ("v", (full, model_dim), f32),
            ("v", hidden_dims, bf16),
            ("v", block_dims, bf16),
            ("v", block_dims, bf16),
            ("v", hidden_dims, bf16),
            ("v", hidden_dims, bf16),
        ],
        [
            ((full, model_dim), f32),
            ((full, model_dim), f32),
            ((full, model_dim), f32),
            ((full, 4), f32),
        ],
    )
    unit_got = swap(unit_far, "mp", 1)
    unit_near, first_small, grad_resid, grad_attended, slot_bias_grad = call(
        pin,
        feed_back_kernel,
        "feed_back",
        [("v", grad_upper), ("v", kept_units[0]), ("v", grad_second), ("v", first_unit)]
        + [("v", first_inv), ("h", vectors), ("v", normed_low)]
        + [("v", a) for a in kept_units[1:]],
        [
            ("v", unit_side, bf16),
            ("h", (8, model_dim), f32),
            ("v", (full, model_dim), f32),
            ("v", (full, model_dim), bf16),
            ("h", (ranks, slots), f32),
        ],
        [((full, model_dim), f32), (hidden_dims, bf16)],
    )

    halves = (slots, model_dim // 2)
    down_send, in_send, down_keep, in_keep = call(
        pin,
        merge_kernel,
        "merge",
        [("s", right_one), ("v", unit_near), ("h", unit_got)],
        [
            ("h", (slots, model_dim), bf16),
            ("h", (2,) + halves, bf16),
            ("b", (slots, model_dim), bf16),
            ("b", (2,) + halves, bf16),
        ],
    )
    grad_attended = after(grad_attended, down_send, in_send)
    down_got = swap(down_send, "mp", 2)
    in_got = swap(in_send, "dp", 1)

    head_far, head_near, late, rows_far, rows_near = call(
        pin,
        functools.partial(attend_back_kernel, own_len),
        "attend_back",
        [("s", heads), ("v", grad_attended), ("v", grad_resid), ("b", x_row)]
        + [("v", a) for a in own_saved]
        + [("b", own_heads)]
        + [("v", a) for a in other_saved]
        + [("l", a) for a in other_sources + [layer_out]],
        [
            ("h", (head_slots * tall, model_dim), bf16),
            ("v", (2, half_slots, tall, model_dim), bf16),
            ("h", (8, model_dim), f32),
        ]
        + [("b", (rows // 2, 2, own_len, model_dim), bf16)] * 2,
        [((full, model_dim), f32)],
    )

    head_far, down_got, in_got = lax.optimization_barrier((head_far, down_got, in_got))
    head_got = swap(head_far, "mp", 1)
    block_hit = (jnp.arange(ranks) ^ rank)[:, None] == jnp.arange(ranks)[None, :]
    place_ids = jnp.arange(pieces, dtype=i32) ^ (dp_index // 2)
    bits = len(masks_of("dp")) - 1
    place_ids = sum(
        (((place_ids >> b) & 1) << (bits - 1 - b) for b in range(bits)), jnp.zeros((pieces,), i32)
    )
    place_hit = place_ids[:, None] == jnp.arange(pieces)
    by_rank = slot_bias_grad.reshape(ranks, 1, 1, pieces, piece)
    by_rank = jnp.where(block_hit[:, :, None, None, None] & place_hit[:, :, None], by_rank, 0.0)
    by_rank = jnp.sum(by_rank, (0, 3)).reshape(-1)
    bias_count = -(-by_rank.shape[0] // model_dim)
    by_rank = jnp.pad(by_rank, (0, bias_count * model_dim - by_rank.shape[0]))
    device_hit = jnp.arange(model_dim) == dp_index * ranks + rank
    late_row = 10 + bias_count
    fill = -(-(late_row + 2) // 16) * 16 - late_row - 2
    loss_high = lax.reduce_precision(row_loss, 8, 7)
    small = jnp.concatenate(
        [
            first_small[:3],
            loss_small[:5],
            by_rank.reshape(-1, model_dim),
            jnp.where(device_hit, loss_high, 0.0),
            jnp.where(device_hit, row_loss - loss_high, 0.0),
            late[:2],
            jnp.zeros((fill, model_dim), f32),
        ],
        0,
    ).astype(bf16)
    small_got = swap(small, "mp", 1)

    kept = half_slots * tall
    small_dims = small.shape
    head_send, keep, small = call(
        pin,
        first_hop_kernel,
        "first_hop",
        [("v", head_near), ("h", head_got), ("h", small), ("h", small_got)],
        [
            ("h", (kept + small_dims[0], model_dim), bf16),
            ("v", (kept, model_dim), bf16),
            ("v", small_dims, bf16),
        ],
    )
    gots = [swap(head_send, "mp", 2)]
    down_got, in_got = lax.optimization_barrier((down_got, in_got, head_send))[:2]
    group = groups[0]
    parts = 1 << len(group)
    part = (slots // parts, model_dim // 2)
    down_send, down_keep, *in_parts = call(
        pin,
        second_merge_kernel,
        "second_merge",
        [("s", right_one), ("b", down_keep), ("h", down_got), ("b", in_keep), ("h", in_got)],
        [("h", halves, bf16), ("b", halves, bf16), ("b", (2,) + part, bf16)]
        + [("h", (2,) + part, bf16)] * (parts - 1),
    )
    down_got = swap(down_send, "dp", 1)
    in_gots = [swap(in_parts[j], "dp", partner(group, j)) for j in range(1, parts)]

    head_hops = [masks_of("dp")[:1]] + groups

    def head_hop(group, keep, small, gots):
        parts = 1 << len(group)
        own = own_bits(group, dp_index)[None].astype(i32)
        *sends, keep, small = hop(pin, parts, own, keep, small, gots)
        gots = [swap(sends[j - 1], "dp", partner(group, j)) for j in range(1, parts)]
        return keep, small, gots

    def widen(keep, group):
        got = [swap(keep, "dp", partner(group, j)) for j in range(1, 1 << len(group))]
        return jnp.concatenate([keep] + got, 0)

    unit_parts = call(
        pin,
        down_parts_kernel,
        "down_parts",
        [("b", down_keep), ("h", down_got)],
        [("h", part, bf16)] * parts,
    )
    down_gots = [swap(unit_parts[j], "dp", partner(group, j)) for j in range(1, parts)]
    gots[0] = after(gots[0], unit_parts[1])
    keep, small, gots = head_hop(head_hops[0], keep, small, gots)
    in_gots[0] = after(in_gots[0], keep)
    in_send, in_mine = call(
        pin,
        in_sum_kernel,
        "in_sum",
        [("b", in_parts[0])] + [("h", got) for got in in_gots],
        [("h", part, bf16)] * 2,
    )
    in_send, in_mine = (scatter_over(x, groups[1:]) for x in (in_send, in_mine))
    in_got = swap(in_send, "mp", 2)
    gots[0], in_got, *down_gots = lax.optimization_barrier((gots[0], in_got, *down_gots))
    down_mine = scatter_over(scatter_sum(unit_parts[0], down_gots), groups[1:])
    in_mine = scatter_sum(in_mine, [in_got])
    down_all = gather_over(down_mine, groups)
    down_side = swap(down_all, "dp", 1)
    rows_got = swap(after(rows_far, keep), "mp", 1)
    gots[0], rows_got, down_all = lax.optimization_barrier((gots[0], rows_got, down_all))
    rows_across = swap(jnp.stack([rows_near[1], rows_got[1]]), "mp", 2)
    keep, small, gots = head_hop(head_hops[1], keep, small, gots)
    for group in head_hops[2:]:
        keep, small, gots = head_hop(group, keep, small, gots)
    keep, small = hop(pin, 1, jnp.zeros((1,), i32), keep, small, gots)
    for group in reversed(groups):
        got = [swap(keep, "dp", partner(group, j)) for j in range(1, 1 << len(group))]
        keep = jnp.concatenate([keep] + got, 0)
    in_mine, rows_across, keep = lax.optimization_barrier((in_mine, rows_across, keep))
    own_rows = [rows_near[0], rows_got[0], rows_across[0], rows_across[1]]
    in_all = gather_over(in_mine, groups)
    in_side = swap(in_all, "dp", 1)
    mine = widen(keep, head_hops[0])
    w_down_grad = mxu(unit_pick, join_sides(down_all, down_side, right), 0, 0)
    w_in_grad = mxu(join_sides(in_all, in_side, right), unit_pick, 0, 0)
    own_rows = to_own(own_rows, rank)
    layer_out_own = own_rows[:, 0]
    tokens_grad = own_rows[:, 1].astype(f32)
    both = jnp.concatenate([mine, swap(mine, "mp", 1)], 0)

    head_piece = kept // n_dp
    row_ids = jnp.arange(2 * kept, dtype=i32)
    from_core, row_ids = row_ids // kept, row_ids % kept
    own_piece = own_bits([m for group in head_hops for m in group], dp_index)
    natural = ((row_ids // head_piece) ^ own_piece) * head_piece + row_ids % head_piece
    natural = natural + from_core * kept
    columns = jnp.arange(4 * head_width, dtype=i32)
    kind, rest = columns // head_width, columns % head_width
    column_slot = jnp.sum(
        jnp.where((rest // HEAD_DIM)[:, None] == jnp.arange(group_heads), my_slots, 0), 1
    )
    wanted = ((column_slot ^ core) % 2) * kept + (column_slot // 2) * tall
    wanted = wanted + kind * HEAD_DIM + rest % HEAD_DIM
    wanted = jnp.where(column_slot >= 0, wanted, -1)
    row_pick = (natural[:, None] == wanted[None, :]).astype(bf16)
    w_qkv_grad = mxu(both, row_pick[:, : 3 * head_width], 0, 0).reshape(model_dim, 3, head_width)
    w_out_grad = mxu(row_pick[:, 3 * head_width :], both, 0, 0)

    by_rank = small[8 : 8 + bias_count].reshape(-1)[: ranks * slots].reshape(ranks, slots)
    by_rank = pick(by_rank, rank).reshape(pieces, 1, piece)
    by_rank = jnp.sum(jnp.where(place_hit[:, :, None], by_rank, 0.0), 0).reshape(slots)
    b_in_grad = jnp.sum(jnp.where(unit_pick > 0, by_rank[:, None], 0.0), 0)
    losses = small[8 + bias_count] + small[9 + bias_count]
    losses = losses[: n_dp * ranks].reshape(n_dp, ranks)
    losses = lax.dynamic_index_in_dim(losses, dp_index, 0, keepdims=False)
    late = small[late_row : late_row + 2].reshape(2, ranks, head_width)
    b_qv_grad = lax.dynamic_index_in_dim(late, rank, 1, keepdims=False)
    return (
        layer_out_own,
        losses,
        tokens_grad,
        w_qkv_grad,
        b_qv_grad,
        w_out_grad,
        small[2],
        small[0],
        small[1],
        w_in_grad,
        b_in_grad,
        w_down_grad,
        small[5],
        small[3],
        small[4],
        small[6:8].T,
    )


def shards(*args):
    head_order, neuron_order, w_qkv, w_in = args[3], args[4], args[5], args[11]
    ranks = lax.axis_size("mp")
    pair_heads = 2 * w_qkv.shape[2] // HEAD_DIM
    ff_width = w_in.shape[1]
    (fits,) = call(
        False,
        functools.partial(fits_kernel, UNIT_SLOTS, HEAD_SLOTS, ff_width, pair_heads, ranks),
        "fits",
        [("s", head_order), ("h", neuron_order[:LIVE_FF][None])],
        [("s", (1,), i32)],
    )
    return lax.cond(
        fits[0] == 1,
        functools.partial(program, UNIT_SLOTS, HEAD_SLOTS, True),
        functools.partial(program, ff_width, pair_heads, False),
        *args,
    )


def solution(mesh):
    return jax.shard_map(
        shards,
        mesh=mesh,
        in_specs=(
            P("dp", "mp", None),
            P("dp"),
            P("dp", None),
            P(),
            P(),
            P(None, None, "mp"),
            P(None, "mp"),
            P("mp", None),
            P(),
            P(),
            P(),
            P(None, "mp"),
            P("mp"),
            P("mp", None),
            P(),
            P(),
            P(),
            P(),
            P("dp", "mp", None),
        ),
        out_specs=(
            P("dp", "mp", None),
            P("dp"),
            P("dp", "mp", None),
            P(None, None, "mp"),
            P(None, "mp"),
            P("mp", None),
            P(),
            P(),
            P(),
            P(None, "mp"),
            P("mp"),
            P("mp", None),
            P(),
            P(),
            P(),
            P(),
        ),
        check_vma=False,
    )
```

```python
import functools
import math

import jax
import jax.numpy as jnp
from jax import lax
from jax.experimental import pallas as pl
from jax.experimental.pallas import tpu as pltpu
from jax.sharding import PartitionSpec as P

HEAD_DIM = 64
LIVE_HEADS = 6
LIVE_FF = 1536
UNIT_SLOTS = 448
HEAD_SLOTS = 4
EXTRA = 16
MASKED = -1000000000.0
VMEM_MOST = 60 * 2**20
VMEM_SPARE = 8 * 2**20

f32 = jnp.float32
bf16 = jnp.bfloat16
i32 = jnp.int32
epsilon = 1e-12


def swap(x, axis, mask):
    return lax.ppermute(x, axis, [(i, i ^ mask) for i in range(lax.axis_size(axis))])


def masks_of(axis):
    return [1 << b for b in range((lax.axis_size(axis) - 1).bit_length())]


def bit_of(index, mask):
    return (index // mask) % 2


def pick(stacked, index):
    return lax.dynamic_index_in_dim(stacked, index, 0, keepdims=False)


def after(value, *others):
    return lax.optimization_barrier((value,) + others)[0]


def to_own(got, rank):
    for mask in masks_of("mp"):
        moved = bit_of(rank, mask) == 1
        got = [jnp.where(moved, got[r ^ mask], got[r]) for r in range(len(got))]
    return jnp.stack(got, 0)


def z_groups():
    masks = masks_of("dp")[1:]
    return [masks[i : i + 2] for i in range(0, len(masks), 2)]


def partner(group, j):
    return sum(m for i, m in enumerate(group) if (j >> (len(group) - 1 - i)) & 1)


def own_bits(group, dp_index):
    place = 0
    for mask in group:
        place = place * 2 + bit_of(dp_index, mask)
    return place


def join_sides(mine, other, right):
    return jnp.concatenate([jnp.where(right, other, mine), jnp.where(right, mine, other)], -1)


def gather_over(x, groups):
    for group in reversed(groups):
        got = [swap(x, "dp", partner(group, j)) for j in range(1, 1 << len(group))]
        x = jnp.concatenate([x] + got, -2)
    return x


def scatter_sum(x, got):
    x = x.astype(f32)
    for term in got:
        x = x + term.astype(f32)
    return x.astype(bf16)


def scatter_over(x, groups):
    for group in groups:
        n = 1 << len(group)
        rows = x.shape[-2] // n
        parts = [x[..., j * rows : (j + 1) * rows, :] for j in range(n)]
        x = scatter_sum(parts[0], [swap(parts[j], "dp", partner(group, j)) for j in range(1, n)])
    return x


class Incoming:
    def __init__(self, source, held, sem, late):
        self.copy, self.held, self.waiting = pltpu.make_async_copy(source, held, sem), held, True
        self.shape, self.started = held.shape, False
        if not late:
            self.start()

    def start(self):
        if not self.started:
            self.started = True
            self.copy.start()

    def ready(self):
        if self.waiting:
            self.start()
            self.copy.wait()
            self.waiting = False
        return self.held

    def __getitem__(self, index):
        return self.ready()[index]

    @property
    def at(self):
        return self.ready().at


class Outgoing:
    def __init__(self, held, target, sem):
        self.held, self.target, self.sem, self.sent = held, target, sem, False
        self.shape, self.at = held.shape, held.at

    def __getitem__(self, index):
        return self.held[index]

    def __setitem__(self, index, value):
        self.held[index] = value

    def send(self, *index):
        self.sent = True
        if index:
            pltpu.make_async_copy(self.held.at[index], self.target.at[index], self.sem).start()
        else:
            pltpu.make_async_copy(self.held, self.target, self.sem).start()

    def wait(self):
        if not self.sent:
            self.send()
        pltpu.make_async_copy(self.held, self.target, self.sem).wait()


def start(*refs):
    for ref in refs:
        if isinstance(ref, Incoming):
            ref.start()


def ready(*refs):
    for ref in refs:
        if isinstance(ref, Incoming):
            ref.ready()


def send(*refs):
    for ref in refs:
        if isinstance(ref, Outgoing):
            ref.send()


def held(item):
    dims, size = item.shape, jnp.dtype(item.dtype).itemsize
    if len(dims) < 2:
        return 4096
    tall = 32 // size
    return -(-dims[-1] // 128) * 128 * (-(-dims[-2] // tall) * tall) * size * math.prod(dims[:-2])


def shape(dims, kind):
    return jax.ShapeDtypeStruct(dims, kind)


PLACES = {"v": pltpu.VMEM, "b": pltpu.HBM, "l": pltpu.HBM, "r": pltpu.HBM}


def call(pin, kernel, name, ins, outs, scratch=(), sems=0, flops=1e6, moved=5e6):
    in_kinds = [k if k != "v" or pin else "h" for k, _ in ins]
    out_kinds = [k if k != "v" or pin else "h" for k, _, _ in outs]
    args = [
        pltpu.with_memory_space_constraint(a, PLACES[k]) if k in PLACES else a
        for k, (_, a) in zip(in_kinds, ins)
    ]
    out_shape = [
        PLACES[k](d, t) if k in PLACES else shape(d, t) for k, (_, d, t) in zip(out_kinds, outs)
    ]
    buffers = [shape(a.shape, a.dtype) for k, a in zip(in_kinds, args) if k in "hbl"]
    buffers += [shape(d, t) for k, (_, d, t) in zip(out_kinds, outs) if k in "hb"]
    scratch = [shape(d, t) for d, t in scratch]
    count, outs_count = len(in_kinds), len(out_kinds)

    def whole(*refs):
        given, results, refs = refs[:count], refs[count : count + outs_count], refs[count + outs_count :]
        bufs, refs = iter(refs[: len(buffers)]), refs[len(buffers) :]
        in_sem, out_sem = refs[:2]
        given = [
            Incoming(ref, next(bufs), in_sem.at[i], k == "l") if k in "hbl" else ref
            for i, (k, ref) in enumerate(zip(in_kinds, given))
        ]
        results = [
            Outgoing(next(bufs), ref, out_sem.at[i]) if k in "hb" else ref
            for i, (k, ref) in enumerate(zip(out_kinds, results))
        ]
        kernel(*given, *results, *refs[2:])
        ready(*given)
        for ref in results:
            if isinstance(ref, Outgoing):
                ref.wait()

    spaces = {"s": pltpu.SMEM, "v": pltpu.VMEM, "h": pl.ANY, "b": pltpu.HBM, "l": pltpu.HBM, "r": pltpu.HBM}
    limit = sum(held(b) for b in buffers + scratch) + VMEM_SPARE
    return pl.pallas_call(
        whole,
        name=name,
        out_shape=out_shape,
        in_specs=[pl.BlockSpec(memory_space=spaces[k]) for k in in_kinds],
        out_specs=[pl.BlockSpec(memory_space=spaces[k]) for k in out_kinds],
        scratch_shapes=[pltpu.VMEM(b.shape, b.dtype) for b in buffers]
        + [pltpu.SemaphoreType.DMA((count,)), pltpu.SemaphoreType.DMA((outs_count,))]
        + [pltpu.SMEM(s.shape, s.dtype) if s.dtype == i32 else pltpu.VMEM(s.shape, s.dtype) for s in scratch]
        + ([pltpu.SemaphoreType.DMA((sems,))] if sems else []),
        compiler_params=pltpu.CompilerParams(vmem_limit_bytes=min(VMEM_MOST, int(limit))),
        cost_estimate=pl.CostEstimate(flops=int(flops), bytes_accessed=int(moved), transcendentals=0),
    )(*args)


def row_sum(v):
    return jnp.sum(v, 0, keepdims=True)


def lane_mean(v):
    return jnp.mean(v, -1, keepdims=True)


def mxu(a, b, a_dim, b_dim):
    return lax.dot_general(a, b, (((a_dim,), (b_dim,)), ((), ())), preferred_element_type=f32)


def loop(count, body):
    def step(i, carry):
        body(i)
        return carry

    lax.fori_loop(0, count, step, 0)


def span_of(i, size):
    return pl.ds(i * size if isinstance(i, int) else pl.multiple_of(i * size, size), size)


def by_rows(full, size, body):
    loop(full // size, lambda i: body(span_of(i, size)))


def fits_kernel(unit_slots, head_slots, ff_width, pair_heads, ranks, heads_ref, order_ref, fits_ref):
    order = order_ref[...]
    most = jnp.zeros((1, 1), f32)
    for r in range(ranks):
        mine = (order >= r * ff_width) & (order < (r + 1) * ff_width)
        most = jnp.maximum(most, jnp.sum(jnp.where(mine, 1.0, 0.0), keepdims=True))
    fine = jnp.where(most[0, 0] <= unit_slots, 1, 0)
    for pair in range(ranks // 2):
        count = 0
        for k in range(LIVE_HEADS):
            count += jnp.where(heads_ref[k] // pair_heads == pair, 1, 0)
        fine *= jnp.where(count <= head_slots, 1, 0)
    fits_ref[0] = fine


def rows_kernel(qkv_ref, out_ref, rows_ref):
    square = (HEAD_DIM, HEAD_DIM)
    diagonal = lax.broadcasted_iota(i32, square, 0) == lax.broadcasted_iota(i32, square, 1)
    diagonal = jnp.where(diagonal, 1.0, 0.0).astype(bf16)
    for g in range(out_ref.shape[0] // HEAD_DIM):
        at = slice(g * HEAD_DIM, (g + 1) * HEAD_DIM)
        parts = [mxu(diagonal, qkv_ref[c, :, at], 1, 1).astype(bf16) for c in range(3)]
        rows_ref[g * 4 * HEAD_DIM : (g + 1) * 4 * HEAD_DIM] = jnp.concatenate(parts + [out_ref[at]], 0)


def choose_kernel(group, place_ref, order_ref, rows_ref, far_ref, send_ref, heads_ref, slots_ref, table_ref):
    tall = 4 * HEAD_DIM
    rank = place_ref[0]
    core, pair = rank % 2, rank // 2
    counts = {}
    for head in range(order_ref.shape[0]):
        count = counts.get(head // (2 * group), 0)
        live = 0
        for k in range(LIVE_HEADS):
            live += jnp.where(order_ref[k] == head, 1, 0)
        table_ref[head] = jnp.where(live > 0, count, -1)
        counts[head // (2 * group)] = count + live
    half = heads_ref.shape[1] // 2
    for side in range(2):
        for e in range(2 * half):
            heads_ref[side, e] = -1
    for k in range(LIVE_HEADS):
        head = order_ref[k]
        side = jnp.where(head // (2 * group) != pair, 1, 0)
        heads_ref[side, table_ref[head] ^ core] = head
    for g in range(group):
        slots_ref[g] = table_ref[rank * group + g]
    ready(rows_ref, far_ref)
    for j in range(half):
        head = jnp.maximum(heads_ref[0, 2 * j], 0)
        at = pl.ds(pl.multiple_of((head % group) * tall, tall), tall)
        mine = (head // group == rank) | (heads_ref[0, 2 * j] < 0)
        target = slice(j * tall, (j + 1) * tall)

        @pl.when(mine)
        def own():
            send_ref[target] = rows_ref[at]

        @pl.when(jnp.logical_not(mine))
        def far():
            send_ref[target] = far_ref[at]


def units_kernel(zbits, place_ref, order_ref, in_ref, down_ref, *refs):
    sides_ref, pick_ref, rows_ref, at_ref = refs
    slots, width = pick_ref.shape
    side = sides_ref.shape[2]
    piece = slots >> zbits
    rank, dp_index = place_ref[0], place_ref[1]
    lanes = at_ref.shape[1]
    per = width // lanes
    order = order_ref[...]

    def hot(dims, index):
        return jnp.where(lax.broadcasted_iota(i32, dims, 0) == index, 1.0, 0.0).astype(bf16)

    count = order.shape[1]
    row_hot = hot((at_ref.shape[0], count), order // lanes)
    lane_hot = hot((lanes, count), order % lanes)
    live = mxu(row_hot, lane_hot, 1, 1)
    square = (lanes, lanes)
    first, second = (lax.broadcasted_iota(i32, square, d) for d in range(2))
    upto = jnp.where(first <= second, 1.0, 0.0).astype(bf16)
    within = mxu(live.astype(bf16), upto, 1, 0)
    totals = mxu(live.astype(bf16), jnp.ones(square, bf16), 1, 0)
    square = (at_ref.shape[0], at_ref.shape[0])
    first, second = (lax.broadcasted_iota(i32, square, d) for d in range(2))
    earlier = (second < first) & (second // per == first // per)
    offsets = mxu(jnp.where(earlier, 1.0, 0.0).astype(bf16), totals.astype(bf16), 1, 0)
    slot = (offsets + within).astype(i32) - 1
    index = jnp.zeros(slot.shape, i32)
    for p in range(1, slots // piece):
        index += jnp.where(slot >= p * piece, 1, 0)
    inside = slot - index * piece
    index = index ^ (dp_index // 2)
    place = jnp.zeros(slot.shape, i32)
    for b in range(zbits):
        place = place * 2 + ((index >> b) & 1)
    at_ref[...] = jnp.where(live > 0.5, place * piece + inside, -1)
    ids = lax.broadcasted_iota(i32, (slots, lanes), 0)
    for c in range(per):
        row = at_ref[pl.ds(rank * per + c, 1)]
        pick_ref[:, c * lanes : (c + 1) * lanes] = jnp.where(ids == row, 1.0, 0.0).astype(bf16)
    right = dp_index % 2 == 1
    rows_in = mxu(pick_ref[...], in_ref[...], 1, 1).astype(bf16)
    part = sides_ref.shape[1]
    sides_ref[0] = jnp.where(right, rows_in[:part, side:], rows_in[:part, :side])
    rows_ref[0] = rows_in
    rows_down = mxu(pick_ref[...], down_ref[...], 1, 0).astype(bf16)
    sides_ref[1] = jnp.where(right, rows_down[:part, side:], rows_down[:part, :side])
    send(sides_ref)
    rows_ref[1] = rows_down


def source_of(sources, j, i):
    if len(sources) == 1:
        return sources[0].at[2 * j + i]
    return sources[i].at[span_of(j, 4 * HEAD_DIM)]


def each_head(heads_ref, side, body):
    def two(j):
        for i in range(2):
            pl.when(heads_ref[side, 2 * j + i] >= 0)(functools.partial(body, j, i))

    loop(heads_ref.shape[1] // 2, two)


def out_rows(sources, slots):
    parts = [source_of(sources, e // 2, e % 2)[3 * HEAD_DIM :] for e in range(slots)]
    return jnp.concatenate(parts, 0)


def attend_heads(side, x_ref, heads_ref, valid, bias_ref, sources, outs):
    q_ref, k_ref, v_ref, probs_ref, ctx_ref = outs
    wide = 3 * HEAD_DIM
    half = x_ref.shape[0] // 2
    ctx_ref[...] = jnp.zeros(ctx_ref.shape, bf16)

    def attend_head(j, i):
        e = 2 * j + i
        bias = bias_ref[side, e]
        both = mxu(x_ref[...], source_of(sources, j, i)[:wide], 1, 1)
        query = (both[:, :HEAD_DIM] + bias[0:1]).astype(bf16)
        key = both[:, HEAD_DIM : 2 * HEAD_DIM].astype(bf16)
        value = (both[:, 2 * HEAD_DIM :] + bias[1:2]).astype(bf16)
        q_ref[e], k_ref[e], v_ref[e] = query, key, value
        for c in range(2):
            part = slice(c * half, (c + 1) * half)
            scores = mxu(key, query[part], 1, 1) * HEAD_DIM ** (-0.5)
            scores = jnp.where(valid, scores, MASKED)
            exp_scores = jnp.exp(scores - jnp.max(scores, 0, keepdims=True))
            probs = (exp_scores * (1.0 / row_sum(exp_scores))).astype(bf16)
            probs_ref[e, :, part] = probs
            ctx_ref[span_of(e, HEAD_DIM), part] = mxu(value, probs, 0, 0).astype(bf16)

    each_head(heads_ref, side, attend_head)
    send(*outs)
    return mxu(ctx_ref[...], out_rows(sources, heads_ref.shape[1]), 0, 0)


def attend_own_kernel(own, group, place_ref, lengths_ref, heads_ref, rows_ref, far_ref, *refs):
    blocks, refs = refs[:-14], refs[-14:]
    part_ref, x_ref, spots_ref, bias_ref, unit_bias_ref, heads_out_ref = refs[:6]
    outs, (held_ref, table_ref, sem) = refs[6:11], refs[11:]
    rank = place_ref[0]
    tall = 4 * HEAD_DIM
    count = group * tall
    copies = [
        pltpu.make_async_copy(ref, held_ref.at[pl.ds(n * count, count)], sem.at[n])
        for n, ref in enumerate((rows_ref, far_ref))
    ]
    for copy in copies:
        copy.start()
    for o, block in enumerate(blocks):
        x_ref[o * own : (o + 1) * own] = block[:own]
        ids = lax.broadcasted_iota(i32, (own, 1), 0)
        spots_ref[o * own : (o + 1) * own] = ids + (rank ^ o) * own
        extra = block[own : own + EXTRA].astype(f32)
        unit_bias_ref[o : o + 1] = extra[0:1]
        for g in range(group):
            for n in range(2):
                at = (n * group + g) * HEAD_DIM
                table_ref[o * group + g, n : n + 1] = extra[1:2, at : at + HEAD_DIM]
    for side in range(2):
        for e in range(heads_ref.shape[1]):
            head = jnp.maximum(heads_ref[side, e], 0)
            bias_ref[side, e] = table_ref[((head // group) ^ rank) * group + head % group][:2]
    for copy in copies:
        copy.wait()
    for e in range(heads_ref.shape[1]):
        head = jnp.maximum(heads_ref[0, e], 0)
        at = jnp.where(head // group == rank, 0, count) + (head % group) * tall
        heads_out_ref[e] = held_ref[pl.ds(pl.multiple_of(at, tall), tall)]
    valid = spots_ref[...] < lengths_ref[rank]
    part_ref[...] = attend_heads(0, x_ref, heads_ref, valid, bias_ref, [heads_out_ref], outs)


def attend_kernel(place_ref, lengths_ref, heads_ref, spots_ref, bias_ref, vec_ref, part_ref, x_ref, *refs):
    sources, refs = refs[:2], refs[2:]
    unit_ref, inv_ref, low_ref, sum_ref = refs[:3] + refs[-1:]
    valid = spots_ref[...] < lengths_ref[place_ref[0]]
    ready(bias_ref, vec_ref, part_ref, x_ref, *sources)
    sum_ref[...] = attend_heads(1, x_ref, heads_ref, valid, bias_ref, sources, refs[3:-1])

    def norm(rows):
        first_sum = x_ref[rows].astype(f32) + (part_ref[rows] + sum_ref[rows]) + vec_ref[0:1]
        centered = first_sum - lane_mean(first_sum)
        inv = lax.rsqrt(lane_mean(centered * centered) + epsilon)
        unit = centered * inv
        unit_ref[rows] = unit
        inv_ref[rows] = inv
        low_ref[rows] = (unit * vec_ref[1:2] + vec_ref[2:3]).astype(bf16)

    by_rows(sum_ref.shape[0], 128, norm)


def join_block(target, mine, other, kind, right):
    half = mine.shape[-1]
    one, two = mine[kind], other[kind]
    target[:, :half] = jnp.where(right, two, one)
    target[:, half:] = jnp.where(right, one, two)


def feed_kernel(scalar_ref, low_ref, unit_ref, vec_ref, bias_ref, *refs):
    near_units, sides, refs = refs[:2], refs[2:6], refs[6:]
    spots_ref, span_ref, refs = refs[0], refs[1], refs[2:]
    grads, refs = refs[:-14], refs[-14:]
    far_ref, out_ref, loss_ref, small_ref, second_ref, upper_ref, ins_ref = refs[:7]
    downs_ref, hidden_ref, slope_ref, total_ref, layer_ref, two_ref, logit_ref = refs[7:]
    full = low_ref.shape[0]
    half = full // 2
    right = scalar_ref[3] == 1
    ready(low_ref, unit_ref, vec_ref, bias_ref, *near_units)

    def first(rows):
        total_ref[rows] = unit_ref[rows] * vec_ref[1:2] + vec_ref[2:3] + vec_ref[3:4]

    by_rows(full, 128, first)
    for o in range(2):
        ins_ref[o] = near_units[o][0]
        downs_ref[o] = near_units[o][1]

    def forward(o):
        for r in range(2):
            rows = slice(r * half, (r + 1) * half)
            upper = mxu(low_ref[rows], ins_ref[o], 1, 1) + bias_ref[pl.ds(o, 1)]
            cumulative = 0.5 * (1.0 + lax.erf(upper * 0.7071067811865476))
            density = jnp.exp(-0.5 * upper * upper) * 0.3989422804014327
            hidden = (upper * cumulative).astype(bf16)
            hidden_ref[o, rows] = hidden
            slope_ref[o, rows] = (cumulative + upper * density).astype(bf16)
            total_ref[rows] += mxu(hidden, downs_ref[o], 1, 0)

    loop(2, forward)
    ready(*sides)
    for o in range(2):
        join_block(ins_ref.at[2 + o], sides[2 * o], sides[2 * o + 1], 0, right)
        join_block(downs_ref.at[2 + o], sides[2 * o], sides[2 * o + 1], 1, right)
    loop(2, lambda o: forward(o + 2))
    ready(spots_ref, span_ref, *grads)

    def norm(rows):
        second_sum = total_ref[rows]
        centered = second_sum - lane_mean(second_sum)
        inv = lax.rsqrt(lane_mean(centered * centered) + epsilon)
        unit = centered * inv
        layer_out = unit * vec_ref[4:5] + vec_ref[5:6]
        two_ref[rows] = unit
        layer_ref[rows] = layer_out
        out_ref[rows] = layer_out.astype(bf16)
        logit_ref[rows, 2:3] = inv
        for c in range(2):
            logit_ref[rows, c : c + 1] = jnp.sum(layer_out * span_ref[c : c + 1], -1, keepdims=True)

    by_rows(full, 128, norm)
    small_ref[...] = jnp.zeros(small_ref.shape, f32)
    spots = spots_ref[...]
    valid = spots < scalar_ref[0]
    loss = jnp.zeros((1, 1), f32)
    for c in range(2):
        logits = logit_ref[:, c : c + 1]
        masked = jnp.where(valid, logits, MASKED)
        top = jnp.max(masked, 0, keepdims=True)
        exp_logits = jnp.exp(masked - top)
        total = row_sum(exp_logits)
        chosen = spots == scalar_ref[1 + c]
        loss += top + jnp.log(total) - row_sum(jnp.where(chosen, logits, 0.0))
        logit_ref[:, c : c + 1] = exp_logits / total - jnp.where(chosen, 1.0, 0.0)
    loss_ref[...] = loss
    own = full // len(grads)
    for o, grad in enumerate(grads):
        rows = slice(o * own, (o + 1) * own)
        unit, layer_out, inv = two_ref[rows], layer_ref[rows], logit_ref[rows, 2:3]
        grad_out = grad[...].astype(f32)
        for c in range(2):
            grad_logits = logit_ref[rows, c : c + 1]
            grad_out += grad_logits * span_ref[c : c + 1]
            small_ref[3 + c : 4 + c] += row_sum(layer_out * grad_logits)
        small_ref[0:1] += row_sum(grad_out * unit)
        small_ref[1:2] += row_sum(grad_out)
        grad_normed = grad_out * vec_ref[4:5]
        second = inv * (
            grad_normed - lane_mean(grad_normed) - unit * lane_mean(grad_normed * unit)
        )
        second_ref[rows] = second
        small_ref[2:3] += row_sum(second)

    branch_grad = second_ref[...].astype(bf16)
    args = (branch_grad, low_ref, downs_ref, hidden_ref, slope_ref, upper_ref)
    loop(2, lambda j: back_block(2 * j + 1, *args, far_ref.at[:, j]))


def back_block(o, branch_grad, low_ref, downs_ref, hidden_ref, slope_ref, upper_ref, target):
    hidden_grad = mxu(branch_grad, downs_ref[o], 1, 1)
    upper = (hidden_grad * slope_ref[o].astype(f32)).astype(bf16)
    upper_ref[o] = upper
    target[1] = mxu(hidden_ref[o], branch_grad, 0, 0).astype(bf16)
    target[0] = mxu(upper, low_ref[...], 0, 0).astype(bf16)


def feed_back_kernel(upper_ref, ins_ref, second_ref, unit_ref, inv_ref, vec_ref, *refs):
    low_ref, downs_ref, hidden_ref, slope_ref = refs[:4]
    near_ref, small_ref, resid_ref, att_ref, bias_ref, first_ref, near_upper_ref = refs[4:]
    ready(upper_ref, ins_ref, second_ref, low_ref, downs_ref, hidden_ref, slope_ref)
    first_ref[...] = second_ref[...]

    def back(j):
        branch_grad = second_ref[...].astype(bf16)
        args = (branch_grad, low_ref, downs_ref, hidden_ref, slope_ref, near_upper_ref)
        back_block(2 * j, *args, near_ref.at[:, j])
        for upper, o in ((near_upper_ref[2 * j], 2 * j), (upper_ref[2 * j + 1], 2 * j + 1)):
            first_ref[...] += mxu(upper, ins_ref[o], 1, 0)
            bias_ref[pl.ds(o, 1)] = row_sum(upper.astype(f32))

    loop(upper_ref.shape[0] // 2, back)
    ready(unit_ref, inv_ref, vec_ref)
    small_ref[...] = jnp.zeros(small_ref.shape, f32)

    def norm(rows):
        first, unit = first_ref[rows], unit_ref[rows]
        grad_normed = first * vec_ref[1:2]
        resid = inv_ref[rows] * (
            grad_normed - lane_mean(grad_normed) - unit * lane_mean(grad_normed * unit)
        )
        resid_ref[rows] = resid
        att_ref[rows] = resid.astype(bf16)
        small_ref[0:1] += row_sum(first * unit)
        small_ref[1:2] += row_sum(first)
        small_ref[2:3] += row_sum(resid)

    by_rows(first_ref.shape[0], 128, norm)


def merge_kernel(right_ref, near_ref, got_ref, *refs):
    down_send_ref, in_send_ref, down_keep_ref, in_keep_ref = refs
    right = right_ref[0] == 1
    half = in_send_ref.shape[-1]
    ready(near_ref, got_ref)

    def total(kind, o, rows):
        return (near_ref[kind, o, rows].astype(f32) + got_ref[kind, o, rows].astype(f32)).astype(bf16)

    def merge(rows):
        down_send_ref[rows] = total(1, 1, rows)
        down_keep_ref[rows] = total(1, 0, rows)
        for o in range(2):
            block = total(0, o, rows)
            in_send_ref[o, rows] = jnp.where(right, block[:, :half], block[:, half:])
            in_keep_ref[o, rows] = jnp.where(right, block[:, half:], block[:, :half])

    by_rows(down_send_ref.shape[0], down_send_ref.shape[0] // 4, merge)


def second_merge_kernel(right_ref, down_ref, down_got_ref, in_ref, in_got_ref, *refs):
    down_send_ref, down_keep_ref, parts = refs[0], refs[1], refs[2:]
    right = right_ref[0] == 1
    half = down_send_ref.shape[-1]
    each = parts[0].shape[1]
    for j in range(1, len(parts) + 1):
        j %= len(parts)
        rows = slice(j * each, (j + 1) * each)
        for o in range(2):
            parts[j][o] = (in_ref[o, rows].astype(f32) + in_got_ref[o, rows].astype(f32)).astype(bf16)
        send(parts[j])
        block = (down_ref[rows].astype(f32) + down_got_ref[rows].astype(f32)).astype(bf16)
        down_send_ref[rows] = jnp.where(right, block[:, :half], block[:, half:])
        down_keep_ref[rows] = jnp.where(right, block[:, half:], block[:, :half])


def down_parts_kernel(down_ref, got_ref, *parts):
    each = parts[0].shape[0]
    ready(down_ref, got_ref)
    for j in range(1, len(parts) + 1):
        j %= len(parts)
        rows = slice(j * each, (j + 1) * each)
        parts[j][...] = (down_ref[rows].astype(f32) + got_ref[rows].astype(f32)).astype(bf16)
        send(parts[j])


def in_sum_kernel(in_ref, *refs):
    gots, outs = refs[:-2], refs[-2:]
    for o in (1, 0):
        total = in_ref[o].astype(f32)
        for got in gots:
            total += got[o].astype(f32)
        outs[1 - o][...] = total.astype(bf16)
        send(outs[1 - o])


def attend_back_kernel(own, heads_ref, att_ref, resid_ref, x_ref, *refs):
    sides = ((refs[:5], refs[5:6]), (refs[6:11], refs[11:13]))
    layer_ref, far_ref, near_ref, late_ref = refs[13:17]
    moved, total_ref = refs[17:-1], refs[-1]
    wide = 3 * HEAD_DIM
    scale = HEAD_DIM ** (-0.5)
    _, half_slots, tall, width = near_ref.shape
    lane_head = lax.broadcasted_iota(i32, (1, width), 1) // HEAD_DIM
    slots = heads_ref.shape[1]
    late_ref[...] = jnp.zeros(late_ref.shape, f32)
    far_ref[...] = jnp.zeros(far_ref.shape, bf16)
    near_ref[...] = jnp.zeros(near_ref.shape, bf16)
    full = x_ref.shape[0]
    half = full // 2
    ready(att_ref, resid_ref, x_ref)
    total_ref[...] = resid_ref[...]
    for side, (saved, sources) in enumerate(sides):
        q_ref, k_ref, v_ref, probs_ref, ctx_ref = saved
        ready(*saved, *sources)
        if side == 0:
            start(*sides[1][0], *sides[1][1], layer_ref)
        out_grads = mxu(ctx_ref[...], att_ref[...], 1, 0).astype(bf16)
        for e in range(slots):
            part = out_grads[e * HEAD_DIM : (e + 1) * HEAD_DIM]
            at = (side * half_slots + e // 2) * tall + wide
            if e % 2:
                far_ref[at : at + HEAD_DIM] = part
            else:
                near_ref[side, e // 2, wide:] = part

        def back_head(j, i):
            e = 2 * j + i
            source = source_of(sources, j, i)
            ctx_grad = mxu(att_ref[...], source[wide:], 1, 1).astype(bf16)
            query, key, value = q_ref[e], k_ref[e], v_ref[e]
            grad_key = grad_value = None
            grad_query = []
            for c in range(2):
                part = slice(c * half, (c + 1) * half)
                probs_low = probs_ref[e, :, part]
                probs = probs_low.astype(f32)
                grad_probs = mxu(value, ctx_grad[part], 1, 1)
                grad_scores = probs * (grad_probs - row_sum(grad_probs * probs))
                grad_scores = grad_scores.astype(bf16)
                value_term = mxu(probs_low, ctx_grad[part], 1, 0)
                key_term = mxu(grad_scores, query[part], 1, 0)
                grad_value = value_term if grad_value is None else grad_value + value_term
                grad_key = key_term if grad_key is None else grad_key + key_term
                grad_query.append(mxu(grad_scores, key, 0, 0))
            grad_query = jnp.concatenate(grad_query, 0)
            grads = jnp.concatenate([grad_query * scale, grad_key * scale, grad_value], 1)
            grads = grads.astype(bf16)
            sums = row_sum(grads.astype(f32))
            for n in range(2):
                part = sums[:, 2 * n * HEAD_DIM : (2 * n + 1) * HEAD_DIM]
                spread = jnp.concatenate([part] * (width // HEAD_DIM), 1)
                late_ref[n : n + 1] += jnp.where(lane_head == heads_ref[side, e], spread, 0.0)
            total_ref[...] += mxu(grads, source[:wide], 1, 0)
            rows = mxu(grads, x_ref[...], 0, 0).astype(bf16)
            if i:
                at = pl.multiple_of((side * half_slots + j) * tall, tall)
                far_ref[pl.ds(at, wide)] = rows
            else:
                near_ref[side, j, :wide] = rows

        each_head(heads_ref, side, back_head)
    send(far_ref)
    ready(layer_ref)
    for o in range(full // own):
        at = slice(o * own, (o + 1) * own)
        ref = moved[0] if o % 2 else moved[1]
        ref[o // 2, 0] = layer_ref[at]
        ref[o // 2, 1] = total_ref[at].astype(bf16)


def first_hop_kernel(near_ref, got_ref, small_ref, small_got_ref, send_ref, keep_ref, sum_ref):
    _, half_slots, tall, _ = near_ref.shape
    rows = keep_ref.shape[0]
    ready(near_ref, got_ref)

    def add(side, j, target):
        at = pl.multiple_of(j * tall, tall)
        got = got_ref[pl.ds(side * rows + at, tall)]
        target[pl.ds(at, tall)] = (near_ref[side, j].astype(f32) + got.astype(f32)).astype(bf16)

    loop(half_slots, lambda j: add(1, j, send_ref))
    total = (small_ref[...].astype(f32) + small_got_ref[...].astype(f32)).astype(bf16)
    send_ref[rows:] = total
    sum_ref[...] = total
    send(send_ref)
    loop(half_slots, lambda j: add(0, j, keep_ref))


def hop_kernel(parts, own_ref, keep_ref, small_ref, *refs):
    gots, refs = refs[: -parts - 1], refs[-parts - 1 :]
    sends, mine_ref, sum_ref = refs[: parts - 1], refs[-2], refs[-1]
    rows = keep_ref.shape[0]
    ready(keep_ref, *gots)
    small = [part.astype(f32) for part in [small_ref[...]] + [got[rows:] for got in gots]]
    while len(small) > 1:
        small = [small[i] + small[i + 1] for i in range(0, len(small), 2)]
    low = small[0].astype(bf16)
    sum_ref[...] = low if parts > 1 else small[0]
    own = own_ref[0]
    each = rows // parts
    for j in range(1, parts + 1):
        j %= parts
        at = span_of(own ^ j, each)
        total = keep_ref[at].astype(f32)
        for got in gots:
            total += got[at].astype(f32)
        if j == 0:
            mine_ref[...] = total.astype(bf16)
        else:
            sends[j - 1][:each] = total.astype(bf16)
            sends[j - 1][each:] = low
            send(sends[j - 1])


def plain_hop(parts, own, keep, small, gots):
    rows, width = keep.shape
    small = [part.astype(f32) for part in [small] + [got[rows:] for got in gots]]
    while len(small) > 1:
        small = [small[i] + small[i + 1] for i in range(0, len(small), 2)]
    sent = small[0].astype(bf16)
    kept = sent if parts > 1 else small[0]
    total = keep.astype(f32)
    for got in gots:
        total += got[:rows].astype(f32)
    total = total.astype(bf16).reshape(parts, rows // parts, width)
    sends = [jnp.concatenate([pick(total, own[0] ^ j), sent], 0) for j in range(1, parts)]
    return sends + [pick(total, own[0]), kept]


def hop(pin, parts, own, keep, small, gots):
    rows, width = keep.shape
    each = rows // parts
    if each % 16:
        return plain_hop(parts, own, keep, small, gots)
    tall = small.shape[0]
    return call(
        pin,
        functools.partial(hop_kernel, parts),
        "hop",
        [("s", own), ("v", keep), ("v", small)] + [("h", got) for got in gots],
        [("h", (each + tall, width), bf16)] * (parts - 1)
        + [("v", (each, width), bf16) if parts > 1 else ("h", (each, width), bf16)]
        + [("v", small.shape, bf16) if parts > 1 else ("h", small.shape, f32)],
    )


def program(
    slots,
    head_slots,
    pin,
    tokens,
    lengths,
    answer,
    head_order,
    neuron_order,
    w_qkv,
    b_qv,
    w_out,
    b_out,
    ln1_gain,
    ln1_bias,
    w_in,
    b_in,
    w_down,
    b_down,
    ln2_gain,
    ln2_bias,
    w_span,
    out_grad,
):
    rank = lax.axis_index("mp")
    dp_index = lax.axis_index("dp")
    ranks = lax.axis_size("mp")
    n_dp = lax.axis_size("dp")
    rows, own_len, model_dim = tokens.shape
    full = rows * own_len
    head_width = w_qkv.shape[2]
    group_heads = head_width // HEAD_DIM
    all_heads = ranks * group_heads
    ff_width = w_in.shape[1]
    half_slots = head_slots // 2
    core = rank % 2
    others = [rank ^ o for o in range(rows)]
    right = bit_of(dp_index, 1) == 1
    right_one = right.astype(i32)[None]
    groups = z_groups()
    pieces = n_dp // 2
    piece = slots // pieces
    place = jnp.stack([rank, dp_index]).astype(i32)
    lanes = 128

    tall = 4 * HEAD_DIM
    (head_rows,) = call(
        pin,
        rows_kernel,
        "rows",
        [("h", w_qkv.transpose(1, 0, 2)), ("h", w_out)],
        [("h", (group_heads * tall, model_dim), bf16)],
    )
    far_rows = swap(head_rows, "mp", 1)
    extra = jnp.concatenate(
        [
            jnp.pad(b_in[None], ((0, 0), (0, model_dim - ff_width))),
            jnp.pad(b_qv.reshape(1, -1), ((0, 0), (0, model_dim - 2 * head_width))),
            jnp.zeros((EXTRA - 2, model_dim), bf16),
        ],
        0,
    )
    unit_order = after(neuron_order[:LIVE_FF][None], head_rows)
    sent_units, unit_pick, unit_rows, unit_at = call(
        pin,
        functools.partial(units_kernel, (pieces - 1).bit_length()),
        "units",
        [("s", place), ("h", unit_order), ("h", w_in), ("h", w_down)],
        [
            ("h", (2, slots // 2, model_dim // 2), bf16),
            ("h", (slots, ff_width), bf16),
            ("h", (2, slots, model_dim), bf16),
            ("h", (ranks * ff_width // lanes, lanes), i32),
        ],
    )
    far_units = swap(sent_units, "mp", 2)
    sent_blocks = [jnp.concatenate([pick(tokens, other), extra], 0) for other in others]
    *sent_blocks, _, far_rows = lax.optimization_barrier((*sent_blocks, sent_units, far_rows))
    blocks = [swap(block, "mp", o) if o else block for o, block in enumerate(sent_blocks)]

    sent_heads, heads, my_slots = call(
        pin,
        functools.partial(choose_kernel, group_heads),
        "choose",
        [("s", place), ("s", head_order), ("h", after(head_rows, *sent_blocks)), ("h", far_rows)],
        [
            ("h", (half_slots * tall, model_dim), bf16),
            ("s", (2, head_slots), i32),
            ("s", (group_heads,), i32),
        ],
        [((all_heads,), i32)],
    )
    across = swap(after(sent_heads, *blocks), "mp", 2)
    pair_rows = swap(unit_rows, "mp", 1)
    scalars = jnp.concatenate([pick(lengths, rank)[None], pick(answer, rank), right_one])
    vectors = jnp.concatenate([b_out, ln1_gain, ln1_bias, b_down, ln2_gain, ln2_bias, b_out, b_out])
    vectors = vectors.astype(f32).reshape(8, model_dim)
    span = w_span.T
    grad_blocks = [pick(out_grad, other) for other in others]
    far_units, vectors, span, scalars, *grad_blocks = lax.optimization_barrier(
        (far_units, vectors, span, scalars, *grad_blocks, sent_heads)
    )[: 4 + rows]
    far_units = jnp.concatenate([far_units, swap(far_units, "dp", groups[0][0])], 1)
    far_side = swap(far_units, "dp", 1)
    *blocks, pair_rows = lax.optimization_barrier((*blocks, pair_rows, sent_heads))[: rows + 1]

    saved_outs = [("v", (head_slots, full, HEAD_DIM), bf16)] * 3 + [
        ("v", (head_slots, full, full), bf16),
        ("v", (head_slots * HEAD_DIM, full), bf16),
    ]
    lengths_in = [("s", place), ("s", lengths)]
    own_part, x_row, spots, head_bias, bias_in, own_heads, *own_saved = call(
        pin,
        functools.partial(attend_own_kernel, own_len, group_heads),
        "attend_own",
        lengths_in
        + [("s", heads), ("r", head_rows), ("r", far_rows)]
        + [("h", block) for block in blocks],
        [
            ("v", (full, model_dim), f32),
            ("b", (full, model_dim), bf16),
            ("h", (full, 1), i32),
            ("h", (2, head_slots, 2, HEAD_DIM), f32),
            ("h", (rows, model_dim), f32),
            ("b", (head_slots, tall, model_dim), bf16),
        ]
        + saved_outs,
        [((2 * group_heads * tall, model_dim), bf16), ((all_heads, 8, HEAD_DIM), f32)],
        sems=2,
    )
    unit_at = unit_at.reshape(ranks, ff_width)
    near_at = jnp.stack([pick(unit_at, other) for other in others])
    unit_bias = near_at[:, :, None] == jnp.arange(slots, dtype=i32)
    unit_bias = jnp.sum(jnp.where(unit_bias, bias_in[:, :ff_width, None], 0.0), 1)
    far_side, own_part = lax.optimization_barrier((far_side, own_part))
    far_pair = swap(far_units, "mp", 1)
    side_pair = swap(far_side, "mp", 1)
    across = after(across, far_side)
    other_sources = [across, swap(across, "mp", 1)]
    grad_blocks = [
        swap(after(block, across), "mp", o) if o else block for o, block in enumerate(grad_blocks)
    ]
    first_unit, first_inv, normed_low, *other_saved = call(
        pin,
        attend_kernel,
        "attend",
        lengths_in
        + [("s", heads), ("h", spots), ("h", head_bias), ("h", vectors)]
        + [("v", own_part), ("b", x_row)]
        + [("b", source) for source in other_sources],
        [
            ("v", (full, model_dim), f32),
            ("v", (full, 1), f32),
            ("v", (full, model_dim), bf16),
        ]
        + saved_outs,
        [((full, model_dim), f32)],
    )
    normed_low, side_pair, far_pair, *grad_blocks = lax.optimization_barrier(
        (normed_low, side_pair, far_pair, *grad_blocks)
    )
    far_units = [far_units, far_side, far_pair, side_pair]

    unit_side = (2, ranks // 2, slots, model_dim)
    hidden_dims = (ranks, full, slots)
    block_dims = (ranks, slots, model_dim)
    unit_far, layer_out, row_loss, loss_small, grad_second, grad_upper, *kept_units = call(
        pin,
        feed_kernel,
        "feed",
        [("s", scalars), ("v", normed_low), ("v", first_unit), ("h", vectors), ("h", unit_bias)]
        + [("b", unit_rows), ("b", pair_rows)]
        + [("b", u) for u in far_units]
        + [("h", spots), ("h", span)]
        + [("b", block) for block in grad_blocks],
        [
            ("h", unit_side, bf16),
            ("b", (full, model_dim), bf16),
            ("h", (1, 1), f32),
            ("h", (8, model_dim), f32),
            ("v", (full, model_dim), f32),
            ("v", hidden_dims, bf16),
            ("v", block_dims, bf16),
            ("v", block_dims, bf16),
            ("v", hidden_dims, bf16),
            ("v", hidden_dims, bf16),
        ],
        [
            ((full, model_dim), f32),
            ((full, model_dim), f32),
            ((full, model_dim), f32),
            ((full, 4), f32),
        ],
    )
    unit_got = swap(unit_far, "mp", 1)
    unit_near, first_small, grad_resid, grad_attended, slot_bias_grad = call(
        pin,
        feed_back_kernel,
        "feed_back",
        [("v", grad_upper), ("v", kept_units[0]), ("v", grad_second), ("v", first_unit)]
        + [("v", first_inv), ("h", vectors), ("v", normed_low)]
        + [("v", a) for a in kept_units[1:]],
        [
            ("v", unit_side, bf16),
            ("h", (8, model_dim), f32),
            ("v", (full, model_dim), f32),
            ("v", (full, model_dim), bf16),
            ("h", (ranks, slots), f32),
        ],
        [((full, model_dim), f32), (hidden_dims, bf16)],
    )

    halves = (slots, model_dim // 2)
    down_send, in_send, down_keep, in_keep = call(
        pin,
        merge_kernel,
        "merge",
        [("s", right_one), ("v", unit_near), ("h", unit_got)],
        [
            ("h", (slots, model_dim), bf16),
            ("h", (2,) + halves, bf16),
            ("b", (slots, model_dim), bf16),
            ("b", (2,) + halves, bf16),
        ],
    )
    grad_attended = after(grad_attended, down_send, in_send)
    down_got = swap(down_send, "mp", 2)
    in_got = swap(in_send, "dp", 1)

    head_far, head_near, late, rows_far, rows_near = call(
        pin,
        functools.partial(attend_back_kernel, own_len),
        "attend_back",
        [("s", heads), ("v", grad_attended), ("v", grad_resid), ("b", x_row)]
        + [("v", a) for a in own_saved]
        + [("b", own_heads)]
        + [("v", a) for a in other_saved]
        + [("l", a) for a in other_sources + [layer_out]],
        [
            ("h", (head_slots * tall, model_dim), bf16),
            ("v", (2, half_slots, tall, model_dim), bf16),
            ("h", (8, model_dim), f32),
        ]
        + [("b", (rows // 2, 2, own_len, model_dim), bf16)] * 2,
        [((full, model_dim), f32)],
    )

    head_far, down_got, in_got = lax.optimization_barrier((head_far, down_got, in_got))
    head_got = swap(head_far, "mp", 1)
    block_hit = (jnp.arange(ranks) ^ rank)[:, None] == jnp.arange(ranks)[None, :]
    place_ids = jnp.arange(pieces, dtype=i32) ^ (dp_index // 2)
    bits = len(masks_of("dp")) - 1
    place_ids = sum(
        (((place_ids >> b) & 1) << (bits - 1 - b) for b in range(bits)), jnp.zeros((pieces,), i32)
    )
    place_hit = place_ids[:, None] == jnp.arange(pieces)
    by_rank = slot_bias_grad.reshape(ranks, 1, 1, pieces, piece)
    by_rank = jnp.where(block_hit[:, :, None, None, None] & place_hit[:, :, None], by_rank, 0.0)
    by_rank = jnp.sum(by_rank, (0, 3)).reshape(-1)
    bias_count = -(-by_rank.shape[0] // model_dim)
    by_rank = jnp.pad(by_rank, (0, bias_count * model_dim - by_rank.shape[0]))
    device_hit = jnp.arange(model_dim) == dp_index * ranks + rank
    late_row = 10 + bias_count
    fill = -(-(late_row + 2) // 16) * 16 - late_row - 2
    loss_high = lax.reduce_precision(row_loss, 8, 7)
    small = jnp.concatenate(
        [
            first_small[:3],
            loss_small[:5],
            by_rank.reshape(-1, model_dim),
            jnp.where(device_hit, loss_high, 0.0),
            jnp.where(device_hit, row_loss - loss_high, 0.0),
            late[:2],
            jnp.zeros((fill, model_dim), f32),
        ],
        0,
    ).astype(bf16)
    small_got = swap(small, "mp", 1)

    kept = half_slots * tall
    small_dims = small.shape
    head_send, keep, small = call(
        pin,
        first_hop_kernel,
        "first_hop",
        [("v", head_near), ("h", head_got), ("h", small), ("h", small_got)],
        [
            ("h", (kept + small_dims[0], model_dim), bf16),
            ("v", (kept, model_dim), bf16),
            ("v", small_dims, bf16),
        ],
    )
    gots = [swap(head_send, "mp", 2)]
    down_got, in_got = lax.optimization_barrier((down_got, in_got, head_send))[:2]
    group = groups[0]
    parts = 1 << len(group)
    part = (slots // parts, model_dim // 2)
    down_send, down_keep, *in_parts = call(
        pin,
        second_merge_kernel,
        "second_merge",
        [("s", right_one), ("b", down_keep), ("h", down_got), ("b", in_keep), ("h", in_got)],
        [("h", halves, bf16), ("b", halves, bf16), ("b", (2,) + part, bf16)]
        + [("h", (2,) + part, bf16)] * (parts - 1),
    )
    down_got = swap(down_send, "dp", 1)
    in_gots = [swap(in_parts[j], "dp", partner(group, j)) for j in range(1, parts)]

    head_hops = [masks_of("dp")[:1]] + groups

    def head_hop(group, keep, small, gots):
        parts = 1 << len(group)
        own = own_bits(group, dp_index)[None].astype(i32)
        *sends, keep, small = hop(pin, parts, own, keep, small, gots)
        gots = [swap(sends[j - 1], "dp", partner(group, j)) for j in range(1, parts)]
        return keep, small, gots

    def widen(keep, group):
        got = [swap(keep, "dp", partner(group, j)) for j in range(1, 1 << len(group))]
        return jnp.concatenate([keep] + got, 0)

    unit_parts = call(
        pin,
        down_parts_kernel,
        "down_parts",
        [("b", down_keep), ("h", down_got)],
        [("h", part, bf16)] * parts,
    )
    down_gots = [swap(unit_parts[j], "dp", partner(group, j)) for j in range(1, parts)]
    gots[0] = after(gots[0], unit_parts[1])
    keep, small, gots = head_hop(head_hops[0], keep, small, gots)
    in_gots[0] = after(in_gots[0], keep)
    in_send, in_mine = call(
        pin,
        in_sum_kernel,
        "in_sum",
        [("b", in_parts[0])] + [("h", got) for got in in_gots],
        [("h", part, bf16)] * 2,
    )
    in_send, in_mine = (scatter_over(x, groups[1:]) for x in (in_send, in_mine))
    in_got = swap(in_send, "mp", 2)
    gots[0], in_got, *down_gots = lax.optimization_barrier((gots[0], in_got, *down_gots))
    down_mine = scatter_over(scatter_sum(unit_parts[0], down_gots), groups[1:])
    in_mine = scatter_sum(in_mine, [in_got])
    down_all = gather_over(down_mine, groups)
    down_side = swap(down_all, "dp", 1)
    rows_got = swap(after(rows_far, keep), "mp", 1)
    gots[0], rows_got, down_all = lax.optimization_barrier((gots[0], rows_got, down_all))
    rows_across = swap(jnp.stack([rows_near[1], rows_got[1]]), "mp", 2)
    keep, small, gots = head_hop(head_hops[1], keep, small, gots)
    for group in head_hops[2:]:
        keep, small, gots = head_hop(group, keep, small, gots)
    keep, small = hop(pin, 1, jnp.zeros((1,), i32), keep, small, gots)
    for group in reversed(groups):
        got = [swap(keep, "dp", partner(group, j)) for j in range(1, 1 << len(group))]
        keep = jnp.concatenate([keep] + got, 0)
    in_mine, rows_across, keep = lax.optimization_barrier((in_mine, rows_across, keep))
    own_rows = [rows_near[0], rows_got[0], rows_across[0], rows_across[1]]
    in_all = gather_over(in_mine, groups)
    in_side = swap(in_all, "dp", 1)
    mine = widen(keep, head_hops[0])
    w_down_grad = mxu(unit_pick, join_sides(down_all, down_side, right), 0, 0)
    w_in_grad = mxu(join_sides(in_all, in_side, right), unit_pick, 0, 0)
    own_rows = to_own(own_rows, rank)
    layer_out_own = own_rows[:, 0]
    tokens_grad = own_rows[:, 1].astype(f32)
    halves_of = [mine, swap(mine, "mp", 1)]

    head_piece = kept // n_dp
    row_ids = jnp.arange(2 * kept, dtype=i32)
    from_core, row_ids = row_ids // kept, row_ids % kept
    own_piece = own_bits([m for group in head_hops for m in group], dp_index)
    natural = ((row_ids // head_piece) ^ own_piece) * head_piece + row_ids % head_piece
    natural = natural + from_core * kept
    columns = jnp.arange(4 * head_width, dtype=i32)
    kind, rest = columns // head_width, columns % head_width
    column_slot = jnp.sum(
        jnp.where((rest // HEAD_DIM)[:, None] == jnp.arange(group_heads), my_slots, 0), 1
    )
    wanted = ((column_slot ^ core) % 2) * kept + (column_slot // 2) * tall
    wanted = wanted + kind * HEAD_DIM + rest % HEAD_DIM
    wanted = jnp.where(column_slot >= 0, wanted, -1)
    row_pick = (natural[:, None] == wanted[None, :]).astype(bf16)
    picks = [row_pick[:kept], row_pick[kept:]]
    w_qkv_grad = sum(mxu(a, p[:, : 3 * head_width], 0, 0) for a, p in zip(halves_of, picks))
    w_qkv_grad = w_qkv_grad.reshape(model_dim, 3, head_width)
    w_out_grad = sum(mxu(p[:, 3 * head_width :], a, 0, 0) for a, p in zip(halves_of, picks))

    by_rank = small[8 : 8 + bias_count].reshape(-1)[: ranks * slots].reshape(ranks, slots)
    by_rank = pick(by_rank, rank).reshape(pieces, 1, piece)
    by_rank = jnp.sum(jnp.where(place_hit[:, :, None], by_rank, 0.0), 0).reshape(slots)
    b_in_grad = jnp.sum(jnp.where(unit_pick > 0, by_rank[:, None], 0.0), 0)
    losses = small[8 + bias_count] + small[9 + bias_count]
    losses = losses[: n_dp * ranks].reshape(n_dp, ranks)
    losses = lax.dynamic_index_in_dim(losses, dp_index, 0, keepdims=False)
    late = small[late_row : late_row + 2].reshape(2, ranks, head_width)
    b_qv_grad = lax.dynamic_index_in_dim(late, rank, 1, keepdims=False)
    return (
        layer_out_own,
        losses,
        tokens_grad,
        w_qkv_grad,
        b_qv_grad,
        w_out_grad,
        small[2],
        small[0],
        small[1],
        w_in_grad,
        b_in_grad,
        w_down_grad,
        small[5],
        small[3],
        small[4],
        small[6:8].T,
    )


def shards(*args):
    head_order, neuron_order, w_qkv, w_in = args[3], args[4], args[5], args[11]
    ranks = lax.axis_size("mp")
    pair_heads = 2 * w_qkv.shape[2] // HEAD_DIM
    ff_width = w_in.shape[1]
    (fits,) = call(
        False,
        functools.partial(fits_kernel, UNIT_SLOTS, HEAD_SLOTS, ff_width, pair_heads, ranks),
        "fits",
        [("s", head_order), ("h", neuron_order[:LIVE_FF][None])],
        [("s", (1,), i32)],
    )
    return lax.cond(
        fits[0] == 1,
        functools.partial(program, UNIT_SLOTS, HEAD_SLOTS, True),
        functools.partial(program, ff_width, pair_heads, False),
        *args,
    )


def solution(mesh):
    return jax.shard_map(
        shards,
        mesh=mesh,
        in_specs=(
            P("dp", "mp", None),
            P("dp"),
            P("dp", None),
            P(),
            P(),
            P(None, None, "mp"),
            P(None, "mp"),
            P("mp", None),
            P(),
            P(),
            P(),
            P(None, "mp"),
            P("mp"),
            P("mp", None),
            P(),
            P(),
            P(),
            P(),
            P("dp", "mp", None),
        ),
        out_specs=(
            P("dp", "mp", None),
            P("dp"),
            P("dp", "mp", None),
            P(None, None, "mp"),
            P(None, "mp"),
            P("mp", None),
            P(),
            P(),
            P(),
            P(None, "mp"),
            P("mp"),
            P("mp", None),
            P(),
            P(),
            P(),
            P(),
        ),
        check_vma=False,
    )
```
